32 devices in a mesh: seq: 8 (over y, x, core), mp: 4 (over z).
Axes of the slice: x: 2, y: 2, z: 4, core: 2. Of those that a mesh axis runs over, the one named last changes fastest.
Arguments:
- tokens: bfloat16 [1024, 2, 1536], P('seq'), may hold values from -6 to 6
- lengths: int32 [2], replicated, may hold values from 256 to 1024, as said below
- expert_ids: int32 [1024, 2, 6], P('seq'), may hold values from 0 to 15, all different within a row; in each aligned block of 256 rows (0 to 255, 256 to 511, ..., all dimensions but the last counted through in order) at most 192 rows name the same one
- norm_gains: float32 [2, 1536], replicated, may hold values from 0.5 to 1.5
- in_z: bfloat16 [1536, 3072], P(None, 'mp'), may hold values from -0.15625 to 0.15625
- in_x: bfloat16 [1536, 3072], P(None, 'mp'), may hold values from -0.15625 to 0.15625
- in_bc: bfloat16 [1536, 256], replicated, may hold values from -0.15625 to 0.15625
- in_dt: bfloat16 [1536, 48], P(None, 'mp'), may hold values from -0.15625 to 0.15625
- conv_x: float32 [5, 3072], P(None, 'mp'), may hold values from -3 to 3
- conv_bc: float32 [5, 256], replicated, may hold values from -3 to 3
- head_par: float32 [3, 48], P(None, 'mp'), may hold values from -7 to 1.5, as said below
- gn_gain: float32 [3072], P('mp'), may hold values from 0.5 to 1.5
- out_w: bfloat16 [3072, 1536], P('mp'), may hold values from -0.109375 to 0.109375
- router: bfloat16 [1536, 16], replicated, may hold values from -0.078125 to 0.078125
- shared_in: bfloat16 [2, 1536, 1024], P(None, None, 'mp'), may hold values from -0.15625 to 0.15625
- shared_down: bfloat16 [1024, 1536], P('mp'), may hold values from -0.1875 to 0.1875
- expert_in: bfloat16 [32, 2, 1536, 256], P(('seq', 'mp')), may hold values from -0.15625 to 0.15625
- expert_down: bfloat16 [32, 256, 1536], P(('seq', 'mp')), may hold values from -0.5 to 0.5
- d_out: bfloat16 [1024, 2, 1536], P('seq'), may hold values from -6 to 6
Outputs:
- output: float32 [1024, 2, 1536], P('seq')
- d_tokens: float32 [1024, 2, 1536], P('seq')
- g_norm_gains: float32 [2, 1536], replicated
- g_in_z: float32 [1536, 3072], P(None, 'mp')
- g_in_x: float32 [1536, 3072], P(None, 'mp')
- g_in_bc: float32 [1536, 256], replicated
- g_in_dt: float32 [1536, 48], P(None, 'mp')
- g_conv_x: float32 [5, 3072], P(None, 'mp')
- g_conv_bc: float32 [5, 256], replicated
- g_head_par: float32 [3, 48], P(None, 'mp')
- g_gn_gain: float32 [3072], P('mp')
- g_out_w: float32 [3072, 1536], P('mp')
- g_router: float32 [1536, 16], replicated
- g_shared_in: float32 [2, 1536, 1024], P(None, None, 'mp')
- g_shared_down: float32 [1024, 1536], P('mp')
- g_expert_in: float32 [32, 2, 1536, 256], P(('seq', 'mp'))
- g_expert_down: float32 [32, 256, 1536], P(('seq', 'mp'))
The draws below stay inside these ranges and needn't reach their ends.
Inputs may be any that keep to these rules, and one draw needn't show every extreme that they name: `lengths`: one sequence, drawn from the seed, uses all 1024 positions; used positions come first. `expert_ids`: among the tokens of one index of seq (aligned blocks of 256 tokens), no expert is named more than 192 times, a bound that some block reaches. `head_par`: rows are step bias, log decay rate, skip weight.
All inputs are finite; a program needn't handle non-finite values.
Results may differ from the reference program's by a relative error of at most 0.035.
Values may be sent and summed in bfloat16 or wider, within the bound.
No kernel may reach another device: no remote copies, remote signals or barrier semaphores. Data moves between devices by JAX's collectives and lax.ppermute only.
A program may use at most 256 MiB of HBM per device.

```python
import math
import jax
import jax.numpy as jnp
import numpy as np
from jax import lax

D = 1536
HEADS = 48
HEAD_DIM = 64
STATE = 128
KCONV = 4
TOPK = 6
FF_E = 512
FF_S = 1024
PIECE = 128
SEQS = 2
INNER = 3072
EXPERTS = 16
LENGTH = 1024
CAP = 192
N_SEQ = 8


def draw_lengths(key, part):
    key_first, key_second = jax.random.split(jax.random.fold_in(key, 11))
    longest = jax.random.randint(key_first, (), 0, SEQS)
    values = jax.random.randint(key_second, (SEQS,), LENGTH // 4, LENGTH + 1)
    return jnp.where(jnp.arange(SEQS) == longest, LENGTH, values).astype(jnp.int32)


def draw_head_par(key, part):
    key_list = jax.random.split(jax.random.fold_in(key, 23), 3)
    step_bias = jax.random.uniform(key_list[0], (HEADS,), jnp.float32, -6.0, -2.0)
    log_rate = jax.random.uniform(key_list[1], (HEADS,), jnp.float32, -3.0, 0.5)
    skip_gain = jax.random.uniform(key_list[2], (HEADS,), jnp.float32, 0.5, 1.5)
    return jnp.stack([step_bias, log_rate, skip_gain])


def steps_of(stream_key, dims, cuts, low, top_value):
    loudness = 1.0
    for position, shards_of in cuts:
        steps = jax.random.uniform(jax.random.fold_in(jax.random.fold_in(stream_key, 6), position), (shards_of,), jnp.float32, low / len(cuts), top_value / len(cuts))
        loudness = loudness * jnp.repeat(jnp.exp(steps), dims[position] // shards_of).reshape((-1,) + (1,) * (len(dims) - 1 - position))
    return loudness


def deal_out(key, own, number, rows, amount, top, reach, skew):
    ranking = jax.random.permutation(key, amount)
    heavy_load, usual = load_shares(amount, rows * top, reach, skew, True), load_shares(amount, rows * top, reach, skew, False)
    places = jnp.arange(amount)

    def named(tallies, turn):
        used = int((tallies > 0).sum())
        fixed = max(1, used // 4)
        passed = fixed + (places - fixed + turn * (used - fixed)) % max(1, amount - fixed)
        return jnp.zeros((amount,), jnp.int32).at[ranking[jnp.where(places < fixed, places, passed)]].set(jnp.asarray(tallies, jnp.int32))

    tallies = jnp.where(number % 4 == 0, named(heavy_load, number // 4), named(usual, number - number // 4 - 1))
    mixed = jax.random.permutation(jax.random.fold_in(own, 3), amount)
    giver, taker = mixed[0:amount // 2 * 2:2], mixed[1:amount // 2 * 2:2]
    slack = jnp.minimum(tallies[giver] - 1, reach - tallies[taker]) // 2
    slack = jnp.where((giver == ranking[0]) | (taker == ranking[0]) | (tallies[taker] == 0), 0, jnp.maximum(slack, 0))
    passed = jax.random.randint(jax.random.fold_in(own, 4), (amount // 2,), 0, 1 << 20) % (slack + 1)
    tallies = tallies.at[giver].add(-passed).at[taker].add(passed)
    items = jnp.searchsorted(jnp.cumsum(tallies), jnp.arange(rows * top), side="right").astype(jnp.int32)
    table = items.reshape(top, rows).T
    table = table[jax.random.permutation(jax.random.fold_in(own, 1), rows)]
    turn = jax.random.randint(jax.random.fold_in(own, 2), (rows, 1), 0, top)
    return jnp.take_along_axis(table, (jnp.arange(top)[None, :] + turn) % top, axis=1)


def load_shares(amount, total, most, skew, full):
    loads = [(1 << 20) // math.isqrt(grade ** skew) + 1 for grade in range(1, amount + 1)]
    largest = most if full else min(most, max(-(-total // amount), total * loads[0] // sum(loads)))
    least = 1 if total - largest >= amount - 1 else 0
    given, spare = [largest] + [least] * (amount - 1), total - largest - least * (amount - 1)
    while spare > 0:
        movable = [i for i in range(1, amount) if given[i] < largest] or [i for i in range(1, amount) if given[i] < most]
        mass, budget = sum([loads[i] for i in movable]), spare
        for i in movable:
            addition = min(most - given[i], max(1, budget * loads[i] // mass), spare)
            given[i] = given[i] + addition
            spare = spare - addition
    return np.array(given)


def gaussian(key, dims, scale, reach, cuts=(), held_as=jnp.bfloat16):
    values = scale * jax.random.normal(key, dims, jnp.float32)
    if cuts:
        values = values * steps_of(key, dims, cuts, -0.22, 0.18)
    return jnp.clip(values, -reach, reach).astype(held_as)


def setup_inputs(seed: int = 0) -> dict:
    streams_of = jax.random.split(jax.random.key(seed), 20)
    tokens = gaussian(streams_of[0], (LENGTH, SEQS, D), 1.0, 6.0, ((0, 8),))
    lengths = draw_lengths(jax.random.fold_in(streams_of[19], 71), 0)
    expert_ids_keys = jax.random.split(jax.random.fold_in(streams_of[2], 1), LENGTH * SEQS // (PIECE * SEQS))
    expert_ids_turns = jax.random.permutation(jax.random.fold_in(streams_of[2], 3), LENGTH * SEQS // (PIECE * SEQS))
    expert_ids = jax.vmap(lambda own, number: deal_out(jax.random.fold_in(streams_of[2], 2), own, number, PIECE * SEQS, EXPERTS, TOPK, CAP, 1))(expert_ids_keys, expert_ids_turns).reshape((LENGTH, SEQS, TOPK))
    norm_gains = jnp.clip(1.0 + 0.1 * jax.random.normal(streams_of[3], (2, D), jnp.float32), 0.5, 1.5)
    in_z = gaussian(streams_of[4], (D, INNER), D ** -0.5, 0.15625, ((1, 4),))
    in_x = gaussian(streams_of[5], (D, INNER), D ** -0.5, 0.15625, ((1, 4),))
    in_bc = gaussian(streams_of[6], (D, 2 * STATE), D ** -0.5, 0.15625)
    in_dt = gaussian(streams_of[7], (D, HEADS), D ** -0.5, 0.15625, ((1, 4),))
    conv_x = gaussian(streams_of[8], (KCONV + 1, INNER), 0.5, 3.0, ((1, 4),), jnp.float32)
    conv_bc = gaussian(streams_of[9], (KCONV + 1, 2 * STATE), 0.5, 3.0, (), jnp.float32)
    head_par = draw_head_par(jax.random.fold_in(streams_of[19], 71), 0)
    gn_gain = jnp.clip(1.0 + 0.1 * jax.random.normal(streams_of[11], (INNER,), jnp.float32), 0.5, 1.5)
    out_w = gaussian(streams_of[12], (INNER, D), INNER ** -0.5, 0.109375, ((0, 4),))
    router = gaussian(streams_of[13], (D, EXPERTS), (4 * D) ** -0.5, 0.078125)
    shared_in = gaussian(streams_of[14], (2, D, FF_S), D ** -0.5, 0.15625, ((2, 4),))
    shared_down = gaussian(streams_of[15], (FF_S, D), FF_S ** -0.5, 0.1875, ((0, 4),))
    expert_in = gaussian(streams_of[16], (2 * EXPERTS, 2, D, FF_E // 2), D ** -0.5, 0.15625, ((0, 32),))
    expert_down = gaussian(streams_of[17], (2 * EXPERTS, FF_E // 2, D), (FF_E // 4) ** -0.5, 0.5, ((0, 32),))
    d_out = gaussian(streams_of[18], (LENGTH, SEQS, D), 1.0, 6.0, ((0, 8),))
    return dict(tokens=tokens, lengths=lengths, expert_ids=expert_ids, norm_gains=norm_gains, in_z=in_z, in_x=in_x, in_bc=in_bc, in_dt=in_dt, conv_x=conv_x, conv_bc=conv_bc, head_par=head_par, gn_gain=gn_gain, out_w=out_w, router=router, shared_in=shared_in, shared_down=shared_down, expert_in=expert_in, expert_down=expert_down, d_out=d_out)


HIGHEST_PRECISION = lax.Precision.HIGHEST
EPSILON = 1e-05

@jax.custom_vjp
def low(v):
    return lax.optimization_barrier(v.astype(jnp.bfloat16)).astype(jnp.float32)

@jax.custom_vjp
def low_back(v):
    return v

def low_keep(v):
    return (low(v), None)

def low_pass(kept, grad):
    return (grad,)

def back_keep(v):
    return (v, None)

def back_low(kept, grad):
    return (low(grad),)
low.defvjp(low_keep, low_pass)
low_back.defvjp(back_keep, back_low)

def high_dot(left_in, right_in):
    return jnp.dot(left_in, right_in, precision=HIGHEST_PRECISION)

def prepare(xbc_rows, edge_rows, dt_raw, conv_all, rates, live_mask, width_x):
    span_rows = xbc_rows.shape[0]
    padded = jnp.concatenate([edge_rows, xbc_rows], axis=0)
    summed = conv_all[KCONV]
    for tap_index in range(KCONV):
        summed = summed + conv_all[tap_index] * padded[tap_index:tap_index + span_rows]
    active = jax.nn.silu(summed)
    x_ssm = active[..., :width_x] * live_mask[..., None]
    b_mat = active[..., width_x:width_x + STATE]
    c_mat = active[..., width_x + STATE:]
    stepped = jax.nn.softplus(dt_raw + rates[0]) * live_mask[..., None]
    log_decay = -jnp.exp(rates[1]) * stepped
    return (x_ssm.reshape(span_rows, x_ssm.shape[1], -1, HEAD_DIM), b_mat, c_mat, log_decay, stepped)

def ssd_core(x_ssm, b_mat, c_mat, log_decay, stepped, skip_gain):
    span_rows = x_ssm.shape[0]
    cumulative = jnp.cumsum(log_decay, axis=0)
    order_mask = (jnp.arange(span_rows)[:, None] >= jnp.arange(span_rows)[None, :])[:, :, None, None]
    log_gaps = cumulative[:, None] - cumulative[None, :]
    decays = jnp.where(order_mask, jnp.exp(jnp.where(order_mask, log_gaps, 0.0)), 0.0)
    scores = jnp.einsum('tsn,usn->tus', c_mat, b_mat, precision=HIGHEST_PRECISION)
    weighted = x_ssm * stepped[..., None]
    outputs = jnp.einsum('tush,ushp->tshp', decays * scores[..., None], weighted, precision=HIGHEST_PRECISION)
    outputs = outputs + skip_gain[:, None] * x_ssm
    remaining = jnp.exp(cumulative[-1][None] - cumulative)
    local_state = jnp.einsum('ushp,usn->shpn', weighted * remaining[..., None], b_mat, precision=HIGHEST_PRECISION)
    return (outputs, local_state, jnp.exp(cumulative[-1]))

def state_term(c_mat, log_decay, entering):
    cumulative = jnp.cumsum(log_decay, axis=0)
    return jnp.einsum('tsn,shpn->tshp', c_mat, entering, precision=HIGHEST_PRECISION) * jnp.exp(cumulative)[..., None]

def route_table(flat_ids, experts, capacity):
    total_routes = flat_ids.shape[0]
    onehot = (flat_ids[:, None] == jnp.arange(experts, dtype=jnp.int32)[None, :]).astype(jnp.int32)
    slot_ranks = lax.optimization_barrier(jnp.sum((jnp.cumsum(onehot, axis=0) - onehot) * onehot, axis=1)).astype(jnp.int32)
    slot_table = jnp.full((experts * capacity,), total_routes, jnp.int32)
    slot_table = slot_table.at[flat_ids * capacity + slot_ranks].set(jnp.arange(total_routes, dtype=jnp.int32))
    return (slot_table.reshape(experts, capacity), slot_ranks)

def mixer(tokens_f, norm_gains, in_z, in_x, in_bc, in_dt, conv_x, conv_bc, head_par, gn_gain, out_w, live_mask):
    scale_one = lax.rsqrt(lax.optimization_barrier(jnp.mean(tokens_f * tokens_f, axis=-1, keepdims=True)) + EPSILON)
    normed = low(tokens_f * scale_one * norm_gains[0])
    gate_z = low_back(high_dot(normed, in_z))
    xbc_rows = low_back(low(jnp.concatenate([high_dot(normed, in_x), high_dot(normed, in_bc)], axis=-1)))
    dt_raw = low_back(high_dot(normed, in_dt))
    conv_all = jnp.concatenate([conv_x, conv_bc], axis=-1)
    edge_rows = jnp.zeros((KCONV - 1,) + xbc_rows.shape[1:], jnp.float32)
    prepared = prepare(xbc_rows, edge_rows, dt_raw, conv_all, head_par[:2], live_mask, INNER)
    pieces = LENGTH // PIECE

    def split_up(array_in):
        return array_in.reshape((pieces, PIECE) + array_in.shape[1:])

    def advance(carried, inputs):
        xs_piece, b_piece, c_piece, decay_piece, step_piece = inputs
        base_out, local_state, total_decay = ssd_core(xs_piece, b_piece, c_piece, decay_piece, step_piece, head_par[2])
        outputs = base_out + state_term(c_piece, decay_piece, carried)
        return (total_decay[..., None, None] * carried + local_state, outputs)
    initial = jnp.zeros((SEQS, HEADS, HEAD_DIM, STATE), jnp.float32)
    _, outputs = lax.scan(jax.checkpoint(advance), initial, tuple((split_up(array_in) for array_in in prepared)))
    mixed_y = outputs.reshape(LENGTH, SEQS, INNER)
    gated_y = mixed_y * jax.nn.silu(gate_z)
    inner_scale = lax.rsqrt(lax.optimization_barrier(jnp.mean(gated_y * gated_y, axis=-1, keepdims=True)) + EPSILON)
    normed_y = low(gated_y * inner_scale * gn_gain)
    mixer_out = low_back(high_dot(normed_y, out_w))
    return tokens_f + mixer_out

def routed_block(normed_rows, gate_flat, slot_table, experts_in, experts_down):
    total_routes = gate_flat.shape[0]
    live_slot = slot_table < total_routes
    safe_route = jnp.minimum(slot_table, total_routes - 1)
    picked = normed_rows[safe_route // TOPK] * live_slot[..., None]
    halves_in = low_back(jnp.broadcast_to(picked[:, None], (picked.shape[0], 2) + picked.shape[1:]))
    gate_h = low_back(jnp.einsum('ehcd,ehdf->ehcf', halves_in, experts_in[:, :, 0], precision=HIGHEST_PRECISION))
    up_h = low_back(jnp.einsum('ehcd,ehdf->ehcf', halves_in, experts_in[:, :, 1], precision=HIGHEST_PRECISION))
    hidden = low(jax.nn.silu(gate_h) * up_h)
    partial_out = low(jnp.einsum('ehcf,ehfd->ehcd', hidden, experts_down, precision=HIGHEST_PRECISION))
    expert_out = low_back(partial_out[:, 0] + partial_out[:, 1])
    weights = gate_flat[safe_route] * live_slot
    placed = (expert_out * weights[..., None]).reshape(-1, expert_out.shape[-1])
    return jnp.zeros(normed_rows.shape, jnp.float32).at[(safe_route // TOPK).reshape(-1)].add(placed)

def reference(tokens, lengths, expert_ids, norm_gains, in_z, in_x, in_bc, in_dt, conv_x, conv_bc, head_par, gn_gain, out_w, router, shared_in, shared_down, expert_in, expert_down, d_out):
    live_mask = (jnp.arange(LENGTH, dtype=jnp.int32)[:, None] < lengths[None, :]).astype(jnp.float32)
    block_rows = PIECE * SEQS

    def per_block(flat_ids):
        return route_table(flat_ids, EXPERTS, CAP)[0]
    tables = jax.vmap(per_block)(expert_ids.reshape(N_SEQ, block_rows * TOPK))
    pick_mask = (expert_ids[..., None] == jnp.arange(EXPERTS, dtype=jnp.int32)).astype(jnp.float32)

    def forward(tokens_f, norm_gains, in_z, in_x, in_bc, in_dt, conv_x, conv_bc, head_par, gn_gain, out_w, router, shared_in, shared_down, expert_in, expert_down):
        residual = mixer(tokens_f, norm_gains, in_z, in_x, in_bc, in_dt, conv_x, conv_bc, head_par, gn_gain, out_w, live_mask)
        scale_two = lax.rsqrt(lax.optimization_barrier(jnp.mean(residual * residual, axis=-1, keepdims=True)) + EPSILON)
        normed_two = low(residual * scale_two * norm_gains[1])
        logits = low_back(high_dot(normed_two, router))
        chosen = lax.optimization_barrier(jnp.sum(pick_mask * logits[..., None, :], axis=-1))
        gate_probs = jax.nn.softmax(chosen, axis=-1)
        shared_gate = low_back(high_dot(normed_two, shared_in[0]))
        shared_up = low_back(high_dot(normed_two, shared_in[1]))
        shared_hidden = low(jax.nn.silu(shared_gate) * shared_up)
        shared_out = high_dot(shared_hidden, shared_down)
        experts_in = expert_in.reshape(EXPERTS, 2, 2, D, FF_E // 2)
        experts_down = expert_down.reshape(EXPERTS, 2, FF_E // 2, D)

        def one_block(block_parts):
            rows_blk, gate_blk, table_blk = block_parts
            return routed_block(rows_blk, gate_blk, table_blk, experts_in, experts_down)
        routed = lax.map(jax.checkpoint(one_block), (normed_two.reshape(N_SEQ, block_rows, D), gate_probs.reshape(N_SEQ, block_rows * TOPK), tables))
        return residual + shared_out + routed.reshape(LENGTH, SEQS, D)
    weights_f = (norm_gains, in_z.astype(jnp.float32), in_x.astype(jnp.float32), in_bc.astype(jnp.float32), in_dt.astype(jnp.float32), conv_x, conv_bc, head_par, gn_gain, out_w.astype(jnp.float32), router.astype(jnp.float32), shared_in.astype(jnp.float32), shared_down.astype(jnp.float32), expert_in.astype(jnp.float32), expert_down.astype(jnp.float32))
    output, pullback = jax.vjp(forward, tokens.astype(jnp.float32), *weights_f)
    all_grads = pullback(d_out.astype(jnp.float32))
    return (output, all_grads[0], all_grads[1], all_grads[2], all_grads[3], all_grads[4], all_grads[5], all_grads[6], all_grads[7], all_grads[8], all_grads[9], all_grads[10], all_grads[11], all_grads[12], all_grads[13], all_grads[14], all_grads[15])
```

```python
import functools

import jax
import jax.numpy as jnp
from jax import lax
from jax.experimental import pallas as pl
from jax.experimental.pallas import tpu as pltpu
from jax.sharding import PartitionSpec as P

HEAD_DIM = 64
STATE = 128
KCONV = 4
INNER = 3072
LANES = 128
FRONT = 16
EPSILON = 1e-05
F32 = jnp.float32
BF16 = jnp.bfloat16
HIGHEST = lax.Precision.HIGHEST
NN = (((1,), (0,)), ((), ()))
NT = (((1,), (1,)), ((), ()))
TN = (((0,), (0,)), ((), ()))


class Each:
    def __init__(self, array):
        self.array = array


class Scalars:
    def __init__(self, array):
        self.array = array


class Block:
    def __init__(self, array, rows, at):
        self.array, self.rows, self.at = array, rows, at


def struct(shape, dtype):
    return jax.ShapeDtypeStruct(tuple(shape), dtype)


def call(kernel, outs, args, flops, name, grid=1, index=None):
    def spec(a):
        if isinstance(a, Scalars):
            return pl.BlockSpec(memory_space=pltpu.SMEM)
        if isinstance(a, Block):
            return pl.BlockSpec((a.rows, a.array.shape[1]), lambda s, at, k=a.at: (at[k], 0))
        if isinstance(a, Each):
            rest = a.array.shape[1:]
            return pl.BlockSpec((None, *rest), lambda s, *_: (s,) + (0,) * len(rest))
        return pl.BlockSpec(a.shape, lambda s, *_: (0,) * len(a.shape))

    def plain(a):
        return a.array if isinstance(a, (Each, Scalars, Block)) else a

    arrays = [plain(a) for a in args]
    shapes = [plain(a) for a in outs]
    moved = sum(
        a.rows * a.array.shape[1] * a.array.dtype.itemsize
        if isinstance(a, Block)
        else plain(a).size * plain(a).dtype.itemsize
        for a in (*args, *outs)
    )
    grid_spec = pltpu.PrefetchScalarGridSpec(
        num_scalar_prefetch=0 if index is None else 1,
        grid=(grid,),
        in_specs=[spec(a) for a in args],
        out_specs=[spec(a) for a in outs],
    )
    return pl.pallas_call(
        kernel,
        out_shape=shapes,
        grid_spec=grid_spec,
        compiler_params=pltpu.CompilerParams(vmem_limit_bytes=60 * 2**20),
        cost_estimate=pl.CostEstimate(flops=int(flops), bytes_accessed=int(moved), transcendentals=0),
        name=name,
    )(*([] if index is None else [index]), *arrays)


def dot(a, b, dims=NN):
    return lax.dot_general(a.astype(BF16), b.astype(BF16), dims, preferred_element_type=F32)


def exact(a, b, dims=NN):
    return lax.dot_general(a, b, dims, precision=HIGHEST, preferred_element_type=F32)


def sigmoid(v):
    return 1.0 / (1.0 + jnp.exp(-v))


def iota(shape, axis):
    return lax.broadcasted_iota(jnp.int32, shape, axis)


def two_terms(v):
    high = v.astype(BF16)
    return high, (v - high.astype(F32)).astype(BF16)


def to_lanes(v):
    return jnp.concatenate([v, jnp.zeros((v.shape[0], LANES - v.shape[1]), v.dtype)], axis=1)


def spread_matrix(width):
    return (iota((LANES, width), 1) // HEAD_DIM == iota((LANES, width), 0)).astype(F32)


def prepared(xbc, dt, conv_x, conv_bc, head_par, meta):
    rows = dt.shape[0]
    width = conv_x.shape[1]
    conv = jnp.concatenate([conv_x[...], conv_bc[...]], axis=1)
    hp = to_lanes(head_par[...])
    where = iota((rows, 1), 0) + meta[2]
    live = (where < meta[pl.program_id(0)]).astype(F32)
    xf = xbc[...].astype(F32)
    summed = conv[KCONV : KCONV + 1]
    taps = []
    for j in range(KCONV):
        shifted = xf[FRONT - (KCONV - 1) + j : FRONT - (KCONV - 1) + j + rows]
        taps.append(shifted)
        summed = summed + conv[j : j + 1] * shifted
    sig = sigmoid(summed)
    act = summed * sig
    xs = act[:, :width] * live
    b = act[:, width : width + STATE]
    c = act[:, width + STATE :]
    raw = dt[...] + hp[0:1]
    step = (jnp.maximum(raw, 0.0) + jnp.log1p(jnp.exp(-jnp.abs(raw)))) * live
    rate = -jnp.exp(hp[1:2])
    logd = rate * step
    lower = (iota((rows, rows), 0) >= iota((rows, rows), 1)).astype(F32)
    cum = exact(lower, logd)
    return dict(
        conv=conv, skip=hp[2:3], live=live, taps=taps, summed=summed, sig=sig, xs=xs, b=b, c=c, raw=raw,
        step=step, rate=rate, logd=logd, cum=cum,
    )


def pack_state(o_send, state, decay):
    size = state.shape[0]
    high, low = two_terms(decay)
    row = iota((FRONT, LANES), 0)
    more = jnp.where(row == 0, high.astype(F32), 0.0) + jnp.where(row == 1, low.astype(F32), 0.0)
    o_send[:size, :] = state.astype(BF16)
    o_send[size:, :] = more.astype(BF16)


def unpack_state(send):
    size = send.shape[0] - FRONT
    more = send[size:, :].astype(F32)
    return send[:size, :].astype(F32), more[0:1] + more[1:2]


def k_in(tok, gains, wz, wx, wbc, wdt, conv_x, conv_bc, head_par, meta, o_norm, o_z, o_xbc, o_dt, o_send, o_tot):
    width = wz.shape[1]
    x = tok[...].astype(F32)
    scale = lax.rsqrt(jnp.mean(x * x, axis=-1, keepdims=True) + EPSILON)
    normed = (x * scale * gains[0:1]).astype(BF16)
    own = normed[FRONT:]
    o_norm[...] = own
    o_xbc[:, :width] = dot(normed, wx[...]).astype(BF16)
    o_xbc[:, width:] = dot(normed, wbc[...]).astype(BF16)
    o_dt[...] = to_lanes(dot(own, wdt[...]))
    o_z[...] = dot(own, wz[...])
    p = prepared(o_xbc, o_dt, conv_x, conv_bc, head_par, meta)
    rows = own.shape[0]
    last = p["cum"][rows - 1 : rows]
    weight = exact(p["step"] * jnp.exp(last - p["cum"]), spread_matrix(width))
    decay = jnp.exp(last)
    pack_state(o_send, dot(p["xs"] * weight, p["b"], TN), decay)
    o_tot[...] = jnp.broadcast_to(decay, o_tot.shape)


def pair_masks(rows):
    low = iota((rows, LANES), 1) < HEAD_DIM
    return low, jnp.logical_not(low)


def decays(cum, cum_t, h, ahead):
    gap = cum[:, h : h + 1] - cum_t[h : h + 1, :]
    return jnp.where(ahead, jnp.exp(jnp.where(ahead, gap, 0.0)), 0.0)


def by_halves(v, low, high):
    return jnp.concatenate(
        [jnp.where(low, v, 0.0).astype(BF16), jnp.where(high, v, 0.0).astype(BF16)], axis=0
    )


def k_intra(xbc, dt, conv_x, conv_bc, head_par, meta, o_y, o_c, o_ecum):
    width = o_y.shape[1]
    p = prepared(xbc, dt, conv_x, conv_bc, head_par, meta)
    xs, cum = p["xs"], p["cum"]
    rows = cum.shape[0]
    spread = spread_matrix(width)
    ahead = iota((rows, rows), 0) >= iota((rows, rows), 1)
    cum_t = cum.T
    scores = dot(p["c"], p["b"], NT)
    spread_out = exact(
        jnp.concatenate([p["step"], jnp.exp(cum), jnp.broadcast_to(p["skip"], (8, LANES))], axis=0), spread
    )
    xw = xs * spread_out[:rows]
    skip = spread_out[2 * rows : 2 * rows + 1]
    low, high = pair_masks(rows)
    o_c[...] = p["c"].astype(BF16)
    o_ecum[...] = spread_out[rows : 2 * rows]
    for pair in range(width // LANES):
        cols = slice(pair * LANES, (pair + 1) * LANES)
        mats = [(decays(cum, cum_t, h, ahead) * scores).astype(BF16) for h in (2 * pair, 2 * pair + 1)]
        within = dot(jnp.concatenate(mats, axis=1), by_halves(xw[:, cols], low, high))
        o_y[:, cols] = within + skip[:, cols] * xs[:, cols]


def k_scan(first, last, after, recv, send_in, total, whole, before, reach, *outs):
    own, own_decay = unpack_state(send_in)
    if first:
        whole_now, total_now = own, own_decay
        before_now, reach_now = None, None
    else:
        whole_now, total_now = whole[...], total[0:1]
        before_now, reach_now = before[...], reach[0:1]
    state, decay = unpack_state(recv)
    size = state.shape[0]
    mine = iota((size, LANES), 1) == iota((size, LANES), 0) // HEAD_DIM

    def rows_of(d):
        return jnp.sum(jnp.where(mine, d, 0.0), axis=1, keepdims=True)

    is_after = after[0] == 1
    if first:
        new_before = jnp.where(is_after, state, 0.0)
        new_reach = jnp.where(is_after, decay, 1.0)
    else:
        new_before = jnp.where(is_after, before_now + rows_of(reach_now) * state, before_now)
        new_reach = jnp.where(is_after, reach_now * decay, reach_now)
    outs[0][...] = new_before
    if last:
        return
    o_before, o_reach, o_whole, o_total, o_send = outs
    o_reach[...] = jnp.broadcast_to(new_reach, o_reach.shape)
    new_whole = jnp.where(
        is_after, whole_now + rows_of(total_now) * state, state + rows_of(decay) * whole_now
    )
    new_total = total_now * decay
    o_whole[...] = new_whole
    o_total[...] = jnp.broadcast_to(new_total, o_total.shape)
    pack_state(o_send, new_whole, new_total)


def k_out(y0, c, ecum, entering, z, gain, w, o_y, o_part):
    model = w.shape[1]
    y = y0[...] + ecum[...] * dot(c[...], entering[...], NT)
    o_y[...] = y
    zv = z[...]
    gated = y * zv * sigmoid(zv)
    high, low = two_terms(jnp.sum(gated * gated, axis=-1, keepdims=True))
    o_part[:, :model] = dot(gated * gain[...], w[...]).astype(BF16)
    o_part[:, model:] = to_lanes(jnp.concatenate([high, low], axis=1))


def k_back_gate(dm, y, z, gain, w, c, ecum, total, o_dz, o_dy, o_send, o_gain, o_norm):
    model = w.shape[1]
    more = dm[:, model:].astype(F32)
    stat = more[:, 0:1] + more[:, 1:2]
    scale = more[:, 2:3] + more[:, 3:4]
    dn = dot(dm[:, :model], w[...], NT)
    zv = z[...]
    sig = sigmoid(zv)
    silu = zv * sig
    yv = y[...]
    gated = yv * silu
    dgated = scale * gain[...] * dn - gated * (scale * scale * stat / INNER)
    o_dz[...] = (dgated * yv * sig * (1.0 + zv * (1.0 - sig))).astype(BF16)
    dy = dgated * silu
    o_dy[...] = dy
    o_gain[...] = jnp.broadcast_to(jnp.sum(dn * gated * scale, axis=0, keepdims=True), o_gain.shape)
    o_norm[...] = (gated * scale * gain[...]).astype(BF16)
    pack_state(o_send, dot(ecum[...] * dy, c[...], TN), total[0:1])


def k_back_intra(xbc, dt, conv_x, conv_bc, head_par, meta, dy, dz, wz, o_dxw, o_db, o_dc, o_dcum, o_dn):
    width = dy.shape[1]
    p = prepared(xbc, dt, conv_x, conv_bc, head_par, meta)
    cum = p["cum"]
    rows = cum.shape[0]
    o_dn[...] = dot(dz[...], wz[...], NT)
    ahead = iota((rows, rows), 0) >= iota((rows, rows), 1)
    cum_t = cum.T
    scores = dot(p["c"], p["b"], NT)
    xw = p["xs"] * exact(p["step"], spread_matrix(width))
    low, high = pair_masks(rows)
    lane = iota((rows, LANES), 1)
    sub = iota((LANES, rows), 0)
    dscores = jnp.zeros((rows, rows), F32)
    plus = jnp.zeros((rows, LANES), F32)
    minus = jnp.zeros((LANES, rows), F32)
    for pair in range(width // LANES):
        cols = slice(pair * LANES, (pair + 1) * LANES)
        dstack = by_halves(dy[:, cols], low, high)
        dmats = dot(dstack, xw[:, cols], NT)
        mats = []
        for i, h in enumerate((2 * pair, 2 * pair + 1)):
            decay = decays(cum, cum_t, h, ahead)
            mat = decay * scores
            dmat = dmats[i * rows : (i + 1) * rows]
            dscores = dscores + dmat * decay
            flow = dmat * mat
            plus = jnp.where(lane == h, jnp.sum(flow, axis=1, keepdims=True), plus)
            minus = jnp.where(sub == h, jnp.sum(flow, axis=0, keepdims=True), minus)
            mats.append(mat.astype(BF16))
        o_dxw[:, cols] = dot(jnp.concatenate(mats, axis=0), dstack, TN)
    o_dcum[...] = plus - minus.T
    o_dc[...] = dot(dscores, p["b"])
    o_db[...] = dot(dscores, p["c"], TN)


def k_back_state(
    xbc, dt, conv_x, conv_bc, head_par, meta, dy, dxw0, db0, dc0, dcum0, entering, leaving,
    o_dxbc, o_ddt, o_conv, o_hp,
):
    width = dy.shape[1]
    p = prepared(xbc, dt, conv_x, conv_bc, head_par, meta)
    xs, b, c, cum, step, rate, live = (p[k] for k in ("xs", "b", "c", "cum", "step", "rate", "live"))
    summed, sig, conv = p["summed"], p["sig"], p["conv"]
    rows = cum.shape[0]
    spread = spread_matrix(width)
    last = cum[rows - 1 : rows]
    spread_out = exact(
        jnp.concatenate(
            [step, jnp.exp(cum), jnp.exp(last - cum), jnp.broadcast_to(p["skip"], (8, LANES))], axis=0
        ),
        spread,
    )
    step_x, ecum_x, rem_x = (spread_out[i * rows : (i + 1) * rows] for i in range(3))
    skip_x = spread_out[3 * rows : 3 * rows + 1]
    dyv = dy[...]
    h0 = entering[...]
    h1 = leaving[...]
    xw = xs * step_x
    scaled_dy = ecum_x * dyv
    dc = dc0[...] + dot(scaled_dy, h0)
    from_state = scaled_dy * dot(c, h0, NT)
    to_state = rem_x * dot(b, h1, NT)
    dxw = dxw0[...] + to_state
    db = db0[...] + dot(xw * rem_x, h1)
    dtotal = jnp.sum(exact(spread, h1 * h0), axis=1, keepdims=True)
    sums = exact(jnp.concatenate([from_state, xw * to_state, dxw * xs, dyv * xs], axis=0), spread, NT)
    flow = sums[rows : 2 * rows]
    dlast = jnp.broadcast_to(dtotal, (LANES, LANES)).T[0:1] * jnp.exp(last) + jnp.sum(
        flow, axis=0, keepdims=True
    )
    dcum = dcum0[...] + sums[:rows] - flow
    dcum = dcum + jnp.where(iota((rows, LANES), 0) == rows - 1, dlast, 0.0)
    upper = (iota((rows, rows), 0) <= iota((rows, rows), 1)).astype(F32)
    dlogd = exact(upper, dcum)
    draw = (sums[2 * rows : 3 * rows] + dlogd * rate) * live * sigmoid(p["raw"])
    o_ddt[...] = draw.astype(BF16)
    row = iota((8, LANES), 0)
    o_hp[...] = (
        jnp.where(row == 0, jnp.sum(draw, axis=0, keepdims=True), 0.0)
        + jnp.where(row == 1, jnp.sum(dlogd * p["logd"], axis=0, keepdims=True), 0.0)
        + jnp.where(row == 2, jnp.sum(sums[3 * rows : 4 * rows], axis=0, keepdims=True), 0.0)
    )
    dx = (dxw * step_x + skip_x * dyv) * live
    dsummed = jnp.concatenate([dx, db, dc], axis=1) * sig * (1.0 + summed * (1.0 - sig))
    zeros = jnp.zeros((FRONT, dsummed.shape[1]), F32)
    padded = jnp.concatenate([zeros, dsummed, zeros], axis=0)
    total = rows + FRONT
    out = jnp.zeros((total, dsummed.shape[1]), F32)
    for j in range(KCONV):
        shift = KCONV - 1 - j
        out = out + conv[j : j + 1] * padded[shift : shift + total]
        o_conv[j : j + 1] = jnp.sum(dsummed * p["taps"][j], axis=0, keepdims=True)
    o_conv[KCONV : KCONV + 1] = jnp.sum(dsummed, axis=0, keepdims=True)
    o_conv[KCONV + 1 :] = jnp.zeros((o_conv.shape[0] - KCONV - 1, dsummed.shape[1]), F32)
    o_dxbc[...] = out


def k_back_in(dn0, dxbc, edge, ddt, tok, wx, wbc, wdt, o_part, o_dx, o_bc, o_gain):
    width = wx.shape[1]
    rows = dn0.shape[0]
    tail = jnp.concatenate([jnp.zeros((rows - FRONT, edge.shape[1]), F32), edge[...]], axis=0)
    own = (dxbc[FRONT:, :] + tail).astype(BF16)
    dx, dbc = own[:, :width], own[:, width:]
    o_dx[:, :width] = dx
    o_dx[:, width:] = ddt[...]
    o_bc[...] = dbc
    dn = dn0[...] + dot(dx, wx[...], NT) + dot(dbc, wbc[...], NT) + dot(ddt[...], to_lanes(wdt[...]), NT)
    o_part[...] = dn.astype(BF16)
    x = tok[FRONT:, :].astype(F32)
    scale = lax.rsqrt(jnp.mean(x * x, axis=-1, keepdims=True) + EPSILON)
    o_gain[...] = jnp.broadcast_to(jnp.sum(dn * x * scale, axis=0, keepdims=True), o_gain.shape)


def k_rows_one(arrived, tok, gains, o_residual, o_mixer, o_two, o_scales):
    model = tok.shape[1]
    total = sum(arrived[k].astype(F32) for k in range(arrived.shape[0]))
    scale = lax.rsqrt((total[:, model : model + 1] + total[:, model + 1 : model + 2]) / INNER + EPSILON)
    mixer = total[:, :model] * scale
    residual = tok[...].astype(F32) + mixer
    scale_two = lax.rsqrt(jnp.mean(residual * residual, axis=-1, keepdims=True) + EPSILON)
    o_residual[...] = residual
    o_mixer[...] = mixer
    o_two[...] = (residual * scale_two * gains[1:2]).astype(BF16)
    o_scales[...] = to_lanes(jnp.concatenate([scale, scale_two], axis=1))


def k_rows_two(arrived, dout, two, residual, mixer, scales, gains, router, o_dm, o_dr, o_gain, o_router):
    model = two.shape[1]
    experts = router.shape[1]
    both = sum(arrived[k].astype(F32) for k in range(arrived.shape[0]))
    dn2, dgate = both[:, :model], both[:, model:]
    w = to_lanes(router[...])
    probs = masked_softmax(dot(two[...], w), dout[:, model:].astype(F32))
    dlog = (probs * (dgate - jnp.sum(probs * dgate, axis=-1, keepdims=True))).astype(BF16)
    dn2 = dn2 + dot(dlog, w, NT)
    o_router[...] = dot(dlog, two[...], TN)[:experts]
    scale, scale_two = scales[:, 0:1], scales[:, 1:2]
    scaled = residual[...] * scale_two
    o_gain[...] = jnp.broadcast_to(jnp.sum(dn2 * scaled, axis=0, keepdims=True), o_gain.shape)
    gg = dn2 * gains[1:2]
    dr = dout[:, :model].astype(F32) + scale_two * (
        gg - scaled * jnp.mean(gg * scaled, axis=-1, keepdims=True)
    )
    o_dr[...] = dr
    dm = dr.astype(BF16)
    o_dm[:, :model] = dm
    stat = jnp.sum(dm.astype(F32) * mixer[...], axis=-1, keepdims=True)
    o_dm[:, model:] = to_lanes(jnp.concatenate([*two_terms(stat), *two_terms(scale)], axis=1))


def k_rows_three(arrived, tok, dr, gains, o_dtok):
    dn1 = sum(arrived[k].astype(F32) for k in range(arrived.shape[0]))
    x = tok[...].astype(F32)
    scale = lax.rsqrt(jnp.mean(x * x, axis=-1, keepdims=True) + EPSILON)
    scaled = x * scale
    gg = dn1 * gains[0:1]
    o_dtok[...] = (
        dr[...] + scale * (gg - scaled * jnp.mean(gg * scaled, axis=-1, keepdims=True))
    ).astype(BF16)


def k_rows_out(arrived, residual, o_out):
    total = sum(arrived[k].astype(F32) for k in range(arrived.shape[0]))
    o_out[...] = (residual[...] + total).astype(BF16)


def masked_softmax(logits, mask):
    on = mask > 0.0
    top = jnp.max(jnp.where(on, logits, -3.0e38), axis=-1, keepdims=True)
    e = jnp.where(on, jnp.exp(jnp.where(on, logits - top, 0.0)), 0.0)
    return e / jnp.sum(e, axis=-1, keepdims=True)


def mlp(x, do, wg, wu, wd, gate):
    g = dot(x, wg)
    u = dot(x, wu)
    sig = sigmoid(g)
    silu = g * sig
    hid = (silu * u).astype(BF16)
    dh = dot(do, wd, NT)
    if gate is None:
        hg, dgate = hid, None
    else:
        hf = hid.astype(F32)
        dgate = jnp.sum(hf * dh, axis=-1, keepdims=True)
        hg = (hf * gate).astype(BF16)
        dh = dh * gate
    dg = (dh * u * sig * (1.0 + g * (1.0 - sig))).astype(BF16)
    du = (dh * silu).astype(BF16)
    return hg, dg, du, dgate


def k_expert(slots, index, *refs):
    router, w_in, w_down = refs[:3]
    count = sum(slots)
    xs, ds = refs[3 : 3 + count], refs[3 + count : 3 + 2 * count]
    outs = refs[3 + 2 * count :]
    width = w_in.shape[2]
    wg, wu, wd = w_in[0, 0], w_in[0, 1], w_down[0]
    w = to_lanes(router[...])
    at = 0
    for i, pieces in enumerate(slots):
        o_out, o_dx, o_keep = outs[3 * i : 3 * i + 3]
        x = jnp.concatenate([xs[at + j][...] for j in range(pieces)], axis=0)
        dall = jnp.concatenate([ds[at + j][...] for j in range(pieces)], axis=0)
        at += pieces
        do = dall[:, :width]
        mask = dall[:, width:].astype(F32)
        lane = iota(mask.shape, 1)
        probs = masked_softmax(dot(x, w), mask)
        gate = jnp.sum(jnp.where(lane == index[0], probs, 0.0), axis=-1, keepdims=True)
        hg, dg, du, dgate = mlp(x, do, wg, wu, wd, gate)
        half = hg.shape[1]
        o_keep[:, :half] = hg
        o_keep[:, half : 2 * half] = dg
        o_keep[:, 2 * half :] = du
        o_out[...] = dot(hg, wd).astype(BF16)
        o_dx[:, :width] = (dot(dg, wg, NT) + dot(du, wu, NT)).astype(BF16)
        chosen = jnp.sum(jnp.where(lane == index[0], mask, 0.0), axis=-1, keepdims=True) > 0.0
        o_dx[:, width:] = jnp.where(jnp.logical_and(lane == index[0], chosen), dgate, 0.0).astype(BF16)


def k_shared(x, do, w_in, w_down, o_out, o_dx):
    width = w_in.shape[1]
    wg, wu, wd = w_in[0], w_in[1], w_down[...]
    hg, dg, du, _ = mlp(x[...], do[:, :width], wg, wu, wd, None)
    o_out[...] = dot(hg, wd).astype(BF16)
    o_dx[...] = (dot(dg, wg, NT) + dot(du, wu, NT)).astype(BF16)


def taken(xs, i, slots):
    at = sum(slots[:i])
    return jnp.concatenate([xs[at + j][...] for j in range(slots[i])], axis=0)


def k_weights(slots, index, *refs):
    s_in, s_down = refs[:2]
    pieces, count = sum(slots), len(slots)
    xs = refs[2 : 2 + pieces]
    ds = refs[2 + pieces : 2 + pieces + count]
    ks = refs[2 + pieces + count : 2 + pieces + 2 * count]
    o_in, o_down, o_s_in, o_s_down = refs[2 + pieces + 2 * count :]
    width, half = o_in.shape[1], o_in.shape[2]
    for i in range(count):
        x = taken(xs, i, slots)
        do = ds[i][:, :width]
        kept = ks[i][...]
        hg, dg, du, _ = mlp(x, do, s_in[0], s_in[1], s_down[...], None)
        parts = (
            dot(x, kept[:, half : 2 * half], TN),
            dot(x, kept[:, 2 * half :], TN),
            dot(kept[:, :half], do, TN),
            dot(x, dg, TN),
            dot(x, du, TN),
            dot(hg, do, TN),
        )
        into = (o_in.at[0], o_in.at[1], o_down, o_s_in.at[0], o_s_in.at[1], o_s_down)
        for ref, part in zip(into, parts):
            if i == 0:
                ref[...] = part
            else:
                ref[...] += part


def k_outer(slots_a, slots_b, count_b, *refs):
    refs = refs[1:]
    na = sum(slots_a)
    a_refs = refs[:na]
    b_refs = [refs[na + j * sum(slots_b) : na + (j + 1) * sum(slots_b)] for j in range(count_b)]
    outs = refs[na + count_b * sum(slots_b) :]
    totals = [None] * count_b
    for i in range(len(slots_a)):
        a = taken(a_refs, i, slots_a)
        for j in range(count_b):
            part = dot(a, taken(b_refs[j], i, slots_b), TN)
            totals[j] = part if totals[j] is None else totals[j] + part
    for j in range(count_b):
        outs[j][...] = totals[j]


def outer(a, bs, name):
    step = 256
    columns = a.pieces[0].shape[1]
    args, specs = [], []
    for g in (a, *bs):
        for piece in g.pieces:
            args.append(piece)
            if g is a:
                specs.append(pl.BlockSpec((piece.shape[0], step), lambda i, *_: (0, i)))
            else:
                specs.append(pl.BlockSpec(piece.shape, lambda i, *_: (0, 0)))
    widths = [b.pieces[0].shape[1] for b in bs]
    rows = sum(p.shape[0] for p in a.pieces)
    grid_spec = pltpu.PrefetchScalarGridSpec(
        num_scalar_prefetch=1,
        grid=(columns // step,),
        in_specs=specs,
        out_specs=[pl.BlockSpec((step, w), lambda i, *_: (i, 0)) for w in widths],
    )
    moved = sum(x.size * x.dtype.itemsize for x in args) + sum(4 * columns * w for w in widths)
    return pl.pallas_call(
        functools.partial(k_outer, a.slots, bs[0].slots, len(bs)),
        out_shape=[struct((columns, w), F32) for w in widths],
        grid_spec=grid_spec,
        compiler_params=pltpu.CompilerParams(vmem_limit_bytes=60 * 2**20),
        cost_estimate=pl.CostEstimate(
            flops=2 * rows * columns * sum(widths), bytes_accessed=int(moved), transcendentals=0
        ),
        name=name,
    )(a.index, *args)


def flip(array, axis, bit):
    return lax.ppermute(array, axis, [(i, i ^ bit) for i in range(lax.axis_size(axis))])


def bits_of(axis):
    return [1 << b for b in range(lax.axis_size(axis).bit_length() - 1)]


class Gathered:
    def __init__(self, pieces, slots, index):
        self.pieces, self.slots, self.index = pieces, slots, index

    def part(self, first, last):
        at, to = sum(self.slots[:first]), sum(self.slots[:last])
        return Gathered(self.pieces[at:to], self.slots[first:last], self.index[first:last])


XOR_ORDER = (0, 1, 2, 3, 4, 5, 6, 7)


def gather(own):
    size = lax.axis_size("seq")
    place = lax.axis_index("seq")
    if size != 8:
        every = lax.all_gather(own, "seq")
        return Gathered([every[k] for k in range(size)], [1] * size, jnp.arange(size, dtype=jnp.int32))
    core, x, y = bits_of("seq")
    half = own.shape[0] // 2
    by_x = flip(own, "seq", x)
    by_y = flip(own, "seq", y)
    top = flip(by_x[:half], "seq", y)
    bottom = flip(by_y[half:], "seq", x)
    near = [own, by_x, by_y, top, bottom]
    far = [flip(a, "seq", core) for a in near]
    pieces = [near[0], far[0], near[1], far[1], near[2], far[2], near[3], near[4], far[3], far[4]]
    index = jnp.stack([place ^ k for k in XOR_ORDER]).astype(jnp.int32)
    return Gathered(pieces, [1, 1, 1, 1, 1, 1, 2, 2], index)


def low_sum(*terms):
    return sum(t.astype(F32) for t in terms).astype(BF16)


def k_split(x0, x1, y0, y1, d0, d1, o_x, o_y, o_x_late, o_y_late):
    half = o_x_late.shape[0]
    x = low_sum(x0[...], x1[...])
    y = low_sum(y0[...], y1[...])
    d = low_sum(d0[...], d1[...])
    o_x[:half, :] = d[:half]
    o_x[half:, :] = x[:half]
    o_y[:half, :] = d[half:]
    o_y[half:, :] = y[half:]
    o_x_late[...] = x[half:]
    o_y_late[...] = y[:half]


def k_late(x, y, ax, ay, o_x, o_y):
    half = x.shape[0]
    o_x[...] = low_sum(x[...], ay[:half, :])
    o_y[...] = low_sum(y[...], ax[:half, :])


def k_join(a, b, more, ax, ay, bx, by, o):
    half = bx.shape[0]
    w = more.shape[1]
    total = a[...].astype(F32) + b[...].astype(F32)
    o[:half, :] = low_sum(total[:half], ax[half:, :], by[...])
    o[half:, :] = low_sum(total[half:], ay[half:, :], bx[...])
    o[:, :w] = low_sum(o[:, :w], more[...])


def scatter(parts, more, name):
    size = lax.axis_size("seq")
    if size != 8:
        every = jnp.concatenate(parts, axis=0)
        total = lax.psum_scatter(every, "seq", scatter_dimension=0, tiled=True)
        return jnp.concatenate(
            [low_sum(total[:, : more.shape[1]], more), total[:, more.shape[1] :]], axis=1
        )
    core, x, y = bits_of("seq")
    rows, width = parts[0].shape
    r1, r3, r5, r7 = (flip(parts[k], "seq", core) for k in (1, 3, 5, 7))
    full, part = struct((rows, width), BF16), struct((rows // 2, width), BF16)
    to_x, to_y, late_x, late_y = call(
        k_split, [full, full, part, part], [parts[2], r3, parts[4], r5, parts[6], r7], 0, name + "_split"
    )
    ax, ay = flip(to_x, "seq", x), flip(to_y, "seq", y)
    late_x, late_y = call(k_late, [part, part], [late_x, late_y, ax, ay], 0, name + "_late")
    bx, by = flip(late_x, "seq", x), flip(late_y, "seq", y)
    [out] = call(k_join, [full], [parts[0], r1, more, ax, ay, bx, by], 0, name + "_join")
    return out


def scan(send, backward, name):
    place = lax.axis_index("seq")
    seqs, size = send.shape[0], send.shape[1] - FRONT
    bits = bits_of("seq")
    state = struct((seqs, size, LANES), F32)
    row = struct((seqs, 8, LANES), F32)
    total = whole = before = reach = None
    own = send
    for bit in bits:
        recv = flip(send, "seq", bit)
        is_set = (place & bit) != 0
        after = (jnp.logical_not(is_set) if backward else is_set).astype(jnp.int32)[None]
        first, last = bit == bits[0], bit == bits[-1]
        outs = [state] if last else [state, row, state, row, struct(own.shape, BF16)]
        if first:
            held = []
            kernel = lambda after, recv, own, *o, last=last: k_scan(
                True, last, after, recv, own, None, None, None, None, *o
            )
        else:
            held = [Each(a) for a in (total, whole, before, reach)]
            kernel = functools.partial(k_scan, False, last)
        made = call(
            kernel,
            [Each(o) for o in outs],
            [Scalars(after), Each(recv), Each(own), *held],
            0,
            name,
            grid=seqs,
        )
        if last:
            return made[0]
        before, reach, whole, total, send = made
    return before


def rows_of_mp(array):
    share = array.shape[0] // lax.axis_size("mp")
    return lax.dynamic_slice_in_dim(array, lax.axis_index("mp") * share, share, 0)


def shares_of_mp(array):
    size = lax.axis_size("mp")
    cut = array.reshape(size, array.shape[0] // size, array.shape[1])
    return lax.all_to_all(cut, "mp", 0, 0, tiled=True)


def gather_mp(array):
    return lax.all_gather(array, "mp", tiled=True)


def all_sum(array, axes):
    for axis in axes:
        for bit in bits_of(axis):
            array = array + flip(array, axis, bit)
    return array


def passed_along(block, axis, distance):
    devices = range(lax.axis_size(axis))
    route = [(i - distance, i) for i in devices if i - distance in devices]
    return lax.ppermute(block, axis, route)


def body(
    tokens, lengths, expert_ids, norm_gains, in_z, in_x, in_bc, in_dt, conv_x, conv_bc,
    head_par, gn_gain, out_w, router, shared_in, shared_down, expert_in, expert_down, d_out,
):
    piece, seqs, model = tokens.shape
    width = in_z.shape[1]
    heads = head_par.shape[1]
    experts = router.shape[1]
    half = expert_in.shape[-1]
    n_seq, n_mp = lax.axis_size("seq"), lax.axis_size("mp")
    seq_at, mp_at = lax.axis_index("seq"), lax.axis_index("mp")
    rows = seqs * piece
    share = rows // n_mp
    bc = 2 * STATE

    meta = jnp.concatenate([lengths, (seq_at * piece).astype(jnp.int32)[None]])
    tok = jnp.transpose(tokens, (1, 0, 2))
    edge_in = passed_along(tokens[piece - (KCONV - 1) :], "seq", 1)
    front = jnp.pad(jnp.transpose(edge_in, (1, 0, 2)), ((0, 0), (FRONT - (KCONV - 1), 0), (0, 0)))
    tok_front = jnp.concatenate([front, tok], axis=1)
    gn = gn_gain[None]
    picked = jnp.sum(
        (expert_ids[..., None] == jnp.arange(LANES, dtype=jnp.int32)).astype(F32), axis=2
    ).astype(BF16)
    small = [conv_x, conv_bc, head_par, Scalars(meta)]

    def both(*shape, dtype=F32):
        return Each(struct((seqs, *shape), dtype))

    normed, gate_z, xbc, dt_raw, send, totals = call(
        k_in,
        [
            both(piece, model, dtype=BF16),
            both(piece, width),
            both(piece + FRONT, width + bc, dtype=BF16),
            both(piece, LANES),
            both(width + FRONT, LANES, dtype=BF16),
            both(8, LANES),
        ],
        [Each(tok_front), norm_gains, in_z, in_x, in_bc, in_dt, *small],
        2 * rows * model * (2 * width + bc + LANES),
        "mixer_in",
        grid=seqs,
    )
    d_ext, send = lax.optimization_barrier((jnp.transpose(jnp.concatenate([d_out, picked], axis=-1), (1, 0, 2)), send))
    d_ext = d_ext.reshape(rows, model + LANES)
    d_all = lax.all_gather(d_ext, "seq", tiled=True)
    entering = scan(send, False, "scan")
    intra, c_mat, ecum = call(
        k_intra,
        [both(piece, width), both(piece, STATE, dtype=BF16), both(piece, width)],
        [Each(xbc), Each(dt_raw), *small],
        2 * rows * piece * width * 4,
        "mixer_intra",
        grid=seqs,
    )
    mixed, part = call(
        k_out,
        [both(piece, width), both(piece, model + LANES, dtype=BF16)],
        [Each(intra), Each(c_mat), Each(ecum), Each(entering), Each(gate_z), gn, out_w],
        2 * rows * width * (STATE + model),
        "mixer_out",
        grid=seqs,
    )
    tok_own = rows_of_mp(tok.reshape(rows, model))
    d_own = rows_of_mp(d_ext)
    arrived = shares_of_mp(part.reshape(rows, model + LANES))
    normed, part = lax.optimization_barrier((normed, part))
    if n_seq == 8:
        n_got = gather(normed.reshape(rows, model))
    of_share = struct((share, model), F32)
    residual, mixer_own, two_own, scales = call(
        k_rows_one,
        [of_share, of_share, struct((share, model), BF16), struct((share, LANES), F32)],
        [arrived, tok_own, norm_gains],
        0,
        "rows_one",
    )
    two = gather_mp(two_own)

    out_shared, dx_shared = call(
        k_shared,
        [struct((rows, model), BF16), struct((rows, model), BF16)],
        [two, d_ext, shared_in, shared_down],
        2 * rows * model * half * 6,
        "shared",
    )
    x_got = gather(two)
    mine = ((seq_at * n_mp + mp_at) // 2).astype(jnp.int32)[None]
    groups = [(0, 2), (2, 6), (6, 8)] if n_seq == 8 else [(i, i + 4) for i in range(0, n_seq, 4)]
    e_out, e_dx, e_keep = [], [], []
    for first, last in groups:
        part_x = x_got.part(first, last)
        blocks, at = [mine], 1
        d_blocks = []
        for i, pieces in enumerate(part_x.slots):
            for j in range(pieces):
                blocks.append(part_x.index[i : i + 1] * pieces + j)
                d_blocks.append(Block(d_all, rows // pieces, at))
                at += 1
        outs = [
            struct((rows, model), BF16),
            struct((rows, model + LANES), BF16),
            struct((rows, 3 * half), BF16),
        ] * (last - first)
        made = call(
            functools.partial(k_expert, part_x.slots),
            outs,
            [router, expert_in, expert_down, *part_x.pieces, *d_blocks],
            2 * rows * (last - first) * model * half * 6.5,
            "experts",
            index=jnp.concatenate(blocks),
        )
        e_out += made[0::3]
        e_dx += made[1::3]
        e_keep += made[2::3]

    arrived = shares_of_mp(scatter(e_dx, dx_shared, "dx"))
    g_expert_in = g_expert_down = g_shared_in = g_shared_down = 0.0
    for at in range(0, n_seq, 8):
        now = x_got.part(at, at + 8)
        flops = 2 * 8 * rows * model * half
        made = call(
            functools.partial(k_weights, now.slots),
            [struct((2, model, half), F32), struct((half, model), F32)] * 2,
            [shared_in, shared_down, *now.pieces]
            + [Block(d_all, rows, i) for i in range(8)]
            + e_keep[at : at + 8],
            9 * flops,
            "expert_weights",
            index=now.index,
        )
        g_expert_in, g_expert_down = g_expert_in + made[0], g_expert_down + made[1]
        g_shared_in, g_shared_down = g_shared_in + made[2], g_shared_down + made[3]

    dm_own, d_residual, g_gain_two, g_router = call(
        k_rows_two,
        [
            struct((share, model + LANES), BF16),
            of_share,
            struct((8, model), F32),
            struct((experts, model), F32),
        ],
        [arrived, d_own, two_own, residual, mixer_own, scales, norm_gains, router],
        0,
        "rows_two",
    )
    dm = gather_mp(dm_own).reshape(seqs, piece, model + LANES)

    dz, dy, send, g_gn, normed_y = call(
        k_back_gate,
        [
            both(piece, width, dtype=BF16),
            both(piece, width),
            both(width + FRONT, LANES, dtype=BF16),
            both(8, width),
            both(piece, width, dtype=BF16),
        ],
        [Each(dm), Each(mixed), Each(gate_z), gn, out_w, Each(c_mat), Each(ecum), Each(totals)],
        2 * rows * width * (model + STATE),
        "back_gate",
        grid=seqs,
    )
    leaving = scan(send, True, "scan_back")
    if n_seq != 8:
        normed, leaving = lax.optimization_barrier((normed, leaving))
        n_got = gather(normed.reshape(rows, model))
    g_out_w = lax.dot_general(
        normed_y.reshape(rows, width), dm.reshape(rows, model + LANES)[:, :model], TN, preferred_element_type=F32
    )
    g_out_w = lax.psum(g_out_w.astype(BF16), "seq").astype(F32)

    out_arrived = shares_of_mp(scatter(e_out, out_shared, "out"))
    [out_own] = call(
        k_rows_out, [struct((share, model), BF16)], [out_arrived, residual], 0, "rows_out"
    )
    output = jnp.transpose(gather_mp(out_own).reshape(seqs, piece, model), (1, 0, 2)).astype(F32)

    dz_got = gather(dz.reshape(rows, width))
    dxw0, db0, dc0, dcum0, dn0 = call(
        k_back_intra,
        [both(piece, width), both(piece, STATE), both(piece, STATE), both(piece, LANES), both(piece, model)],
        [Each(xbc), Each(dt_raw), *small, Each(dy), Each(dz), in_z],
        2 * rows * width * (model + 4 * piece),
        "back_intra",
        grid=seqs,
    )
    d_xbc, d_dt, g_conv, g_hp = call(
        k_back_state,
        [
            both(piece + FRONT, width + bc),
            both(piece, LANES, dtype=BF16),
            both(8, width + bc),
            both(8, LANES),
        ],
        [
            Each(xbc), Each(dt_raw), *small, Each(dy), Each(dxw0), Each(db0), Each(dc0), Each(dcum0),
            Each(entering), Each(leaving),
        ],
        2 * rows * width * STATE * 20,
        "back_state",
        grid=seqs,
    )
    edge = passed_along(d_xbc[:, :FRONT], "seq", -1)
    part, dx, d_bc, g_gain_one = call(
        k_back_in,
        [
            both(piece, model, dtype=BF16),
            both(piece, width + LANES, dtype=BF16),
            both(piece, bc, dtype=BF16),
            both(8, model),
        ],
        [Each(dn0), Each(d_xbc), Each(edge), Each(d_dt), Each(tok_front), in_x, in_bc, in_dt],
        2 * rows * (width + bc + LANES) * model,
        "back_in",
        grid=seqs,
    )
    arrived = shares_of_mp(part.reshape(rows, model))
    d_bc = all_sum(d_bc.reshape(rows, bc), ("mp",))
    dx_got = gather(dx.reshape(rows, width + LANES))
    bc_got = gather(d_bc)
    [dtok_own] = call(
        k_rows_three, [struct((share, model), BF16)], [arrived, tok_own, d_residual, norm_gains], 0, "rows_three"
    )
    d_tokens = jnp.transpose(gather_mp(dtok_own).reshape(seqs, piece, model), (1, 0, 2)).astype(F32)

    g_in_z = g_in_x = g_in_bc = 0.0
    for at in range(0, n_seq, 8):
        now = n_got.part(at, at + 8)
        [a] = outer(now, [dz_got.part(at, at + 8)], "weights_z")
        b, c = outer(now, [dx_got.part(at, at + 8), bc_got.part(at, at + 8)], "weights_x")
        g_in_z, g_in_x, g_in_bc = g_in_z + a, g_in_x + b, g_in_bc + c

    g_conv = jnp.sum(g_conv, axis=0)
    g_gn, g_hp = jnp.sum(g_gn, axis=0)[:1], jnp.sum(g_hp, axis=0)[:3]
    rest = model - width - LANES
    along = jnp.concatenate(
        [
            jnp.concatenate([g_conv[: KCONV + 1, :width], g_gn, jnp.zeros((2, width), F32)], axis=0),
            jnp.pad(g_hp, ((0, 5), (0, rest))),
        ],
        axis=1,
    )
    every = jnp.concatenate(
        [
            jnp.pad(g_conv[: KCONV + 1, width:], ((0, 0), (0, model - bc))),
            jnp.sum(g_gain_one, axis=0)[:1],
            g_gain_two[:2],
            g_router,
        ],
        axis=0,
    )
    summed = all_sum(jnp.concatenate([along, every], axis=0), ("seq",))
    every = all_sum(summed[8:], ("mp",))
    return (
        output,
        d_tokens,
        every[5:7],
        g_in_z,
        g_in_x[:, :width],
        g_in_bc,
        g_in_x[:, width : width + heads],
        summed[: KCONV + 1, :width],
        every[: KCONV + 1, :bc],
        summed[:3, width : width + heads],
        summed[KCONV + 1, :width],
        g_out_w,
        every[8:].T,
        g_shared_in,
        g_shared_down,
        g_expert_in[None],
        g_expert_down[None],
    )


def solution(mesh):
    in_specs = (
        P("seq", None, None),
        P(),
        P("seq", None, None),
        P(),
        P(None, "mp"),
        P(None, "mp"),
        P(),
        P(None, "mp"),
        P(None, "mp"),
        P(),
        P(None, "mp"),
        P("mp"),
        P("mp", None),
        P(),
        P(None, None, "mp"),
        P("mp", None),
        P(("seq", "mp"), None, None, None),
        P(("seq", "mp"), None, None),
        P("seq", None, None),
    )
    out_specs = (
        P("seq", None, None),
        P("seq", None, None),
        P(),
        P(None, "mp"),
        P(None, "mp"),
        P(),
        P(None, "mp"),
        P(None, "mp"),
        P(),
        P(None, "mp"),
        P("mp"),
        P("mp", None),
        P(),
        P(None, None, "mp"),
        P("mp", None),
        P(("seq", "mp"), None, None, None),
        P(("seq", "mp"), None, None),
    )
    return jax.shard_map(body, mesh=mesh, in_specs=in_specs, out_specs=out_specs, check_vma=False)
```

```python
import functools

import jax
import jax.numpy as jnp
from jax import lax
from jax.experimental import pallas as pl
from jax.experimental.pallas import tpu as pltpu
from jax.sharding import PartitionSpec as P

HEAD_DIM = 64
STATE = 128
KCONV = 4
INNER = 3072
LANES = 128
SMALL = 16
FRONT = 16
EPSILON = 1e-05
F32 = jnp.float32
BF16 = jnp.bfloat16
HIGHEST = lax.Precision.HIGHEST
NN = (((1,), (0,)), ((), ()))
NT = (((1,), (1,)), ((), ()))
TN = (((0,), (0,)), ((), ()))


class Each:
    def __init__(self, array):
        self.array = array


class Scalars:
    def __init__(self, array):
        self.array = array


class Far:
    def __init__(self, array):
        self.array = array


class Rows:
    def __init__(self, array, rows):
        self.array, self.rows = array, rows


def struct(shape, dtype):
    return jax.ShapeDtypeStruct(tuple(shape), dtype)


def call(kernel, outs, args, flops, name, grid=1, index=None, scratch=(), aliases=None):
    def spec(a):
        if isinstance(a, Scalars):
            return pl.BlockSpec(memory_space=pltpu.SMEM)
        if isinstance(a, Far):
            return pl.BlockSpec(memory_space=pl.ANY)
        if isinstance(a, Rows):
            rest = a.array.shape[1:]
            return pl.BlockSpec((a.rows, *rest), lambda s, *_: (s,) + (0,) * len(rest))
        if isinstance(a, Each):
            rest = a.array.shape[1:]
            return pl.BlockSpec((None, *rest), lambda s, *_: (s,) + (0,) * len(rest))
        return pl.BlockSpec(a.shape, lambda s, *_: (0,) * len(a.shape))

    def plain(a):
        return a.array if isinstance(a, (Each, Scalars, Far, Rows)) else a

    arrays = [plain(a) for a in args]
    shapes = [plain(a) for a in outs]
    moved = sum(a.size * a.dtype.itemsize for a in (*arrays, *shapes))
    grid_spec = pltpu.PrefetchScalarGridSpec(
        num_scalar_prefetch=0 if index is None else 1,
        grid=(grid,),
        in_specs=[spec(a) for a in args],
        out_specs=[spec(a) for a in outs],
        scratch_shapes=list(scratch),
    )
    return pl.pallas_call(
        kernel,
        out_shape=shapes,
        grid_spec=grid_spec,
        input_output_aliases=aliases or {},
        compiler_params=pltpu.CompilerParams(vmem_limit_bytes=60 * 2**20),
        cost_estimate=pl.CostEstimate(flops=int(flops), bytes_accessed=int(moved), transcendentals=0),
        name=name,
    )(*([] if index is None else [index]), *arrays)


def dot(a, b, dims=NN):
    return lax.dot_general(a.astype(BF16), b.astype(BF16), dims, preferred_element_type=F32)


def exact(a, b, dims=NN):
    return lax.dot_general(a, b, dims, precision=HIGHEST, preferred_element_type=F32)


def sigmoid(v):
    return 1.0 / (1.0 + jnp.exp(-v))


def iota(shape, axis):
    return lax.broadcasted_iota(jnp.int32, shape, axis)


def two_terms(v):
    high = v.astype(BF16)
    return high, (v - high.astype(F32)).astype(BF16)


def to_lanes(v):
    return jnp.concatenate([v, jnp.zeros((v.shape[0], LANES - v.shape[1]), v.dtype)], axis=1)


def spread_matrix(width):
    return (iota((LANES, width), 1) // HEAD_DIM == iota((LANES, width), 0)).astype(F32)


def prepared(xbc, dt, conv_x, conv_bc, head_par, meta):
    rows = dt.shape[0]
    width = conv_x.shape[1]
    conv = jnp.concatenate([conv_x[...], conv_bc[...]], axis=1)
    hp = to_lanes(head_par[...])
    where = iota((rows, 1), 0) + meta[2]
    live = (where < meta[pl.program_id(0)]).astype(F32)
    xf = xbc[...].astype(F32)
    summed = conv[KCONV : KCONV + 1]
    taps = []
    for j in range(KCONV):
        shifted = xf[FRONT - (KCONV - 1) + j : FRONT - (KCONV - 1) + j + rows]
        taps.append(shifted)
        summed = summed + conv[j : j + 1] * shifted
    sig = sigmoid(summed)
    act = summed * sig
    xs = act[:, :width] * live
    b = act[:, width : width + STATE]
    c = act[:, width + STATE :]
    raw = dt[...] + hp[0:1]
    step = (jnp.maximum(raw, 0.0) + jnp.log1p(jnp.exp(-jnp.abs(raw)))) * live
    rate = -jnp.exp(hp[1:2])
    logd = rate * step
    lower = (iota((rows, rows), 0) >= iota((rows, rows), 1)).astype(F32)
    cum = exact(lower, logd)
    return dict(
        conv=conv, skip=hp[2:3], live=live, taps=taps, summed=summed, sig=sig, xs=xs, b=b, c=c, raw=raw,
        step=step, rate=rate, logd=logd, cum=cum,
    )


def pack_state(o_send, state, decay):
    size = state.shape[0]
    high, low = two_terms(decay)
    row = iota((FRONT, LANES), 0)
    more = jnp.where(row == 0, high.astype(F32), 0.0) + jnp.where(row == 1, low.astype(F32), 0.0)
    o_send[:size, :] = state.astype(BF16)
    o_send[size:, :] = more.astype(BF16)


def unpack_state(send):
    size = send.shape[0] - FRONT
    more = send[size:, :].astype(F32)
    return send[:size, :].astype(F32), more[0:1] + more[1:2]


def k_in(tok, gains, wz, wx, wbc, wdt, conv_x, conv_bc, head_par, meta, o_norm, o_z, o_xbc, o_dt, o_send, o_tot):
    width = wz.shape[1]
    x = tok[...].astype(F32)
    scale = lax.rsqrt(jnp.mean(x * x, axis=-1, keepdims=True) + EPSILON)
    normed = (x * scale * gains[0:1]).astype(BF16)
    own = normed[FRONT:]
    o_norm[...] = own
    o_xbc[:, :width] = dot(normed, wx[...]).astype(BF16)
    o_xbc[:, width:] = dot(normed, wbc[...]).astype(BF16)
    o_dt[...] = to_lanes(dot(own, wdt[...]))
    o_z[...] = dot(own, wz[...])
    p = prepared(o_xbc, o_dt, conv_x, conv_bc, head_par, meta)
    rows = own.shape[0]
    last = p["cum"][rows - 1 : rows]
    weight = exact(p["step"] * jnp.exp(last - p["cum"]), spread_matrix(width))
    decay = jnp.exp(last)
    pack_state(o_send, dot(p["xs"] * weight, p["b"], TN), decay)
    o_tot[...] = jnp.broadcast_to(decay, o_tot.shape)


def pair_masks(rows):
    low = iota((rows, LANES), 1) < HEAD_DIM
    return low, jnp.logical_not(low)


def decays(cum, cum_t, h, ahead):
    gap = cum[:, h : h + 1] - cum_t[h : h + 1, :]
    return jnp.where(ahead, jnp.exp(jnp.where(ahead, gap, 0.0)), 0.0)


def by_halves(v, low, high):
    return jnp.concatenate(
        [jnp.where(low, v, 0.0).astype(BF16), jnp.where(high, v, 0.0).astype(BF16)], axis=0
    )


def k_intra(xbc, dt, conv_x, conv_bc, head_par, meta, o_y, o_c, o_ecum):
    width = o_y.shape[1]
    p = prepared(xbc, dt, conv_x, conv_bc, head_par, meta)
    xs, cum = p["xs"], p["cum"]
    rows = cum.shape[0]
    spread = spread_matrix(width)
    ahead = iota((rows, rows), 0) >= iota((rows, rows), 1)
    cum_t = cum.T
    scores = dot(p["c"], p["b"], NT)
    spread_out = exact(
        jnp.concatenate([p["step"], jnp.exp(cum), jnp.broadcast_to(p["skip"], (8, LANES))], axis=0), spread
    )
    xw = xs * spread_out[:rows]
    skip = spread_out[2 * rows : 2 * rows + 1]
    low, high = pair_masks(rows)
    o_c[...] = p["c"].astype(BF16)
    o_ecum[...] = spread_out[rows : 2 * rows]
    for pair in range(width // LANES):
        cols = slice(pair * LANES, (pair + 1) * LANES)
        mats = [(decays(cum, cum_t, h, ahead) * scores).astype(BF16) for h in (2 * pair, 2 * pair + 1)]
        within = dot(jnp.concatenate(mats, axis=1), by_halves(xw[:, cols], low, high))
        o_y[:, cols] = within + skip[:, cols] * xs[:, cols]


def k_scan(first, last, after, recv, own, *refs):
    whole, total = unpack_state(own)
    state, decay = unpack_state(recv)
    size = state.shape[0]
    mine = iota((size, LANES), 1) == iota((size, LANES), 0) // HEAD_DIM

    def rows_of(d):
        return jnp.sum(jnp.where(mine, d, 0.0), axis=1, keepdims=True)

    is_after = after[0] == 1
    if first:
        outs = refs
        outs[0][...] = jnp.where(is_after, state, 0.0)
        new_reach = jnp.where(is_after, decay, 1.0)
    else:
        before, reach = refs[:2]
        outs = refs[2:]
        outs[0][...] = jnp.where(is_after, before[...] + rows_of(reach[0:1]) * state, before[...])
        new_reach = jnp.where(is_after, reach[0:1] * decay, reach[0:1])
    if last:
        return
    outs[1][...] = jnp.broadcast_to(new_reach, outs[1].shape)
    new_whole = jnp.where(is_after, whole + rows_of(total) * state, state + rows_of(decay) * whole)
    pack_state(outs[2], new_whole, total * decay)


def k_out(y0, c, ecum, entering, z, gain, w, o_y, o_u, o_part):
    model = w.shape[1]
    y = y0[...] + ecum[...] * dot(c[...], entering[...], NT)
    o_y[...] = y
    zv = z[...]
    gated = y * zv * sigmoid(zv)
    high, low = two_terms(jnp.sum(gated * gated, axis=-1, keepdims=True))
    o_u[...] = (gated * gain[...]).astype(BF16)
    o_part[:, :model] = dot(o_u[...], w[...]).astype(BF16)
    o_part[:, model:] = to_lanes(jnp.concatenate([high, low], axis=1))


def k_back_gate(dm, y, z, gain, w, c, ecum, total, o_dz, o_dy, o_send, o_gain):
    model = w.shape[1]
    more = dm[:, model:].astype(F32)
    stat = more[:, 0:1] + more[:, 1:2]
    scale = more[:, 2:3] + more[:, 3:4]
    dn = dot(dm[:, :model], w[...], NT)
    zv = z[...]
    sig = sigmoid(zv)
    silu = zv * sig
    yv = y[...]
    gated = yv * silu
    dgated = scale * gain[...] * dn - gated * (scale * scale * stat / INNER)
    o_dz[...] = (dgated * yv * sig * (1.0 + zv * (1.0 - sig))).astype(BF16)
    dy = dgated * silu
    o_dy[...] = dy
    o_gain[...] = jnp.broadcast_to(jnp.sum(dn * gated * scale, axis=0, keepdims=True), o_gain.shape)
    pack_state(o_send, dot(ecum[...] * dy, c[...], TN), total[0:1])


def k_back_intra(xbc, dt, conv_x, conv_bc, head_par, meta, dy, dz, wz, o_dxw, o_db, o_dc, o_dcum, o_dn):
    width = dy.shape[1]
    p = prepared(xbc, dt, conv_x, conv_bc, head_par, meta)
    cum = p["cum"]
    rows = cum.shape[0]
    o_dn[...] = dot(dz[...], wz[...], NT)
    ahead = iota((rows, rows), 0) >= iota((rows, rows), 1)
    cum_t = cum.T
    scores = dot(p["c"], p["b"], NT)
    xw = p["xs"] * exact(p["step"], spread_matrix(width))
    low, high = pair_masks(rows)
    lane = iota((rows, LANES), 1)
    sub = iota((LANES, rows), 0)
    dscores = jnp.zeros((rows, rows), F32)
    plus = jnp.zeros((rows, LANES), F32)
    minus = jnp.zeros((LANES, rows), F32)
    for pair in range(width // LANES):
        cols = slice(pair * LANES, (pair + 1) * LANES)
        dstack = by_halves(dy[:, cols], low, high)
        dmats = dot(dstack, xw[:, cols], NT)
        mats = []
        for i, h in enumerate((2 * pair, 2 * pair + 1)):
            decay = decays(cum, cum_t, h, ahead)
            mat = decay * scores
            dmat = dmats[i * rows : (i + 1) * rows]
            dscores = dscores + dmat * decay
            flow = dmat * mat
            plus = jnp.where(lane == h, jnp.sum(flow, axis=1, keepdims=True), plus)
            minus = jnp.where(sub == h, jnp.sum(flow, axis=0, keepdims=True), minus)
            mats.append(mat.astype(BF16))
        o_dxw[:, cols] = dot(jnp.concatenate(mats, axis=0), dstack, TN)
    o_dcum[...] = plus - minus.T
    o_dc[...] = dot(dscores, p["b"])
    o_db[...] = dot(dscores, p["c"], TN)


def k_back_state(
    xbc, dt, conv_x, conv_bc, head_par, meta, dy, dxw0, db0, dc0, dcum0, entering, leaving,
    o_dxbc, o_ddt, o_conv, o_hp,
):
    width = dy.shape[1]
    p = prepared(xbc, dt, conv_x, conv_bc, head_par, meta)
    xs, b, c, cum, step, rate, live = (p[k] for k in ("xs", "b", "c", "cum", "step", "rate", "live"))
    summed, sig, conv = p["summed"], p["sig"], p["conv"]
    rows = cum.shape[0]
    spread = spread_matrix(width)
    last = cum[rows - 1 : rows]
    spread_out = exact(
        jnp.concatenate(
            [step, jnp.exp(cum), jnp.exp(last - cum), jnp.broadcast_to(p["skip"], (8, LANES))], axis=0
        ),
        spread,
    )
    step_x, ecum_x, rem_x = (spread_out[i * rows : (i + 1) * rows] for i in range(3))
    skip_x = spread_out[3 * rows : 3 * rows + 1]
    dyv = dy[...]
    h0 = entering[...]
    h1 = leaving[...]
    xw = xs * step_x
    scaled_dy = ecum_x * dyv
    dc = dc0[...] + dot(scaled_dy, h0)
    from_state = scaled_dy * dot(c, h0, NT)
    to_state = rem_x * dot(b, h1, NT)
    dxw = dxw0[...] + to_state
    db = db0[...] + dot(xw * rem_x, h1)
    dtotal = jnp.sum(exact(spread, h1 * h0), axis=1, keepdims=True)
    sums = exact(jnp.concatenate([from_state, xw * to_state, dxw * xs, dyv * xs], axis=0), spread, NT)
    flow = sums[rows : 2 * rows]
    dlast = jnp.broadcast_to(dtotal, (LANES, LANES)).T[0:1] * jnp.exp(last) + jnp.sum(
        flow, axis=0, keepdims=True
    )
    dcum = dcum0[...] + sums[:rows] - flow
    dcum = dcum + jnp.where(iota((rows, LANES), 0) == rows - 1, dlast, 0.0)
    upper = (iota((rows, rows), 0) <= iota((rows, rows), 1)).astype(F32)
    dlogd = exact(upper, dcum)
    draw = (sums[2 * rows : 3 * rows] + dlogd * rate) * live * sigmoid(p["raw"])
    o_ddt[...] = draw.astype(BF16)
    row = iota((8, LANES), 0)
    o_hp[...] = (
        jnp.where(row == 0, jnp.sum(draw, axis=0, keepdims=True), 0.0)
        + jnp.where(row == 1, jnp.sum(dlogd * p["logd"], axis=0, keepdims=True), 0.0)
        + jnp.where(row == 2, jnp.sum(sums[3 * rows : 4 * rows], axis=0, keepdims=True), 0.0)
    )
    dx = (dxw * step_x + skip_x * dyv) * live
    dsummed = jnp.concatenate([dx, db, dc], axis=1) * sig * (1.0 + summed * (1.0 - sig))
    zeros = jnp.zeros((FRONT, dsummed.shape[1]), F32)
    padded = jnp.concatenate([zeros, dsummed, zeros], axis=0)
    total = rows + FRONT
    out = jnp.zeros((total, dsummed.shape[1]), F32)
    for j in range(KCONV):
        shift = KCONV - 1 - j
        out = out + conv[j : j + 1] * padded[shift : shift + total]
        o_conv[j : j + 1] = jnp.sum(dsummed * p["taps"][j], axis=0, keepdims=True)
    o_conv[KCONV : KCONV + 1] = jnp.sum(dsummed, axis=0, keepdims=True)
    o_conv[KCONV + 1 :] = jnp.zeros((o_conv.shape[0] - KCONV - 1, dsummed.shape[1]), F32)
    o_dxbc[...] = out


def beside_rows(experts, model):
    need = (experts + 2) * model // (2 * STATE) + KCONV + 1
    return -(-need // 64) * 64


def k_back_in(dn0, dxbc, edge, ddt, tok, g_conv, g_hp, g_gn, g_two, wx, wbc, wdt, o_dx, o_bc, o_part, gain):
    width = wx.shape[1]
    rows, model = dn0.shape
    experts = g_two.shape[0] - 8
    step = pl.program_id(0)
    tail = jnp.concatenate([jnp.zeros((rows - FRONT, edge.shape[1]), F32), edge[...]], axis=0)
    own = (dxbc[FRONT:, :] + tail).astype(BF16)
    dx, dbc = own[:, :width], own[:, width:]
    to = pl.ds(pl.multiple_of(step * rows, rows), rows)
    o_dx[to, :width] = dx
    o_dx[to, width:] = ddt[...]
    o_bc[to, :] = dbc
    dn = dn0[...] + dot(dx, wx[...], NT) + dot(dbc, wbc[...], NT) + dot(ddt[...], to_lanes(wdt[...]), NT)
    o_part[...] = dn.astype(BF16)
    x = tok[FRONT:, :].astype(F32)
    scale = lax.rsqrt(jnp.mean(x * x, axis=-1, keepdims=True) + EPSILON)
    now = jnp.sum(dn * x * scale, axis=0, keepdims=True)

    @pl.when(step == 0)
    def _():
        gain[0:1, :] = now

    @pl.when(step > 0)
    def _():
        gain[0:1, :] += now

    @pl.when(step == pl.num_programs(0) - 1)
    def _():
        conv = jnp.sum(g_conv[...], axis=0)
        left = jnp.concatenate(
            [
                conv[: KCONV + 1, :width],
                jnp.sum(g_gn[...], axis=0)[0:1],
                jnp.zeros((SMALL - KCONV - 2, width), F32),
            ],
            axis=0,
        )
        right = jnp.concatenate([jnp.sum(g_hp[...], axis=0), jnp.zeros((SMALL - 8, LANES), F32)], axis=0)
        below = rows * pl.num_programs(0)
        more = pl.ds(pl.multiple_of(below, rows), SMALL)
        o_dx[more, :width] = left.astype(BF16)
        o_dx[more, width:] = right.astype(BF16)
        bc = dbc.shape[1]
        cuts = [slice(j * bc, (j + 1) * bc) for j in range(model // bc)]
        kept = [g_two[:experts, c] for c in cuts]
        kept += [gain[0:1, c] for c in cuts] + [g_two[experts : experts + 1, c] for c in cuts]
        kept.append(conv[: KCONV + 1, width:])
        size = beside_rows(experts, model)
        kept.append(jnp.zeros((size - sum(k.shape[0] for k in kept), bc), F32))
        o_bc[pl.ds(pl.multiple_of(below, rows), size), :] = jnp.concatenate(kept, axis=0).astype(BF16)


def total_of(arrived):
    return sum(arrived[k].astype(F32) for k in range(arrived.shape[0]))


def k_rows_one(tok, gains, arrived, o_residual, o_mixer, o_two, o_scales):
    model = tok.shape[1]
    total = total_of(arrived)
    scale = lax.rsqrt((total[:, model : model + 1] + total[:, model + 1 : model + 2]) / INNER + EPSILON)
    mixer = total[:, :model] * scale
    residual = tok[...].astype(F32) + mixer
    scale_two = lax.rsqrt(jnp.mean(residual * residual, axis=-1, keepdims=True) + EPSILON)
    o_residual[...] = residual
    o_mixer[...] = mixer
    o_two[...] = (residual * scale_two * gains[1:2]).astype(BF16)
    o_scales[...] = to_lanes(jnp.concatenate([scale, scale_two], axis=1))


def k_rows_two(dout, two, residual, mixer, scales, gains, router, arrived, o_dm, o_dr, o_small):
    model = two.shape[1]
    experts = router.shape[1]
    both = total_of(arrived)
    dn2, dgate = both[:, :model], both[:, model:]
    w = to_lanes(router[...])
    probs = masked_softmax(dot(two[...], w), dout[:, model:].astype(F32))
    dlog = (probs * (dgate - jnp.sum(probs * dgate, axis=-1, keepdims=True))).astype(BF16)
    dn2 = dn2 + dot(dlog, w, NT)
    scale, scale_two = scales[:, 0:1], scales[:, 1:2]
    scaled = residual[...] * scale_two
    o_small[:experts, :] = dot(dlog, two[...], TN)[:experts]
    o_small[experts:, :] = jnp.broadcast_to(jnp.sum(dn2 * scaled, axis=0, keepdims=True), (8, model))
    gg = dn2 * gains[1:2]
    dr = dout[:, :model].astype(F32) + scale_two * (
        gg - scaled * jnp.mean(gg * scaled, axis=-1, keepdims=True)
    )
    o_dr[...] = dr
    dm = dr.astype(BF16)
    stat = jnp.sum(dm.astype(F32) * mixer[...], axis=-1, keepdims=True)
    o_dm[:, :model] = dm
    o_dm[:, model:] = to_lanes(jnp.concatenate([*two_terms(stat), *two_terms(scale)], axis=1))


def k_rows_out(residual, arrived, o):
    out = (residual[...] + total_of(arrived)).astype(BF16)
    for k in range(o.shape[0]):
        o[k] = out


def k_rows_three(tok, dr, gains, arrived, o):
    dn1 = total_of(arrived)
    x = tok[...].astype(F32)
    scale = lax.rsqrt(jnp.mean(x * x, axis=-1, keepdims=True) + EPSILON)
    scaled = x * scale
    gg = dn1 * gains[0:1]
    dtok = (dr[...] + scale * (gg - scaled * jnp.mean(gg * scaled, axis=-1, keepdims=True))).astype(BF16)
    for k in range(o.shape[0]):
        o[k] = dtok


def masked_softmax(logits, mask):
    on = mask > 0.0
    top = jnp.max(jnp.where(on, logits, -3.0e38), axis=-1, keepdims=True)
    e = jnp.where(on, jnp.exp(jnp.where(on, logits - top, 0.0)), 0.0)
    return e / jnp.sum(e, axis=-1, keepdims=True)


def mlp(x, do, wg, wu, wd, gate):
    g = dot(x, wg)
    u = dot(x, wu)
    sig = sigmoid(g)
    silu = g * sig
    hid = (silu * u).astype(BF16)
    dh = dot(do, wd, NT)
    if gate is None:
        hg, dgate = hid, None
    else:
        hf = hid.astype(F32)
        dgate = jnp.sum(hf * dh, axis=-1, keepdims=True)
        hg = (hf * gate).astype(BF16)
        dh = dh * gate
    dg = (dh * u * sig * (1.0 + g * (1.0 - sig))).astype(BF16)
    du = (dh * silu).astype(BF16)
    return hg, dg, du, dgate


def start_all(copies):
    made = [pltpu.make_async_copy(src, dst, sem) for src, dst, sem in copies]
    for c in made:
        c.start()
    return made


def piece_copies(xs, slots, buffer, sems):
    out, at = [], 0
    rows = buffer.shape[0] // len(slots)
    for i, pieces in enumerate(slots):
        size = rows // pieces
        out.append(
            start_all(
                (xs[at + j].at[pl.ds(0, size)], buffer.at[pl.ds(i * rows + j * size, size)], sems.at[at + j])
                for j in range(pieces)
            )
        )
        at += pieces
    return out


def finish(copies):
    for c in copies:
        c.wait()


def k_expert(slots, with_shared, index, *refs):
    mine, router, w_in, w_down = refs[:4]
    pieces, count = sum(slots), len(slots)
    xs, ds = refs[4 : 4 + pieces], refs[4 + pieces : 4 + 2 * pieces]
    shared = refs[4 + 2 * pieces : 6 + 2 * pieces] if with_shared else ()
    refs = refs[len(refs) - 9 - 2 * count :]
    o_all, outs = refs[0], refs[1 : 1 + 2 * count]
    x_buf, d_buf, out_buf, dx_buf, keep_buf, x_sem, d_sem, o_sem = refs[1 + 2 * count :]
    rows = x_buf.shape[0] // count
    x_copies = piece_copies(xs, slots, x_buf, x_sem)
    d_copies = piece_copies(ds, slots, d_buf, d_sem)
    width = w_in.shape[2]
    wg, wu, wd = w_in[0, 0], w_in[0, 1], w_down[0]
    w = to_lanes(router[...])
    half = wg.shape[1]
    stores = []
    for i in range(count):
        at = pl.ds(i * rows, rows)
        finish(x_copies[i] + d_copies[i])
        x = x_buf[at, :]
        do = d_buf[at, :width]
        mask = d_buf[at, width:].astype(F32)
        lane = iota(mask.shape, 1)
        probs = masked_softmax(dot(x, w), mask)
        gate = jnp.sum(jnp.where(lane == mine[0], probs, 0.0), axis=-1, keepdims=True)
        hg, dg, du, dgate = mlp(x, do, wg, wu, wd, gate)
        dx = dot(dg, wg, NT) + dot(du, wu, NT)
        out = dot(hg, wd)
        if with_shared and i == 0:
            out = out + shared[0][...].astype(F32)
            dx = dx + shared[1][...].astype(F32)
        dx_buf[at, :width] = dx.astype(BF16)
        chosen = jnp.sum(jnp.where(lane == mine[0], mask, 0.0), axis=-1, keepdims=True) > 0.0
        dx_buf[at, width:] = jnp.where(jnp.logical_and(lane == mine[0], chosen), dgate, 0.0).astype(BF16)
        stores += start_all([(dx_buf.at[at], outs[2 * i], o_sem.at[3 * i + 1])])
        out_buf[at, :] = out.astype(BF16)
        keep_buf[at, :half] = hg
        keep_buf[at, half : 2 * half] = dg
        keep_buf[at, 2 * half :] = du
        stores += start_all(
            [
                (
                    out_buf.at[at],
                    o_all.at[pl.ds(pl.multiple_of(index[i] * rows, rows), rows)],
                    o_sem.at[3 * i],
                ),
                (keep_buf.at[at], outs[2 * i + 1], o_sem.at[3 * i + 2]),
            ]
        )
    finish(stores)


def k_shared(x, do, w_in, w_down, o_out, o_dx):
    width = w_in.shape[1]
    wg, wu, wd = w_in[0], w_in[1], w_down[...]
    hg, dg, du, _ = mlp(x[...], do[:, :width], wg, wu, wd, None)
    o_out[...] = dot(hg, wd).astype(BF16)
    o_dx[...] = (dot(dg, wg, NT) + dot(du, wu, NT)).astype(BF16)


def store_in_cuts(buffer, at, cuts, outs, sems, first):
    return start_all(
        (buffer.at[at, pl.ds(begin, size)], out.at[at], sems.at[first + j])
        for j, (out, (begin, size)) in enumerate(zip(outs, cuts))
    )


def weight_products(x_buf, d_buf, keep_buf, in_buf, down_buf, o_in, o_down, o_sem):
    half = down_buf.shape[0]
    width = in_buf.shape[0]
    step = 256
    stores = []
    for c in range(width // step):
        to = pl.ds(c * step, step)
        in_buf[to, :] = dot(x_buf[:, to], keep_buf[:, half:], TN)
        stores += store_in_cuts(in_buf, to, [(0, half), (half, half)], [o_in.at[0], o_in.at[1]], o_sem, 3 * c)
        down_buf[:, to] = dot(keep_buf[:, :half], d_buf[:, to], TN)
        stores += start_all([(down_buf.at[:, to], o_down.at[:, to], o_sem.at[3 * c + 2])])
    finish(stores)


def k_expert_weights(slots, index, *refs):
    pieces, count = sum(slots), len(slots)
    xs, ds, ks = refs[:pieces], refs[pieces : 2 * pieces], refs[2 * pieces : 2 * pieces + count]
    o_in, o_down, x_buf, d_buf, keep_buf, in_buf, down_buf, x_sem, d_sem, k_sem, o_sem = refs[2 * pieces + count :]
    rows = x_buf.shape[0] // count
    copies = piece_copies(xs, slots, x_buf, x_sem) + piece_copies(ds, slots, d_buf, d_sem)
    copies += [start_all([(ks[i], keep_buf.at[pl.ds(i * rows, rows)], k_sem.at[i])]) for i in range(count)]
    for c in copies:
        finish(c)
    weight_products(x_buf, d_buf, keep_buf, in_buf, down_buf, o_in, o_down, o_sem)


def k_shared_weights(slots, index, *refs):
    s_in, s_down = refs[:2]
    pieces, count = sum(slots), len(slots)
    xs, ds = refs[2 : 2 + pieces], refs[2 + pieces : 2 + 2 * pieces]
    o_in, o_down, x_buf, d_buf, keep_buf, in_buf, down_buf, x_sem, d_sem, o_sem = refs[2 + 2 * pieces :]
    rows = x_buf.shape[0] // count
    x_copies = piece_copies(xs, slots, x_buf, x_sem)
    d_copies = piece_copies(ds, slots, d_buf, d_sem)
    half = s_down.shape[0]
    width = s_in.shape[1]
    for i in range(count):
        at = pl.ds(i * rows, rows)
        finish(x_copies[i] + d_copies[i])
        hg, dg, du, _ = mlp(x_buf[at, :], d_buf[at, :width], s_in[0], s_in[1], s_down[...], None)
        keep_buf[at, :half] = hg
        keep_buf[at, half : 2 * half] = dg
        keep_buf[at, 2 * half :] = du
    weight_products(x_buf, d_buf, keep_buf, in_buf, down_buf, o_in, o_down, o_sem)


def k_outer(groups, cuts, index, *refs):
    counts = [sum(g) for g in groups]
    total = sum(counts)
    outs = refs[total : total + len(cuts)]
    a_buf, b_buf, o_buf, sem, o_sem = refs[total + len(cuts) :]
    copies, at, column = [], 0, 0
    for g, slots in enumerate(groups):
        pieces = refs[at : at + counts[g]]
        width = pieces[0].shape[1]
        buffer = a_buf if g == 0 else b_buf.at[:, pl.ds(column, width)]
        column += 0 if g == 0 else width
        copies += piece_copies(pieces, slots, buffer, sem.at[pl.ds(at, counts[g])])
        at += counts[g]
    for c in copies:
        finish(c)
    step = 256
    stores = []
    for c in range(a_buf.shape[1] // step):
        at = pl.ds(c * step, step)
        o_buf[at, :] = dot(a_buf[:, at], b_buf[...], TN).astype(BF16)
        stores += store_in_cuts(o_buf, at, cuts, outs, o_sem, len(cuts) * c)
    finish(stores)


def outer(a, bs, widths, rows, name):
    columns = a.pieces[0].shape[1]
    total = sum(widths)
    cuts = [(sum(widths[:i]), w) for i, w in enumerate(widths)]
    pieces = [p for g in (a, *bs) for p in g.pieces]
    dma = pltpu.SemaphoreType.DMA
    return call(
        functools.partial(k_outer, [g.slots for g in (a, *bs)], cuts),
        [Far(struct((columns, w), BF16)) for w in widths],
        [Far(p) for p in pieces],
        2 * rows * columns * total,
        name,
        index=a.index,
        scratch=[
            pltpu.VMEM((rows, columns), BF16),
            pltpu.VMEM((rows, total), BF16),
            pltpu.VMEM((columns, total), BF16),
            dma((len(pieces),)),
            dma((len(widths) * (columns // 256),)),
        ],
    )


def k_out_weights(slots, index, *refs):
    n = sum(slots)
    us, ds = refs[:n], refs[n : 2 * n]
    o, u_buf, d_buf, o_buf, u_sem, d_sem, o_sem = refs[2 * n :]
    model = o.shape[1]
    u_copies = piece_copies(us, slots, u_buf, u_sem)
    d_copies = piece_copies(ds, slots, d_buf, d_sem)
    rows = d_buf.shape[0] // len(slots)
    for i in range(len(slots)):
        finish(u_copies[i] + d_copies[i])
        at = pl.ds(i * rows, rows)
        more = d_buf[at, model:].astype(F32)
        d_buf[at, :model] = (d_buf[at, :model].astype(F32) * (more[:, 2:3] + more[:, 3:4])).astype(BF16)
    step = 256
    stores = []
    for c in range(u_buf.shape[1] // step):
        at = pl.ds(c * step, step)
        o_buf[at, :] = dot(u_buf[:, at], d_buf[:, :model], TN).astype(BF16)
        stores += start_all([(o_buf.at[at], o.at[at], o_sem.at[c])])
    finish(stores)


def out_weights(u, d, rows):
    width, model = u.pieces[0].shape[1], d.pieces[0].shape[1] - LANES
    n = len(u.pieces)
    dma = pltpu.SemaphoreType.DMA
    [out] = call(
        functools.partial(k_out_weights, u.slots),
        [Far(struct((width, model), BF16))],
        [Far(p) for p in (*u.pieces, *d.pieces)],
        2 * rows * width * model,
        "out_weights",
        index=u.index,
        scratch=[
            pltpu.VMEM((rows, width), BF16),
            pltpu.VMEM((rows, model + LANES), BF16),
            pltpu.VMEM((width, model), BF16),
            dma((n,)),
            dma((n,)),
            dma((width // 256,)),
        ],
    )
    return out


def k_pair(*refs):
    half = len(refs) // 3
    for a, b, o in zip(refs[:half], refs[half : 2 * half], refs[2 * half :]):
        o[...] = a[...].astype(F32) + b[...].astype(F32)


def both_cores(arrays, name):
    if lax.axis_size("seq") != 8:
        return [a.astype(F32) for a in arrays]
    others = [flip(a, "seq", 1) for a in arrays]
    steps = 4
    return call(
        k_pair,
        [Rows(struct(a.shape, F32), a.shape[0] // steps) for a in arrays],
        [Rows(a, a.shape[0] // steps) for a in (*arrays, *others)],
        0,
        name,
        grid=steps,
    )


def flip(array, axis, bit):
    return lax.ppermute(array, axis, [(i, i ^ bit) for i in range(lax.axis_size(axis))])


def bits_of(axis):
    return [1 << b for b in range(lax.axis_size(axis).bit_length() - 1)]


class Gathered:
    def __init__(self, pieces, slots, index):
        self.pieces, self.slots, self.index = pieces, slots, index

    def tails(self, first, half):
        out, at = [], 0
        for pieces in self.slots:
            last = self.pieces[at + pieces - 1]
            out.append(last[first - half * (pieces - 1) :])
            at += pieces
        return out

    def part(self, first, last):
        at, to = sum(self.slots[:first]), sum(self.slots[:last])
        return Gathered(self.pieces[at:to], self.slots[first:last], self.index[first:last])


XOR_ORDER = (0, 1, 2, 4, 3, 5, 6, 7)


def gather(own, half, cores=True, between=(None, None)):
    size = lax.axis_size("seq")
    place = lax.axis_index("seq")
    if size != 8:
        every = lax.all_gather(own, "seq")
        return Gathered([every[k] for k in range(size)], [1] * size, jnp.arange(size, dtype=jnp.int32))
    core, x, y = bits_of("seq")
    by_x = flip(own, "seq", x)
    by_y = flip(own, "seq", y)
    first_far = []
    if between[0] is not None and not cores:
        by_x, by_y = after((by_x, by_y), between[0])
    elif between[0] is not None:
        first_far = [flip(own, "seq", core)]
        by_x, by_y = after((by_x, by_y), between[0](own, first_far[0]))
    top = flip(by_x[:half], "seq", y)
    bottom = flip(by_y[half:], "seq", x)
    if between[1] is not None:
        first_far += [flip(by_x, "seq", core), flip(by_y, "seq", core)]
        top, bottom = after((top, bottom), between[1](by_x, by_y))
    near = [own, by_x, by_y, top, bottom]
    if not cores:
        index = jnp.stack([place ^ k for k in (0, x, y, x | y)]).astype(jnp.int32)
        return Gathered(near, [1, 1, 1, 2], index)
    far = first_far + [flip(a, "seq", core) for a in near[len(first_far) :]]
    pieces = [own, far[0], by_x, by_y, far[1], far[2], top, bottom, far[3], far[4]]
    return Gathered(pieces, [1, 1, 1, 1, 1, 1, 2, 2], xor_index())


def xor_index():
    return jnp.stack([lax.axis_index("seq") ^ k for k in XOR_ORDER]).astype(jnp.int32)


def low_sum(*terms):
    return sum(t.astype(F32) for t in terms).astype(BF16)


def k_split(x0, x1, y0, y1, d0, d1, o_x, o_y, o_x_late, o_y_late):
    half = o_x_late.shape[0]
    x = low_sum(x0[...], x1[...])
    y = low_sum(y0[...], y1[...])
    d = low_sum(d0[...], d1[...])
    o_x[:half, :] = d[:half]
    o_x[half:, :] = x[:half]
    o_y[:half, :] = d[half:]
    o_y[half:, :] = y[half:]
    o_x_late[...] = x[half:]
    o_y_late[...] = y[:half]


def k_late(x, y, ax, ay, o_x, o_y):
    half = x.shape[0]
    o_x[...] = low_sum(x[...], ay[:half, :])
    o_y[...] = low_sum(y[...], ax[:half, :])


def k_join(a, b, ax, ay, bx, by, o):
    half = bx.shape[0]
    total = a[...].astype(F32) + b[...].astype(F32)
    o[:half, :] = low_sum(total[:half], ax[half:, :], by[...])
    o[half:, :] = low_sum(total[half:], ay[half:, :], bx[...])


def scatter_first(parts, name):
    if lax.axis_size("seq") != 8:
        return [lax.psum_scatter(jnp.concatenate(parts, axis=0), "seq", scatter_dimension=0, tiled=True)]
    parts = dict(zip(XOR_ORDER, parts))
    core, x, y = bits_of("seq")
    rows, width = parts[0].shape
    r3, r5, r7, r1 = (flip(parts[k], "seq", core) for k in (3, 5, 7, 1))
    full, part = struct((rows, width), BF16), struct((rows // 2, width), BF16)
    to_x, to_y, late_x, late_y = call(
        k_split, [full, full, part, part], [parts[2], r3, parts[4], r5, parts[6], r7], 0, name + "_split"
    )
    return [parts[0], r1, flip(to_x, "seq", x), flip(to_y, "seq", y), late_x, late_y]


def scatter_second(state, name):
    if lax.axis_size("seq") != 8:
        return state
    own, r1, ax, ay, late_x, late_y = state
    _, x, y = bits_of("seq")
    part = struct(late_x.shape, BF16)
    late_x, late_y = call(k_late, [part, part], [late_x, late_y, ax, ay], 0, name + "_late")
    return [own, r1, ax, ay, flip(late_x, "seq", x), flip(late_y, "seq", y)]


def scatter_last(state, name):
    if lax.axis_size("seq") != 8:
        return state[0]
    [out] = call(k_join, [struct(state[0].shape, BF16)], state, 0, name + "_join")
    return out


def scan(send, backward, name, between=None, steps=None):
    place = lax.axis_index("seq")
    seqs, size = send.shape[0], send.shape[1] - FRONT
    bits = bits_of("seq")
    state = struct((seqs, size, LANES), F32)
    row = struct((seqs, 8, LANES), F32)
    held = []
    for bit in bits_of("seq"):
        recv = flip(send, "seq", bit)
        is_set = (place & bit) != 0
        ahead = (jnp.logical_not(is_set) if backward else is_set).astype(jnp.int32)[None]
        last = bit == bits[-1]
        if last and between is not None:
            recv = after(recv, between)
        outs = [state] if last else [state, row, struct(send.shape, BF16)]
        made = call(
            functools.partial(k_scan, not held, last),
            [Each(o) for o in outs],
            [Scalars(ahead), Each(recv), Each(send), *(Each(a) for a in held)],
            0,
            name,
            grid=seqs,
        )
        if last:
            return made[0]
        held, send = made[:2], made[2]
        if steps is not None:
            steps.append(send)
    return before


def rows_of_mp(array):
    share = array.shape[0] // lax.axis_size("mp")
    return lax.dynamic_slice_in_dim(array, lax.axis_index("mp") * share, share, 0)


def exchange_mp(array):
    return lax.all_to_all(array, "mp", 0, 0, tiled=True)


def to_shares(array):
    size = lax.axis_size("mp")
    return exchange_mp(array.reshape(size, array.shape[0] // size, array.shape[1]))


def gather_mp(array):
    return lax.all_gather(array, "mp", tiled=True)


def after(values, others):
    return lax.optimization_barrier((values, others))[0]


def all_sum(array, axes):
    for axis in axes:
        for bit in bits_of(axis):
            array = array + flip(array, axis, bit)
    return array


def passed_along(block, axis, distance):
    devices = range(lax.axis_size(axis))
    route = [(i - distance, i) for i in devices if i - distance in devices]
    return lax.ppermute(block, axis, route)


def body(
    tokens, lengths, expert_ids, norm_gains, in_z, in_x, in_bc, in_dt, conv_x, conv_bc,
    head_par, gn_gain, out_w, router, shared_in, shared_down, expert_in, expert_down, d_out,
):
    piece, seqs, model = tokens.shape
    width = in_z.shape[1]
    heads = head_par.shape[1]
    experts = router.shape[1]
    half = expert_in.shape[-1]
    n_seq, n_mp = lax.axis_size("seq"), lax.axis_size("mp")
    seq_at, mp_at = lax.axis_index("seq"), lax.axis_index("mp")
    rows = seqs * piece
    share = rows // n_mp
    bc = 2 * STATE
    beside = beside_rows(experts, model)
    dma = pltpu.SemaphoreType.DMA

    meta = jnp.concatenate([lengths, (seq_at * piece).astype(jnp.int32)[None]])
    tok = jnp.transpose(tokens, (1, 0, 2))
    edge_in = passed_along(tokens[piece - (KCONV - 1) :], "seq", 1)
    front = jnp.pad(jnp.transpose(edge_in, (1, 0, 2)), ((0, 0), (FRONT - (KCONV - 1), 0), (0, 0)))
    tok_front = jnp.concatenate([front, tok], axis=1)
    gn = gn_gain[None]
    picked = jnp.sum(
        (expert_ids[..., None] == jnp.arange(LANES, dtype=jnp.int32)).astype(F32), axis=2
    ).astype(BF16)
    small = [conv_x, conv_bc, head_par, Scalars(meta)]
    d_ext = jnp.transpose(jnp.concatenate([d_out, picked], axis=-1), (1, 0, 2)).reshape(rows, model + LANES)

    def both(*shape, dtype=F32):
        return Each(struct((seqs, *shape), dtype))

    normed, gate_z, xbc, dt_raw, send, totals = call(
        k_in,
        [
            both(piece, model, dtype=BF16),
            both(piece, width),
            both(piece + FRONT, width + bc, dtype=BF16),
            both(piece, LANES),
            both(width + FRONT, LANES, dtype=BF16),
            both(8, LANES),
        ],
        [Each(tok_front), norm_gains, in_z, in_x, in_bc, in_dt, *small],
        2 * rows * model * (2 * width + bc + LANES),
        "mixer_in",
        grid=seqs,
    )
    entering = scan(send, False, "scan")
    intra, c_mat, ecum = call(
        k_intra,
        [both(piece, width), both(piece, STATE, dtype=BF16), both(piece, width)],
        [Each(xbc), Each(dt_raw), *small],
        2 * rows * piece * width * 4,
        "mixer_intra",
        grid=seqs,
    )
    of_rows = struct((share, model), F32)
    mixed, u, part = call(
        k_out,
        [both(piece, width), both(piece, width, dtype=BF16), both(piece, model + LANES, dtype=BF16)],
        [Each(intra), Each(c_mat), Each(ecum), Each(entering), Each(gate_z), gn, out_w],
        2 * rows * width * (STATE + model),
        "mixer_out",
        grid=seqs,
    )
    tok_own = rows_of_mp(tok.reshape(rows, model))
    d_own = rows_of_mp(d_ext)
    arrived = to_shares(part.reshape(rows, model + LANES))
    residual, mixer_own, two_own, scales = call(
        k_rows_one,
        [of_rows, of_rows, struct((share, model), BF16), struct((share, LANES), F32)],
        [tok_own, norm_gains, arrived],
        0,
        "rows_one",
    )
    d_got = gather(d_ext, piece, between=(lambda *_: entering, lambda *_: two_own))
    two = gather_mp(two_own)

    mine = ((seq_at * n_mp + mp_at) // 2).astype(jnp.int32)[None]

    def expert(pieces, first, last, o_all, shared=()):
        part_d = d_got.part(first, last)
        slots, index = part_d.slots, part_d.index
        count = len(slots)
        size = rows * count
        return call(
            functools.partial(k_expert, slots, bool(shared)),
            [Far(struct((n_seq * rows, model), BF16))]
            + [Far(struct((rows, model + LANES), BF16)), Far(struct((rows, 3 * half), BF16))] * count,
            [
                Scalars(mine), router, expert_in, expert_down, *(Far(p) for p in (*pieces, *part_d.pieces)),
                *shared, *(Far(o) for o in o_all),
            ],
            2 * size * model * half * 6.5,
            "experts",
            index=index,
            aliases={5 + 2 * len(pieces): 0} if o_all else None,
            scratch=[
                pltpu.VMEM((size, model), BF16),
                pltpu.VMEM((size, model + LANES), BF16),
                pltpu.VMEM((size, model), BF16),
                pltpu.VMEM((size, model + LANES), BF16),
                pltpu.VMEM((size, 3 * half), BF16),
                dma((len(pieces),)),
                dma((len(pieces),)),
                dma((3 * count,)),
            ],
        )

    def shared_of(x):
        return call(
            k_shared,
            [struct((rows, model), BF16), struct((rows, model), BF16)],
            [x, d_ext, shared_in, shared_down],
            2 * rows * model * half * 6,
            "shared",
        )

    made = []

    def near_experts(own, far):
        made.append(expert([own, far], 0, 2, [], shared_of(own)))
        return made

    def chip_experts(by_x, by_y):
        made.append(expert([by_x, by_y], 2, 4, made[-1][:1]))
        return made[-1]

    if n_seq == 8:
        two, d_got.pieces = lax.optimization_barrier((two, d_got.pieces))
        x_got = gather(two, piece, between=(near_experts, chip_experts))
        made.append(expert(x_got.pieces[4:], 4, 8, made[-1][:1]))
    else:
        x_got = gather(two, piece)
        out_shared, dx_shared = shared_of(two)
        for i in range(0, n_seq, 4):
            made.append(expert(x_got.part(i, i + 4).pieces, i, i + 4, made[-1][:1] if made else []))
    out_all = made[-1][0]
    e_dx = [a for m in made for a in m[1::2]]
    e_keep = [a for m in made for a in m[2::2]]

    g_expert_in = g_expert_down = g_shared_in = g_shared_down = 0.0
    weight_outs = [Far(struct((2, model, half), F32)), Far(struct((half, model), F32))]

    def weight_scratch(keeps, pieces):
        return [
            pltpu.VMEM((8 * rows, model), BF16),
            pltpu.VMEM((8 * rows, model + LANES), BF16),
            pltpu.VMEM((8 * rows, 3 * half), BF16),
            pltpu.VMEM((model, 2 * half), F32),
            pltpu.VMEM((half, model), F32),
            dma((pieces,)),
            dma((pieces,)),
            *([dma((8,))] if keeps else []),
            dma((3 * (model // 256),)),
        ]

    def shared_weights(first, others):
        x = x_got.part(first, first + 8)
        return call(
            functools.partial(k_shared_weights, x.slots),
            weight_outs,
            [shared_in, shared_down, *(Far(a) for a in (*after(x.pieces, others), *d_got.part(first, first + 8).pieces))],
            6 * 2 * 8 * rows * model * half,
            "shared_weights",
            index=x.index,
            scratch=weight_scratch(False, len(x.pieces)),
        )

    def expert_weights(first, others):
        x = x_got.part(first, first + 8)
        return call(
            functools.partial(k_expert_weights, x.slots),
            weight_outs,
            [Far(a) for a in (*after(x.pieces, others), *d_got.part(first, first + 8).pieces, *e_keep[first : first + 8])],
            3 * 2 * 8 * rows * model * half,
            "expert_weights",
            index=x.index,
            scratch=weight_scratch(True, len(x.pieces)),
        )

    state = scatter_first(e_dx, "dx")
    if n_seq == 8:
        g_shared_in, g_shared_down = shared_weights(0, e_dx)
        state, g_shared_in, g_shared_down = lax.optimization_barrier((state, g_shared_in, g_shared_down))
        state = scatter_second(state, "dx")
        g_expert_in, g_expert_down = expert_weights(0, g_shared_down)
        state, g_expert_in, g_expert_down = lax.optimization_barrier((state, g_expert_in, g_expert_down))
    else:
        for first in range(0, n_seq, 8):
            a, b = shared_weights(first, e_dx)
            c, d = expert_weights(first, e_dx)
            g_shared_in, g_shared_down = g_shared_in + a, g_shared_down + b
            g_expert_in, g_expert_down = g_expert_in + c, g_expert_down + d
    dx_sum = scatter_last(state, "dx")
    if n_seq != 8:
        dx_sum = jnp.concatenate([low_sum(dx_sum[:, :model], dx_shared), dx_sum[:, model:]], axis=1)
    arrived = to_shares(dx_sum)
    out_sum = lax.psum_scatter(after(out_all, dx_sum), "seq", scatter_dimension=0, tiled=True)
    if n_seq != 8:
        out_sum = low_sum(out_sum, out_shared)
    dm_own, d_residual, g_two = call(
        k_rows_two,
        [struct((share, model + LANES), BF16), of_rows, struct((experts + 8, model), F32)],
        [d_own, two_own, residual, mixer_own, scales, norm_gains, router, arrived],
        0,
        "rows_two",
    )
    dm = gather_mp(dm_own)
    if n_seq == 8:
        n_got = gather(after(normed, part).reshape(rows, model), piece, False, (dx_sum, None))
    else:
        normed, u = after((normed, u), (dm, g_expert_in, g_shared_in))
        n_got = gather(normed.reshape(rows, model), piece, False)
    u_got = gather(after(u, dx_sum).reshape(rows, width), piece, False)
    if n_seq == 8:
        dm, u_got.pieces = lax.optimization_barrier((dm, u_got.pieces))

    dz, dy, send, g_gn = call(
        k_back_gate,
        [
            both(piece, width, dtype=BF16),
            both(piece, width),
            both(width + FRONT, LANES, dtype=BF16),
            both(8, width),
        ],
        [Rows(dm, piece), Each(mixed), Each(gate_z), gn, out_w, Each(c_mat), Each(ecum), Each(totals)],
        2 * rows * width * (model + STATE),
        "back_gate",
        grid=seqs,
    )
    intra_back = call(
        k_back_intra,
        [both(piece, width), both(piece, STATE), both(piece, STATE), both(piece, LANES), both(piece, model)],
        [Each(xbc), Each(dt_raw), *small, Each(dy), Each(dz), in_z],
        2 * rows * width * (model + 4 * piece),
        "back_intra",
        grid=seqs,
    )
    dxw0, db0, dc0, dcum0, dn0 = intra_back
    steps = []
    leaving = scan(send, True, "scan_back", intra_back, steps)
    dz_got = gather(after(dz, leaving).reshape(rows, width), piece, False)
    dm_got = gather(after(dm, leaving), piece, False)
    out_arrived = to_shares(after(out_sum, steps[0]))
    [out_own] = call(k_rows_out, [struct((n_mp, share, model), BF16)], [residual, out_arrived], 0, "rows_out")
    out_rows = exchange_mp(out_own)

    def in_order(rows):
        return jnp.transpose(rows.reshape(seqs, piece, model), (1, 0, 2)).astype(F32)

    d_xbc, d_dt, g_conv, g_hp = call(
        k_back_state,
        [
            both(piece + FRONT, width + bc),
            both(piece, LANES, dtype=BF16),
            both(8, width + bc),
            both(8, LANES),
        ],
        [
            Each(xbc), Each(dt_raw), *small, Each(dy), Each(dxw0), Each(db0), Each(dc0), Each(dcum0),
            Each(entering), Each(leaving),
        ],
        2 * rows * width * STATE * 20,
        "back_state",
        grid=seqs,
    )
    edge = passed_along(d_xbc[:, :FRONT], "seq", -1)
    if n_seq == 8:
        edge, dz_got.pieces[1:3], out_rows = lax.optimization_barrier((edge, dz_got.pieces[1:3], out_rows))
    output = in_order(out_rows)
    dx, d_bc, part = call(
        k_back_in,
        [
            struct((rows + SMALL, width + LANES), BF16),
            struct((rows + beside, bc), BF16),
            both(piece, model, dtype=BF16),
        ],
        [
            Each(dn0), Each(d_xbc), Each(edge), Each(d_dt), Each(tok_front), g_conv, g_hp, g_gn, g_two,
            in_x, in_bc, in_dt,
        ],
        2 * rows * (width + bc + LANES) * model,
        "back_in",
        grid=seqs,
        scratch=[pltpu.VMEM((8, model), F32)],
    )
    arrived = to_shares(part.reshape(rows, model))
    *head_bits, last_bit = bits_of("mp")
    for bit in head_bits:
        d_bc = low_sum(d_bc, flip(d_bc, "mp", bit))
    d_bc = low_sum(d_bc, flip(d_bc, "mp", last_bit))
    bc_got = gather(d_bc, piece, False)
    dx_got = gather(dx, piece, False)

    g_in_z = g_in_x = g_dt = g_in_bc = g_out_w = 0.0
    size = min(8, len(n_got.slots))
    for first in range(0, len(n_got.slots), size):
        last = first + size
        [a] = outer(n_got.part(first, last), [dz_got.part(first, last)], [width], size * rows, "weights_z")
        g_in_z = g_in_z + a
        g_out_w = g_out_w + out_weights(u_got.part(first, last), dm_got.part(first, last), size * rows)
    if n_seq == 8:
        arrived, g_in_z, g_out_w, d_bc, dx_got.pieces[1:3] = lax.optimization_barrier(
            (arrived, g_in_z, g_out_w, d_bc, dx_got.pieces[1:3])
        )
    [rows_own] = call(
        k_rows_three,
        [struct((n_mp, share, model), BF16)],
        [tok_own, d_residual, norm_gains, arrived],
        0,
        "rows_three",
    )
    rows_all = exchange_mp(rows_own)
    [g_in_z] = both_cores([g_in_z], "cores_z")
    [g_out_w] = both_cores([g_out_w], "cores_out")
    for first in range(0, len(n_got.slots), size):
        last = first + size
        a, b, c = outer(
            n_got.part(first, last), [dx_got.part(first, last), bc_got.part(first, last)], [width, LANES, bc],
            size * rows, "weights_x",
        )
        g_in_x, g_dt, g_in_bc = g_in_x + a, g_dt + b, g_in_bc + c
    if n_seq == 8:
        rows_all, g_in_x, g_dt, g_in_bc, g_in_z, g_out_w = lax.optimization_barrier(
            (rows_all, g_in_x, g_dt, g_in_bc, g_in_z, g_out_w)
        )

    d_tokens = in_order(rows_all)
    small = sum(t.astype(F32) for t in dx_got.tails(rows, piece))
    summed = sum(t.astype(F32) for t in bc_got.tails(rows, piece))
    if n_seq == 8:
        small = small + flip(small, "seq", 1)
        summed = summed + flip(summed, "seq", 1)
    g_in_x, g_dt, g_in_bc = both_cores([g_in_x, g_dt, g_in_bc], "cores_x")
    cuts = model // bc
    g_router = summed[: cuts * experts].reshape(cuts, experts, bc)
    first = cuts * experts
    return (
        output,
        d_tokens,
        summed[first : first + 2 * cuts].reshape(2, model),
        g_in_z,
        g_in_x,
        g_in_bc,
        g_dt[:, :heads],
        small[: KCONV + 1, :width],
        summed[first + 2 * cuts : first + 2 * cuts + KCONV + 1],
        small[:3, width : width + heads],
        small[KCONV + 1, :width],
        g_out_w,
        jnp.transpose(g_router, (0, 2, 1)).reshape(model, experts),
        g_shared_in,
        g_shared_down,
        g_expert_in[None],
        g_expert_down[None],
    )


def solution(mesh):
    in_specs = (
        P("seq", None, None),
        P(),
        P("seq", None, None),
        P(),
        P(None, "mp"),
        P(None, "mp"),
        P(),
        P(None, "mp"),
        P(None, "mp"),
        P(),
        P(None, "mp"),
        P("mp"),
        P("mp", None),
        P(),
        P(None, None, "mp"),
        P("mp", None),
        P(("seq", "mp"), None, None, None),
        P(("seq", "mp"), None, None),
        P("seq", None, None),
    )
    out_specs = (
        P("seq", None, None),
        P("seq", None, None),
        P(),
        P(None, "mp"),
        P(None, "mp"),
        P(),
        P(None, "mp"),
        P(None, "mp"),
        P(),
        P(None, "mp"),
        P("mp"),
        P("mp", None),
        P(),
        P(None, None, "mp"),
        P("mp", None),
        P(("seq", "mp"), None, None, None),
        P(("seq", "mp"), None, None),
    )
    return jax.shard_map(body, mesh=mesh, in_specs=in_specs, out_specs=out_specs, check_vma=False)
```

```python
import functools

import jax
import jax.numpy as jnp
from jax import lax
from jax.experimental import pallas as pl
from jax.experimental.pallas import tpu as pltpu
from jax.sharding import PartitionSpec as P

HEAD_DIM = 64
STATE = 128
KCONV = 4
INNER = 3072
LANES = 128
SMALL = 16
FRONT = 16
EPSILON = 1e-05
F32 = jnp.float32
BF16 = jnp.bfloat16
HIGHEST = lax.Precision.HIGHEST
NN = (((1,), (0,)), ((), ()))
NT = (((1,), (1,)), ((), ()))
TN = (((0,), (0,)), ((), ()))


class Each:
    def __init__(self, array):
        self.array = array


class Scalars:
    def __init__(self, array):
        self.array = array


class Far:
    def __init__(self, array):
        self.array = array


class Rows:
    def __init__(self, array, rows):
        self.array, self.rows = array, rows


def struct(shape, dtype):
    return jax.ShapeDtypeStruct(tuple(shape), dtype)


def call(kernel, outs, args, flops, name, grid=1, index=None, scratch=(), aliases=None):
    def spec(a):
        if isinstance(a, Scalars):
            return pl.BlockSpec(memory_space=pltpu.SMEM)
        if isinstance(a, Far):
            return pl.BlockSpec(memory_space=pl.ANY)
        if isinstance(a, Rows):
            rest = a.array.shape[1:]
            return pl.BlockSpec((a.rows, *rest), lambda s, *_: (s,) + (0,) * len(rest))
        if isinstance(a, Each):
            rest = a.array.shape[1:]
            return pl.BlockSpec((None, *rest), lambda s, *_: (s,) + (0,) * len(rest))
        return pl.BlockSpec(a.shape, lambda s, *_: (0,) * len(a.shape))

    def plain(a):
        return a.array if isinstance(a, (Each, Scalars, Far, Rows)) else a

    arrays = [plain(a) for a in args]
    shapes = [plain(a) for a in outs]
    moved = sum(a.size * a.dtype.itemsize for a in (*arrays, *shapes))
    grid_spec = pltpu.PrefetchScalarGridSpec(
        num_scalar_prefetch=0 if index is None else 1,
        grid=(grid,),
        in_specs=[spec(a) for a in args],
        out_specs=[spec(a) for a in outs],
        scratch_shapes=list(scratch),
    )
    return pl.pallas_call(
        kernel,
        out_shape=shapes,
        grid_spec=grid_spec,
        input_output_aliases=aliases or {},
        compiler_params=pltpu.CompilerParams(vmem_limit_bytes=60 * 2**20),
        cost_estimate=pl.CostEstimate(flops=int(flops), bytes_accessed=int(moved), transcendentals=0),
        name=name,
    )(*([] if index is None else [index]), *arrays)


def dot(a, b, dims=NN):
    return lax.dot_general(a.astype(BF16), b.astype(BF16), dims, preferred_element_type=F32)


def exact(a, b, dims=NN):
    return lax.dot_general(a, b, dims, precision=HIGHEST, preferred_element_type=F32)


def fine(a, b, dims=NN):
    high, low = two_terms(a)
    return dot(high, b, dims) + dot(low, b, dims)


def sigmoid(v):
    return 1.0 / (1.0 + jnp.exp(-v))


def iota(shape, axis):
    return lax.broadcasted_iota(jnp.int32, shape, axis)


def two_terms(v):
    high = v.astype(BF16)
    return high, (v - high.astype(F32)).astype(BF16)


def to_lanes(v):
    return jnp.concatenate([v, jnp.zeros((v.shape[0], LANES - v.shape[1]), v.dtype)], axis=1)


def to_rows(v):
    return jnp.concatenate([v, jnp.zeros((LANES - v.shape[0], v.shape[1]), v.dtype)], axis=0)


def spread_matrix(width):
    return (iota((LANES, width), 1) // HEAD_DIM == iota((LANES, width), 0)).astype(BF16)


def prepared(xbc, dt, conv_x, conv_bc, head_par, meta):
    rows = dt.shape[0]
    width = conv_x.shape[1]
    conv = jnp.concatenate([conv_x[...], conv_bc[...]], axis=1)
    hp = to_lanes(head_par[...])
    where = iota((rows, 1), 0) + meta[2]
    live = (where < meta[pl.program_id(0)]).astype(F32)
    xf = xbc[...].astype(F32)
    summed = conv[KCONV : KCONV + 1]
    taps = []
    for j in range(KCONV):
        shifted = xf[FRONT - (KCONV - 1) + j : FRONT - (KCONV - 1) + j + rows]
        taps.append(shifted)
        summed = summed + conv[j : j + 1] * shifted
    sig = sigmoid(summed)
    act = summed * sig
    xs = act[:, :width] * live
    b = act[:, width : width + STATE]
    c = act[:, width + STATE :]
    raw = dt[...] + hp[0:1]
    step = (jnp.maximum(raw, 0.0) + jnp.log1p(jnp.exp(-jnp.abs(raw)))) * live
    rate = -jnp.exp(hp[1:2])
    logd = rate * step
    lower = (iota((rows, rows), 0) >= iota((rows, rows), 1)).astype(F32)
    cum = exact(lower, logd)
    return dict(
        conv=conv, skip=hp[2:3], live=live, taps=taps, summed=summed, sig=sig, xs=xs, b=b, c=c, raw=raw,
        step=step, rate=rate, logd=logd, cum=cum,
    )


def pack_state(o_send, state, decay):
    size = state.shape[0]
    high, low = two_terms(decay)
    row = iota((FRONT, LANES), 0)
    more = jnp.where(row == 0, high.astype(F32), 0.0) + jnp.where(row == 1, low.astype(F32), 0.0)
    o_send[:size, :] = state.astype(BF16)
    o_send[size:, :] = more.astype(BF16)


def unpack_state(send):
    size = send.shape[0] - FRONT
    more = send[size:, :].astype(F32)
    return send[:size, :].astype(F32), more[0:1] + more[1:2]


def k_in(tok, gains, wz, wx, wbc, wdt, conv_x, conv_bc, head_par, meta, o_norm, o_z, o_xbc, o_dt, o_send, o_tot):
    width = wz.shape[1]
    x = tok[...].astype(F32)
    scale = lax.rsqrt(jnp.mean(x * x, axis=-1, keepdims=True) + EPSILON)
    normed = (x * scale * gains[0:1]).astype(BF16)
    own = normed[FRONT:]
    o_norm[...] = own
    o_xbc[:, :width] = dot(normed, wx[...]).astype(BF16)
    o_xbc[:, width:] = dot(normed, wbc[...]).astype(BF16)
    o_dt[...] = to_lanes(dot(own, wdt[...], NT))
    o_z[...] = dot(own, wz[...])
    p = prepared(o_xbc, o_dt, conv_x, conv_bc, head_par, meta)
    rows = own.shape[0]
    last = p["cum"][rows - 1 : rows]
    weight = fine(p["step"] * jnp.exp(last - p["cum"]), spread_matrix(width))
    decay = jnp.exp(last)
    pack_state(o_send, dot(p["xs"] * weight, p["b"], TN), decay)
    o_tot[...] = jnp.broadcast_to(decay, o_tot.shape)


def pair_masks(rows):
    low = iota((rows, LANES), 1) < HEAD_DIM
    return low, jnp.logical_not(low)


def decays(cum, cum_t, h, ahead):
    gap = cum[:, h : h + 1] - cum_t[h : h + 1, :]
    return jnp.where(ahead, jnp.exp(jnp.where(ahead, gap, 0.0)), 0.0)


def by_halves(v, low, high):
    return jnp.concatenate(
        [jnp.where(low, v, 0.0).astype(BF16), jnp.where(high, v, 0.0).astype(BF16)], axis=0
    )


def k_intra(xbc, dt, conv_x, conv_bc, head_par, meta, o_y, o_c, o_ecum):
    width = o_y.shape[1]
    p = prepared(xbc, dt, conv_x, conv_bc, head_par, meta)
    xs, cum = p["xs"], p["cum"]
    rows = cum.shape[0]
    spread = spread_matrix(width)
    ahead = iota((rows, rows), 0) >= iota((rows, rows), 1)
    cum_t = cum.T
    scores = dot(p["c"], p["b"], NT)
    spread_out = fine(
        jnp.concatenate([p["step"], jnp.exp(cum), jnp.broadcast_to(p["skip"], (8, LANES))], axis=0), spread
    )
    xw = xs * spread_out[:rows]
    skip = spread_out[2 * rows : 2 * rows + 1]
    low, high = pair_masks(rows)
    o_c[...] = p["c"].astype(BF16)
    o_ecum[...] = spread_out[rows : 2 * rows]
    for pair in range(width // LANES):
        cols = slice(pair * LANES, (pair + 1) * LANES)
        mats = [(decays(cum, cum_t, h, ahead) * scores).astype(BF16) for h in (2 * pair, 2 * pair + 1)]
        within = dot(jnp.concatenate(mats, axis=1), by_halves(xw[:, cols], low, high))
        o_y[:, cols] = within + skip[:, cols] * xs[:, cols]


def k_scan(first, last, after, recv, own, *refs):
    whole, total = unpack_state(own)
    state, decay = unpack_state(recv)
    size = state.shape[0]
    mine = iota((size, LANES), 1) == iota((size, LANES), 0) // HEAD_DIM

    def rows_of(d):
        return jnp.sum(jnp.where(mine, d, 0.0), axis=1, keepdims=True)

    is_after = after[0] == 1
    if first:
        outs = refs
        outs[0][...] = jnp.where(is_after, state, 0.0)
        new_reach = jnp.where(is_after, decay, 1.0)
    else:
        before, reach = refs[:2]
        outs = refs[2:]
        outs[0][...] = jnp.where(is_after, before[...] + rows_of(reach[0:1]) * state, before[...])
        new_reach = jnp.where(is_after, reach[0:1] * decay, reach[0:1])
    if last:
        return
    outs[1][...] = jnp.broadcast_to(new_reach, outs[1].shape)
    new_whole = jnp.where(is_after, whole + rows_of(total) * state, state + rows_of(decay) * whole)
    pack_state(outs[2], new_whole, total * decay)


def k_out(y0, c, ecum, entering, z, gain, w, o_y, o_u, o_part):
    model = w.shape[1]
    y = y0[...] + ecum[...] * dot(c[...], entering[...], NT)
    o_y[...] = y
    zv = z[...]
    gated = y * zv * sigmoid(zv)
    high, low = two_terms(jnp.sum(gated * gated, axis=-1, keepdims=True))
    o_u[...] = (gated * gain[...]).astype(BF16)
    o_part[:, :model] = dot(o_u[...], w[...]).astype(BF16)
    o_part[:, model:] = to_lanes(jnp.concatenate([high, low], axis=1))


def k_back_gate(dm, y, z, gain, w, c, ecum, total, o_dz, o_dy, o_send, o_gain):
    model = w.shape[1]
    more = dm[:, model:].astype(F32)
    stat = more[:, 0:1] + more[:, 1:2]
    scale = more[:, 2:3] + more[:, 3:4]
    dn = dot(dm[:, :model], w[...], NT)
    zv = z[...]
    sig = sigmoid(zv)
    silu = zv * sig
    yv = y[...]
    gated = yv * silu
    dgated = scale * gain[...] * dn - gated * (scale * scale * stat / INNER)
    o_dz[...] = (dgated * yv * sig * (1.0 + zv * (1.0 - sig))).astype(BF16)
    dy = dgated * silu
    o_dy[...] = dy
    o_gain[...] = jnp.broadcast_to(jnp.sum(dn * gated * scale, axis=0, keepdims=True), o_gain.shape)
    pack_state(o_send, dot(ecum[...] * dy, c[...], TN), total[0:1])


def k_back_intra(xbc, dt, conv_x, conv_bc, head_par, meta, dy, dz, wz, o_dxw, o_db, o_dc, o_dcum, o_dn):
    width = dy.shape[1]
    p = prepared(xbc, dt, conv_x, conv_bc, head_par, meta)
    cum = p["cum"]
    rows = cum.shape[0]
    o_dn[...] = dot(dz[...], wz[...], NT)
    ahead = iota((rows, rows), 0) >= iota((rows, rows), 1)
    cum_t = cum.T
    scores = dot(p["c"], p["b"], NT)
    xw = p["xs"] * fine(p["step"], spread_matrix(width))
    low, high = pair_masks(rows)
    lane = iota((rows, LANES), 1)
    sub = iota((LANES, rows), 0)
    dscores = jnp.zeros((rows, rows), F32)
    plus = jnp.zeros((rows, LANES), F32)
    minus = jnp.zeros((LANES, rows), F32)
    for pair in range(width // LANES):
        cols = slice(pair * LANES, (pair + 1) * LANES)
        dstack = by_halves(dy[:, cols], low, high)
        dmats = dot(dstack, xw[:, cols], NT)
        mats = []
        for i, h in enumerate((2 * pair, 2 * pair + 1)):
            decay = decays(cum, cum_t, h, ahead)
            mat = decay * scores
            dmat = dmats[i * rows : (i + 1) * rows]
            dscores = dscores + dmat * decay
            flow = dmat * mat
            plus = jnp.where(lane == h, jnp.sum(flow, axis=1, keepdims=True), plus)
            minus = jnp.where(sub == h, jnp.sum(flow, axis=0, keepdims=True), minus)
            mats.append(mat.astype(BF16))
        o_dxw[:, cols] = dot(jnp.concatenate(mats, axis=0), dstack, TN)
    o_dcum[...] = plus - minus.T
    o_dc[...] = dot(dscores, p["b"])
    o_db[...] = dot(dscores, p["c"], TN)


def k_back_state(
    xbc, dt, conv_x, conv_bc, head_par, meta, dy, dxw0, db0, dc0, dcum0, entering, leaving,
    o_dxbc, o_ddt, o_conv, o_hp,
):
    width = dy.shape[1]
    p = prepared(xbc, dt, conv_x, conv_bc, head_par, meta)
    xs, b, c, cum, step, rate, live = (p[k] for k in ("xs", "b", "c", "cum", "step", "rate", "live"))
    summed, sig, conv = p["summed"], p["sig"], p["conv"]
    rows = cum.shape[0]
    spread = spread_matrix(width)
    last = cum[rows - 1 : rows]
    spread_out = fine(
        jnp.concatenate(
            [step, jnp.exp(cum), jnp.exp(last - cum), jnp.broadcast_to(p["skip"], (8, LANES))], axis=0
        ),
        spread,
    )
    step_x, ecum_x, rem_x = (spread_out[i * rows : (i + 1) * rows] for i in range(3))
    skip_x = spread_out[3 * rows : 3 * rows + 1]
    dyv = dy[...]
    h0 = entering[...]
    h1 = leaving[...]
    xw = xs * step_x
    scaled_dy = ecum_x * dyv
    dc = dc0[...] + dot(scaled_dy, h0)
    from_state = scaled_dy * dot(c, h0, NT)
    to_state = rem_x * dot(b, h1, NT)
    dxw = dxw0[...] + to_state
    db = db0[...] + dot(xw * rem_x, h1)
    high, low = two_terms(h1 * h0)
    dtotal = jnp.sum(dot(spread, high) + dot(spread, low), axis=1, keepdims=True)
    sums = fine(jnp.concatenate([from_state, xw * to_state, dxw * xs, dyv * xs], axis=0), spread, NT)
    flow = sums[rows : 2 * rows]
    dlast = jnp.broadcast_to(dtotal, (LANES, LANES)).T[0:1] * jnp.exp(last) + jnp.sum(
        flow, axis=0, keepdims=True
    )
    dcum = dcum0[...] + sums[:rows] - flow
    dcum = dcum + jnp.where(iota((rows, LANES), 0) == rows - 1, dlast, 0.0)
    upper = (iota((rows, rows), 0) <= iota((rows, rows), 1)).astype(F32)
    dlogd = exact(upper, dcum)
    draw = (sums[2 * rows : 3 * rows] + dlogd * rate) * live * sigmoid(p["raw"])
    o_ddt[...] = draw.astype(BF16)
    row = iota((8, LANES), 0)
    o_hp[...] = (
        jnp.where(row == 0, jnp.sum(draw, axis=0, keepdims=True), 0.0)
        + jnp.where(row == 1, jnp.sum(dlogd * p["logd"], axis=0, keepdims=True), 0.0)
        + jnp.where(row == 2, jnp.sum(sums[3 * rows : 4 * rows], axis=0, keepdims=True), 0.0)
    )
    dx = (dxw * step_x + skip_x * dyv) * live
    dsummed = jnp.concatenate([dx, db, dc], axis=1) * sig * (1.0 + summed * (1.0 - sig))
    zeros = jnp.zeros((FRONT, dsummed.shape[1]), F32)
    padded = jnp.concatenate([zeros, dsummed, zeros], axis=0)
    total = rows + FRONT
    out = jnp.zeros((total, dsummed.shape[1]), F32)
    for j in range(KCONV):
        shift = KCONV - 1 - j
        out = out + conv[j : j + 1] * padded[shift : shift + total]
        o_conv[j : j + 1] = jnp.sum(dsummed * p["taps"][j], axis=0, keepdims=True)
    o_conv[KCONV : KCONV + 1] = jnp.sum(dsummed, axis=0, keepdims=True)
    o_conv[KCONV + 1 :] = jnp.zeros((o_conv.shape[0] - KCONV - 1, dsummed.shape[1]), F32)
    o_dxbc[...] = out


def beside_rows(experts, model):
    need = (experts + 2) * model // (2 * STATE) + KCONV + 1
    return -(-need // 64) * 64


def k_back_in(dn0, dxbc, edge, ddt, tok, g_conv, g_hp, g_gn, g_two, wx, wbc, wdt, o_dx, o_bc, o_part, gain):
    width = wx.shape[1]
    rows, model = dn0.shape
    experts = g_two.shape[0] - 8
    step = pl.program_id(0)
    tail = jnp.concatenate([jnp.zeros((rows - FRONT, edge.shape[1]), F32), edge[...]], axis=0)
    own = (dxbc[FRONT:, :] + tail).astype(BF16)
    dx, dbc = own[:, :width], own[:, width:]
    to = pl.ds(pl.multiple_of(step * rows, rows), rows)
    o_dx[to, :width] = dx
    o_dx[to, width:] = ddt[...]
    o_bc[to, :] = dbc
    dn = dn0[...] + dot(dx, wx[...], NT) + dot(dbc, wbc[...], NT) + dot(ddt[...], to_rows(wdt[...]))
    o_part[...] = dn.astype(BF16)
    x = tok[FRONT:, :].astype(F32)
    scale = lax.rsqrt(jnp.mean(x * x, axis=-1, keepdims=True) + EPSILON)
    now = jnp.sum(dn * x * scale, axis=0, keepdims=True)

    @pl.when(step == 0)
    def _():
        gain[0:1, :] = now

    @pl.when(step > 0)
    def _():
        gain[0:1, :] += now

    @pl.when(step == pl.num_programs(0) - 1)
    def _():
        conv = jnp.sum(g_conv[...], axis=0)
        left = jnp.concatenate(
            [
                conv[: KCONV + 1, :width],
                jnp.sum(g_gn[...], axis=0)[0:1],
                jnp.zeros((SMALL - KCONV - 2, width), F32),
            ],
            axis=0,
        )
        right = jnp.concatenate([jnp.sum(g_hp[...], axis=0), jnp.zeros((SMALL - 8, LANES), F32)], axis=0)
        below = rows * pl.num_programs(0)
        more = pl.ds(pl.multiple_of(below, rows), SMALL)
        o_dx[more, :width] = left.astype(BF16)
        o_dx[more, width:] = right.astype(BF16)
        bc = dbc.shape[1]
        cuts = [slice(j * bc, (j + 1) * bc) for j in range(model // bc)]
        kept = [g_two[:experts, c] for c in cuts]
        kept += [gain[0:1, c] for c in cuts] + [g_two[experts : experts + 1, c] for c in cuts]
        kept.append(conv[: KCONV + 1, width:])
        size = beside_rows(experts, model)
        kept.append(jnp.zeros((size - sum(k.shape[0] for k in kept), bc), F32))
        o_bc[pl.ds(pl.multiple_of(below, rows), size), :] = jnp.concatenate(kept, axis=0).astype(BF16)


def total_of(arrived):
    return sum(arrived[k].astype(F32) for k in range(arrived.shape[0]))


def k_rows_one(tok, gains, arrived, o_residual, o_mixer, o_two, o_scales):
    model = tok.shape[1]
    total = total_of(arrived)
    scale = lax.rsqrt((total[:, model : model + 1] + total[:, model + 1 : model + 2]) / INNER + EPSILON)
    mixer = total[:, :model] * scale
    residual = tok[...].astype(F32) + mixer
    scale_two = lax.rsqrt(jnp.mean(residual * residual, axis=-1, keepdims=True) + EPSILON)
    o_residual[...] = residual
    o_mixer[...] = mixer
    o_two[...] = (residual * scale_two * gains[1:2]).astype(BF16)
    o_scales[...] = to_lanes(jnp.concatenate([scale, scale_two], axis=1))


def k_rows_two(dout, two, residual, mixer, scales, gains, router, arrived, o_dm, o_dr, o_small):
    model = two.shape[1]
    experts = router.shape[0]
    both = total_of(arrived)
    dn2, dgate = both[:, :model], both[:, model:]
    w = to_rows(router[...])
    probs = masked_softmax(dot(two[...], w, NT), dout[:, model:].astype(F32))
    dlog = (probs * (dgate - jnp.sum(probs * dgate, axis=-1, keepdims=True))).astype(BF16)
    dn2 = dn2 + dot(dlog, w)
    scale, scale_two = scales[:, 0:1], scales[:, 1:2]
    scaled = residual[...] * scale_two
    o_small[:experts, :] = dot(dlog, two[...], TN)[:experts]
    o_small[experts:, :] = jnp.broadcast_to(jnp.sum(dn2 * scaled, axis=0, keepdims=True), (8, model))
    gg = dn2 * gains[1:2]
    dr = dout[:, :model].astype(F32) + scale_two * (
        gg - scaled * jnp.mean(gg * scaled, axis=-1, keepdims=True)
    )
    o_dr[...] = dr
    dm = dr.astype(BF16)
    stat = jnp.sum(dm.astype(F32) * mixer[...], axis=-1, keepdims=True)
    o_dm[:, :model] = dm
    o_dm[:, model:] = to_lanes(jnp.concatenate([*two_terms(stat), *two_terms(scale)], axis=1))


def k_rows_out(residual, arrived, o):
    o[...] = (residual[...] + total_of(arrived)).astype(BF16)


def k_assemble(at, *refs):
    o = refs[-1]
    share = refs[0].shape[0]
    for k, r in enumerate(refs[:-1]):
        o[pl.ds(pl.multiple_of(at[k] * share, share), share), :] = r[...]


def k_rows_three(tok, dr, gains, arrived, o):
    dn1 = total_of(arrived)
    x = tok[...].astype(F32)
    scale = lax.rsqrt(jnp.mean(x * x, axis=-1, keepdims=True) + EPSILON)
    scaled = x * scale
    gg = dn1 * gains[0:1]
    dtok = (dr[...] + scale * (gg - scaled * jnp.mean(gg * scaled, axis=-1, keepdims=True))).astype(BF16)
    for k in range(o.shape[0]):
        o[k] = dtok


def masked_softmax(logits, mask):
    on = mask > 0.0
    top = jnp.max(jnp.where(on, logits, -3.0e38), axis=-1, keepdims=True)
    e = jnp.where(on, jnp.exp(jnp.where(on, logits - top, 0.0)), 0.0)
    return e / jnp.sum(e, axis=-1, keepdims=True)


def mlp(x, do, wg, wu, wd, gate):
    g = dot(x, wg)
    u = dot(x, wu)
    sig = sigmoid(g)
    silu = g * sig
    hid = (silu * u).astype(BF16)
    dh = dot(do, wd, NT)
    if gate is None:
        hg, dgate = hid, None
    else:
        hf = hid.astype(F32)
        dgate = jnp.sum(hf * dh, axis=-1, keepdims=True)
        hg = (hf * gate).astype(BF16)
        dh = dh * gate
    dg = (dh * u * sig * (1.0 + g * (1.0 - sig))).astype(BF16)
    du = (dh * silu).astype(BF16)
    return hg, dg, du, dgate


def start_all(copies):
    made = [pltpu.make_async_copy(src, dst, sem) for src, dst, sem in copies]
    for c in made:
        c.start()
    return made


def piece_copies(xs, slots, buffer, sems):
    out, at = [], 0
    rows = buffer.shape[0] // len(slots)
    for i, pieces in enumerate(slots):
        size = rows // pieces
        out.append(
            start_all(
                (xs[at + j].at[pl.ds(0, size)], buffer.at[pl.ds(i * rows + j * size, size)], sems.at[at + j])
                for j in range(pieces)
            )
        )
        at += pieces
    return out


def finish(copies):
    for c in copies:
        c.wait()


def k_expert(slots, with_shared, index, *refs):
    mine, router, w_in, w_down = refs[:4]
    slots, d_slots = slots
    pieces, d_pieces, count = sum(slots), sum(d_slots), len(slots)
    xs, ds = refs[4 : 4 + pieces], refs[4 + pieces : 4 + pieces + d_pieces]
    at = 4 + pieces + d_pieces
    shared = refs[at : at + 2] if with_shared else ()
    refs = refs[len(refs) - 9 - 2 * count :]
    o_all, outs = refs[0], refs[1 : 1 + 2 * count]
    x_buf, d_buf, out_buf, dx_buf, keep_buf, x_sem, d_sem, o_sem = refs[1 + 2 * count :]
    rows = x_buf.shape[0] // count
    x_copies = piece_copies(xs, slots, x_buf, x_sem)
    d_copies = piece_copies(ds, d_slots, d_buf, d_sem)
    width = w_in.shape[2]
    wg, wu, wd = w_in[0, 0], w_in[0, 1], w_down[0]
    w = to_rows(router[...])
    half = wg.shape[1]
    stores = []
    for i in range(count):
        at = pl.ds(i * rows, rows)
        finish(x_copies[i] + d_copies[i])
        x = x_buf[at, :]
        do = d_buf[at, :width]
        mask = d_buf[at, width:].astype(F32)
        lane = iota(mask.shape, 1)
        probs = masked_softmax(dot(x, w, NT), mask)
        gate = jnp.sum(jnp.where(lane == mine[0], probs, 0.0), axis=-1, keepdims=True)
        hg, dg, du, dgate = mlp(x, do, wg, wu, wd, gate)
        dx = dot(dg, wg, NT) + dot(du, wu, NT)
        out = dot(hg, wd)
        if with_shared and i == 0:
            out = out + shared[0][...].astype(F32)
            dx = dx + shared[1][...].astype(F32)
        dx_buf[at, :width] = dx.astype(BF16)
        chosen = jnp.sum(jnp.where(lane == mine[0], mask, 0.0), axis=-1, keepdims=True) > 0.0
        dx_buf[at, width:] = jnp.where(jnp.logical_and(lane == mine[0], chosen), dgate, 0.0).astype(BF16)
        stores += start_all([(dx_buf.at[at], outs[2 * i], o_sem.at[3 * i + 1])])
        out_buf[at, :] = out.astype(BF16)
        keep_buf[at, :half] = hg
        keep_buf[at, half : 2 * half] = dg
        keep_buf[at, 2 * half :] = du
        stores += start_all(
            [
                (
                    out_buf.at[at],
                    o_all.at[pl.ds(pl.multiple_of(index[i] * rows, rows), rows)],
                    o_sem.at[3 * i],
                ),
                (keep_buf.at[at], outs[2 * i + 1], o_sem.at[3 * i + 2]),
            ]
        )
    finish(stores)


def k_shared(x, do, w_in, w_down, o_out, o_dx):
    width = w_in.shape[1]
    wg, wu, wd = w_in[0], w_in[1], w_down[...]
    hg, dg, du, _ = mlp(x[...], do[:, :width], wg, wu, wd, None)
    o_out[...] = dot(hg, wd).astype(BF16)
    o_dx[...] = (dot(dg, wg, NT) + dot(du, wu, NT)).astype(BF16)


def store_in_cuts(buffer, at, cuts, outs, sems, first):
    return start_all(
        (buffer.at[at, pl.ds(begin, size)], out.at[at], sems.at[first + j])
        for j, (out, (begin, size)) in enumerate(zip(outs, cuts))
    )


def weight_products(x_buf, d_buf, keep_buf, in_buf, down_buf, o_in, o_down, o_sem):
    half = down_buf.shape[0]
    width = in_buf.shape[0]
    step = 256
    stores = []
    for c in range(width // step):
        to = pl.ds(c * step, step)
        in_buf[to, :] = dot(x_buf[:, to], keep_buf[:, half:], TN)
        stores += store_in_cuts(in_buf, to, [(0, half), (half, half)], [o_in.at[0], o_in.at[1]], o_sem, 3 * c)
        down_buf[:, to] = dot(keep_buf[:, :half], d_buf[:, to], TN)
        stores += start_all([(down_buf.at[:, to], o_down.at[:, to], o_sem.at[3 * c + 2])])
    finish(stores)


def k_expert_weights(slots, index, *refs):
    pieces, count = sum(slots), len(slots)
    xs, ds, ks = refs[:pieces], refs[pieces : 2 * pieces], refs[2 * pieces : 2 * pieces + count]
    o_in, o_down, x_buf, d_buf, keep_buf, in_buf, down_buf, x_sem, d_sem, k_sem, o_sem = refs[2 * pieces + count :]
    rows = x_buf.shape[0] // count
    copies = piece_copies(xs, slots, x_buf, x_sem) + piece_copies(ds, slots, d_buf, d_sem)
    copies += [start_all([(ks[i], keep_buf.at[pl.ds(i * rows, rows)], k_sem.at[i])]) for i in range(count)]
    for c in copies:
        finish(c)
    weight_products(x_buf, d_buf, keep_buf, in_buf, down_buf, o_in, o_down, o_sem)


def k_shared_weights(slots, index, *refs):
    s_in, s_down = refs[:2]
    pieces, count = sum(slots), len(slots)
    xs, ds = refs[2 : 2 + pieces], refs[2 + pieces : 2 + 2 * pieces]
    o_in, o_down, x_buf, d_buf, keep_buf, in_buf, down_buf, x_sem, d_sem, o_sem = refs[2 + 2 * pieces :]
    rows = x_buf.shape[0] // count
    x_copies = piece_copies(xs, slots, x_buf, x_sem)
    d_copies = piece_copies(ds, slots, d_buf, d_sem)
    half = s_down.shape[0]
    width = s_in.shape[1]
    for i in range(count):
        at = pl.ds(i * rows, rows)
        finish(x_copies[i] + d_copies[i])
        hg, dg, du, _ = mlp(x_buf[at, :], d_buf[at, :width], s_in[0], s_in[1], s_down[...], None)
        keep_buf[at, :half] = hg
        keep_buf[at, half : 2 * half] = dg
        keep_buf[at, 2 * half :] = du
    weight_products(x_buf, d_buf, keep_buf, in_buf, down_buf, o_in, o_down, o_sem)


def k_outer(groups, small, index, *refs):
    counts = [sum(g) for g in groups]
    total = sum(counts)
    o = refs[total]
    a_buf, b_buf, o_buf, sem, o_sem = refs[total + 1 + small : total + 6 + small]
    copies, at, column = [], 0, 0
    tails = []
    for g, slots in enumerate(groups):
        pieces = refs[at : at + counts[g]]
        width = pieces[0].shape[1]
        buffer = a_buf if g == 0 else b_buf.at[:, pl.ds(column, width)]
        column += 0 if g == 0 else width
        copies += piece_copies(pieces, slots, buffer, sem.at[pl.ds(at, counts[g])])
        at += counts[g]
        if small and g > 0:
            rows = a_buf.shape[0] // len(slots)
            first = 0
            for n in slots:
                piece = pieces[first + n - 1]
                tails.append((piece, rows // n, column - width, width))
                first += n
    if small:
        o_small, t_buf, t_sem = refs[total + 1], refs[-2], refs[-1]
        moves = []
        for k, (piece, begin, to, width) in enumerate(tails):
            size = piece.shape[0] - begin
            into = t_buf.at[k % len(groups[0]), pl.ds(0, size), pl.ds(to, width)]
            moves.append((piece.at[pl.ds(begin, size)], into, t_sem.at[k]))
        finish(start_all(moves))
        for k in (0, len(groups[0])):
            piece, begin, to, width = tails[k]
            size = piece.shape[0] - begin
            o_small[:, to : to + width] = jnp.zeros((o_small.shape[0], width), F32)
            o_small[:size, to : to + width] = sum(
                t_buf[j, :size, to : to + width].astype(F32) for j in range(len(groups[0]))
            )
    for c in copies:
        finish(c)
    step = 256
    stores = []
    for c in range(a_buf.shape[1] // step):
        at = pl.ds(c * step, step)
        o_buf[at, :] = dot(a_buf[:, at], b_buf[...], TN).astype(BF16)
        stores += start_all([(o_buf.at[at], o.at[at], o_sem.at[c])])
    finish(stores)


def outer(a, bs, rows, name, small=0):
    columns = a.pieces[0].shape[1]
    total = sum(b.pieces[0].shape[1] for b in bs)
    pieces = [p for g in (a, *bs) for p in g.pieces]
    blocks = len(a.slots)
    dma = pltpu.SemaphoreType.DMA
    more = [pltpu.VMEM((blocks, small, total), BF16), dma((blocks * len(bs),))] if small else []
    return call(
        functools.partial(k_outer, [g.slots for g in (a, *bs)], int(small > 0)),
        [Far(struct((columns, total), BF16)), *([struct((small, total), F32)] if small else [])],
        [Far(p) for p in pieces],
        2 * rows * columns * total,
        name,
        index=a.index,
        scratch=[
            pltpu.VMEM((rows, columns), BF16),
            pltpu.VMEM((rows, total), BF16),
            pltpu.VMEM((columns, total), BF16),
            dma((len(pieces),)),
            dma((columns // 256,)),
            *more,
        ],
    )


def k_out_weights(slots, d_slots, index, *refs):
    n, total = sum(slots), sum(slots) + sum(d_slots)
    us, ds = refs[:n], refs[n:total]
    o, u_buf, d_buf, o_buf, u_sem, d_sem, o_sem = refs[total:]
    model = o.shape[1]
    u_copies = piece_copies(us, slots, u_buf, u_sem)
    d_copies = piece_copies(ds, d_slots, d_buf, d_sem)
    rows = d_buf.shape[0] // len(slots)
    for i in range(len(slots)):
        finish(u_copies[i] + d_copies[i])
        at = pl.ds(i * rows, rows)
        more = d_buf[at, model:].astype(F32)
        d_buf[at, :model] = (d_buf[at, :model].astype(F32) * (more[:, 2:3] + more[:, 3:4])).astype(BF16)
    step = 256
    stores = []
    for c in range(u_buf.shape[1] // step):
        at = pl.ds(c * step, step)
        o_buf[at, :] = dot(u_buf[:, at], d_buf[:, :model], TN).astype(BF16)
        stores += start_all([(o_buf.at[at], o.at[at], o_sem.at[c])])
    finish(stores)


def out_weights(u, d, rows):
    width, model = u.pieces[0].shape[1], d.pieces[0].shape[1] - LANES
    dma = pltpu.SemaphoreType.DMA
    [out] = call(
        functools.partial(k_out_weights, u.slots, d.slots),
        [Far(struct((width, model), BF16))],
        [Far(p) for p in (*u.pieces, *d.pieces)],
        2 * rows * width * model,
        "out_weights",
        index=u.index,
        scratch=[
            pltpu.VMEM((rows, width), BF16),
            pltpu.VMEM((rows, model + LANES), BF16),
            pltpu.VMEM((width, model), BF16),
            dma((len(u.pieces),)),
            dma((len(d.pieces),)),
            dma((width // 256,)),
        ],
    )
    return out


def k_pair(widths, a, b, *refs):
    outs = refs[: len(widths)]
    a_buf, b_buf = refs[len(widths) : len(widths) + 2]
    bufs, sem, o_sem = refs[len(widths) + 2 : -2], refs[-2], refs[-1]
    steps = sem.shape[0] // 2
    rows = a_buf.shape[0] // steps
    loads = [
        start_all(
            (src.at[pl.ds(i * rows, rows)], buf.at[pl.ds(i * rows, rows)], sem.at[2 * i + j])
            for j, (src, buf) in enumerate(((a, a_buf), (b, b_buf)))
        )
        for i in range(steps)
    ]
    stores = []
    for i in range(steps):
        finish(loads[i])
        at = pl.ds(i * rows, rows)
        first = 0
        for k, (o, buf, w) in enumerate(zip(outs, bufs, widths)):
            total = a_buf[at, first : first + w].astype(F32) + b_buf[at, first : first + w].astype(F32)
            first += w
            where = (slice(None), at) if w == LANES else (at,)
            buf[where if w == LANES else (at, slice(None))] = total.T if w == LANES else total
            stores += start_all([(buf.at[where], o.at[where], o_sem.at[len(widths) * i + k])])
    finish(stores)


def both_cores(array, widths, name):
    if lax.axis_size("seq") != 8:
        outs = jnp.split(array.astype(F32), [sum(widths[:i]) for i in range(1, len(widths))], axis=1)
        return [o.T if w == LANES else o for o, w in zip(outs, widths)]
    rows = array.shape[0]
    steps = rows // 256
    shapes = [(w, rows) if w == LANES else (rows, w) for w in widths]
    dma = pltpu.SemaphoreType.DMA
    return call(
        functools.partial(k_pair, widths),
        [Far(struct(shape, F32)) for shape in shapes],
        [Far(array), Far(flip(array, "seq", 1))],
        0,
        name,
        scratch=[
            pltpu.VMEM(array.shape, BF16),
            pltpu.VMEM(array.shape, BF16),
            *(pltpu.VMEM(shape, F32) for shape in shapes),
            dma((2 * steps,)),
            dma((len(widths) * steps,)),
        ],
    )


def flip(array, axis, bit):
    return lax.ppermute(array, axis, [(i, i ^ bit) for i in range(lax.axis_size(axis))])


def bits_of(axis):
    return [1 << b for b in range(lax.axis_size(axis).bit_length() - 1)]


class Gathered:
    def __init__(self, pieces, slots, index):
        self.pieces, self.slots, self.index = pieces, slots, index

    def part(self, first, last):
        at, to = sum(self.slots[:first]), sum(self.slots[:last])
        return Gathered(self.pieces[at:to], self.slots[first:last], self.index[first:last])


XOR_ORDER = (0, 1, 2, 4, 3, 5, 6, 7)


def gather_all(own):
    every = lax.all_gather(own, "seq")
    size = every.shape[0]
    return Gathered([every[k] for k in range(size)], [1] * size, jnp.arange(size, dtype=jnp.int32))


def gather(own, half, between):
    if lax.axis_size("seq") != 8:
        return gather_all(own)
    core, x, y = bits_of("seq")
    by_x = flip(own, "seq", x)
    by_y = flip(own, "seq", y)
    far = [flip(own, "seq", core)]
    by_x, by_y = after((by_x, by_y), between[0](own, far[0]))
    top = flip(by_x[:half], "seq", y)
    bottom = flip(by_y[half:], "seq", x)
    far += [flip(by_x, "seq", core), flip(by_y, "seq", core)]
    top, bottom = after((top, bottom), between[1](by_x, by_y))
    far += [flip(top, "seq", core), flip(bottom, "seq", core)]
    pieces = [own, far[0], by_x, by_y, far[1], far[2], top, bottom, far[3], far[4]]
    return Gathered(pieces, [1, 1, 1, 1, 1, 1, 2, 2], xor_index())


def near_index():
    core, x, y = bits_of("seq")
    return jnp.stack([lax.axis_index("seq") ^ k for k in (0, x, y, x | y)]).astype(jnp.int32)


def gather_near(own, half, wait, first=None):
    if lax.axis_size("seq") != 8:
        return gather_all(own)
    core, x, y = bits_of("seq")
    by_x, by_y = after(first or first_hop(own), wait)
    near = [own, by_x, by_y, flip(by_x[:half], "seq", y), flip(by_y[half:], "seq", x)]
    return Gathered(near, [1, 1, 1, 2], near_index())


def first_hop(own):
    core, x, y = bits_of("seq")
    return flip(own, "seq", x), flip(own, "seq", y)


def gather_lean(own, wait, along_x, first=None):
    if lax.axis_size("seq") != 8:
        return gather_all(own)
    core, x, y = bits_of("seq")
    by_x, by_y = first or first_hop(own)
    diagonal = flip(after(by_y, wait), "seq", x) if along_x else flip(after(by_x, wait), "seq", y)
    return Gathered([own, by_x, by_y, diagonal], [1, 1, 1, 1], near_index())


def xor_index():
    return jnp.stack([lax.axis_index("seq") ^ k for k in XOR_ORDER]).astype(jnp.int32)


def low_sum(*terms):
    return sum(t.astype(F32) for t in terms).astype(BF16)


def k_split(x0, x1, y0, y1, d0, d1, o_x, o_y, o_x_late, o_y_late):
    half = o_x_late.shape[0]
    x = low_sum(x0[...], x1[...])
    y = low_sum(y0[...], y1[...])
    d = low_sum(d0[...], d1[...])
    o_x[:half, :] = d[:half]
    o_x[half:, :] = x[:half]
    o_y[:half, :] = d[half:]
    o_y[half:, :] = y[half:]
    o_x_late[...] = x[half:]
    o_y_late[...] = y[:half]


def k_late(x, y, ax, ay, o_x, o_y):
    half = x.shape[0]
    o_x[...] = low_sum(x[...], ay[:half, :])
    o_y[...] = low_sum(y[...], ax[:half, :])


def k_join(a, b, ax, ay, bx, by, o):
    half = bx.shape[0]
    total = a[...].astype(F32) + b[...].astype(F32)
    o[:half, :] = low_sum(total[:half], ax[half:, :], by[...])
    o[half:, :] = low_sum(total[half:], ay[half:, :], bx[...])


def scatter_first(parts, name):
    if lax.axis_size("seq") != 8:
        return [lax.psum_scatter(jnp.concatenate(parts, axis=0), "seq", scatter_dimension=0, tiled=True)]
    parts = dict(zip(XOR_ORDER, parts))
    core, x, y = bits_of("seq")
    rows, width = parts[0].shape
    r3, r5, r7, r1 = (flip(parts[k], "seq", core) for k in (3, 5, 7, 1))
    full, part = struct((rows, width), BF16), struct((rows // 2, width), BF16)
    to_x, to_y, late_x, late_y = call(
        k_split, [full, full, part, part], [parts[2], r3, parts[4], r5, parts[6], r7], 0, name + "_split"
    )
    return [parts[0], r1, flip(to_x, "seq", x), flip(to_y, "seq", y), late_x, late_y]


def scatter_second(state, name):
    if lax.axis_size("seq") != 8:
        return state
    own, r1, ax, ay, late_x, late_y = state
    _, x, y = bits_of("seq")
    part = struct(late_x.shape, BF16)
    late_x, late_y = call(k_late, [part, part], [late_x, late_y, ax, ay], 0, name + "_late")
    return [own, r1, ax, ay, flip(late_x, "seq", x), flip(late_y, "seq", y)]


def scatter_last(state, name):
    if lax.axis_size("seq") != 8:
        return state[0]
    [out] = call(k_join, [struct(state[0].shape, BF16)], state, 0, name + "_join")
    return out


def scan(send, backward, name, beside=(None, None, None), steps=None):
    place = lax.axis_index("seq")
    seqs, size = send.shape[0], send.shape[1] - FRONT
    bits = bits_of("seq")
    state = struct((seqs, size, LANES), F32)
    row = struct((seqs, 8, LANES), F32)
    held = []
    for bit in bits_of("seq"):
        recv = flip(send, "seq", bit)
        is_set = (place & bit) != 0
        ahead = (jnp.logical_not(is_set) if backward else is_set).astype(jnp.int32)[None]
        last = bit == bits[-1]
        wait = beside[min(bit.bit_length() - 1, 2)]
        if wait is not None:
            recv = after(recv, wait)
        outs = [state] if last else [state, row, struct(send.shape, BF16)]
        made = call(
            functools.partial(k_scan, not held, last),
            [Each(o) for o in outs],
            [Scalars(ahead), Each(recv), Each(send), *(Each(a) for a in held)],
            0,
            name,
            grid=seqs,
        )
        if last:
            return made[0]
        held, send = made[:2], made[2]
        if steps is not None:
            steps.append(send)
    return before


def rows_of_mp(array):
    share = array.shape[0] // lax.axis_size("mp")
    return lax.dynamic_slice_in_dim(array, lax.axis_index("mp") * share, share, 0)


def exchange_mp(array):
    return lax.all_to_all(array, "mp", 0, 0, tiled=True)


def to_shares(array):
    size = lax.axis_size("mp")
    return exchange_mp(array.reshape(size, array.shape[0] // size, array.shape[1]))


def gather_mp(array):
    return lax.all_gather(array, "mp", tiled=True)


def after(values, others):
    return lax.optimization_barrier((values, others))[0]


def all_sum(array, axes):
    for axis in axes:
        for bit in bits_of(axis):
            array = array + flip(array, axis, bit)
    return array


def passed_along(block, axis, distance):
    devices = range(lax.axis_size(axis))
    route = [(i - distance, i) for i in devices if i - distance in devices]
    return lax.ppermute(block, axis, route)


def body(
    tokens, lengths, expert_ids, norm_gains, in_z, in_x, in_bc, in_dt, conv_x, conv_bc,
    head_par, gn_gain, out_w, router, shared_in, shared_down, expert_in, expert_down, d_out,
):
    piece, seqs, model = tokens.shape
    width = in_z.shape[1]
    heads = head_par.shape[1]
    experts = router.shape[1]
    half = expert_in.shape[-1]
    n_seq, n_mp = lax.axis_size("seq"), lax.axis_size("mp")
    seq_at, mp_at = lax.axis_index("seq"), lax.axis_index("mp")
    rows = seqs * piece
    share = rows // n_mp
    bc = 2 * STATE
    beside = beside_rows(experts, model)
    dma = pltpu.SemaphoreType.DMA

    meta = jnp.concatenate([lengths, (seq_at * piece).astype(jnp.int32)[None]])
    tok = jnp.transpose(tokens, (1, 0, 2))
    edge_in = passed_along(tokens[piece - (KCONV - 1) :], "seq", 1)
    front = jnp.pad(jnp.transpose(edge_in, (1, 0, 2)), ((0, 0), (FRONT - (KCONV - 1), 0), (0, 0)))
    tok_front = jnp.concatenate([front, tok], axis=1)
    gn = gn_gain[None]
    picked = jnp.sum(
        (expert_ids[..., None] == jnp.arange(LANES, dtype=jnp.int32)).astype(F32), axis=2
    ).astype(BF16)
    small = [conv_x, conv_bc, head_par, Scalars(meta)]
    d_ext = jnp.transpose(jnp.concatenate([d_out, picked], axis=-1), (1, 0, 2)).reshape(rows, model + LANES)

    def both(*shape, dtype=F32):
        return Each(struct((seqs, *shape), dtype))

    normed, gate_z, xbc, dt_raw, send, totals = call(
        k_in,
        [
            both(piece, model, dtype=BF16),
            both(piece, width),
            both(piece + FRONT, width + bc, dtype=BF16),
            both(piece, LANES),
            both(width + FRONT, LANES, dtype=BF16),
            both(8, LANES),
        ],
        [Each(tok_front), norm_gains, in_z, in_x, in_bc, in_dt.T, *small],
        2 * rows * model * (2 * width + bc + LANES),
        "mixer_in",
        grid=seqs,
    )
    entering = scan(send, False, "scan")
    intra, c_mat, ecum = call(
        k_intra,
        [both(piece, width), both(piece, STATE, dtype=BF16), both(piece, width)],
        [Each(xbc), Each(dt_raw), *small],
        2 * rows * piece * width * 4,
        "mixer_intra",
        grid=seqs,
    )
    of_rows = struct((share, model), F32)
    mixed, u, part = call(
        k_out,
        [both(piece, width), both(piece, width, dtype=BF16), both(piece, model + LANES, dtype=BF16)],
        [Each(intra), Each(c_mat), Each(ecum), Each(entering), Each(gate_z), gn, out_w],
        2 * rows * width * (STATE + model),
        "mixer_out",
        grid=seqs,
    )
    tok_own = rows_of_mp(tok.reshape(rows, model))
    d_own = rows_of_mp(d_ext)
    arrived = to_shares(part.reshape(rows, model + LANES))
    residual, mixer_own, two_own, scales = call(
        k_rows_one,
        [of_rows, of_rows, struct((share, model), BF16), struct((share, LANES), F32)],
        [tok_own, norm_gains, arrived],
        0,
        "rows_one",
    )
    d_got = gather(d_ext, piece, (lambda *_: entering, lambda *_: two_own))
    two = gather_mp(two_own)

    mine = ((seq_at * n_mp + mp_at) // 2).astype(jnp.int32)[None]

    x_slots = [1] * (n_seq - 2) + ([2, 2] if n_seq == 8 else [1, 1])

    def expert(pieces, first, last, o_all, shared=()):
        part_d = d_got.part(first, last)
        index, count = part_d.index, last - first
        slots = x_slots[first:last]
        size = rows * count
        return call(
            functools.partial(k_expert, (slots, part_d.slots), bool(shared)),
            [Far(struct((n_seq * rows, model), BF16))]
            + [Far(struct((rows, model + LANES), BF16)), Far(struct((rows, 3 * half), BF16))] * count,
            [
                Scalars(mine), router.T, expert_in, expert_down, *(Far(p) for p in (*pieces, *part_d.pieces)),
                *shared, *(Far(o) for o in o_all),
            ],
            2 * size * model * half * 6.5,
            "experts",
            index=index,
            aliases={5 + len(pieces) + len(part_d.pieces): 0} if o_all else None,
            scratch=[
                pltpu.VMEM((size, model), BF16),
                pltpu.VMEM((size, model + LANES), BF16),
                pltpu.VMEM((size, model), BF16),
                pltpu.VMEM((size, model + LANES), BF16),
                pltpu.VMEM((size, 3 * half), BF16),
                dma((len(pieces),)),
                dma((len(part_d.pieces),)),
                dma((3 * count,)),
            ],
        )

    def shared_of(x):
        return call(
            k_shared,
            [struct((rows, model), BF16), struct((rows, model), BF16)],
            [x, d_ext, shared_in, shared_down],
            2 * rows * model * half * 6,
            "shared",
        )

    made = []

    def near_experts(own, far):
        made.append(expert([own, far], 0, 2, [], shared_of(own)))
        return made[-1][1:]

    def chip_experts(by_x, by_y):
        made.append(expert([by_x, by_y], 2, 4, made[-1][:1]))
        return made[-1][1:]

    if n_seq == 8:
        normed, u = normed.reshape(rows, model), u.reshape(rows, width)
        n_first = first_hop(after(normed, part))
        two, d_got.pieces = lax.optimization_barrier((two, d_got.pieces))
        x_got = gather(two, piece, (near_experts, chip_experts))
        made.append(expert(x_got.pieces[4:], 4, 8, made[-1][:1]))
    else:
        x_got = gather_all(two)
        out_shared, dx_shared = shared_of(two)
        for i in range(0, n_seq, 4):
            made.append(expert(x_got.part(i, i + 4).pieces, i, i + 4, made[-1][:1] if made else []))
    out_all = made[-1][0]
    e_dx = [a for m in made for a in m[1::2]]
    e_keep = [a for m in made for a in m[2::2]]

    g_expert_in = g_expert_down = g_shared_in = g_shared_down = 0.0
    weight_outs = [Far(struct((2, model, half), F32)), Far(struct((half, model), F32))]

    def weight_scratch(keeps, pieces):
        return [
            pltpu.VMEM((8 * rows, model), BF16),
            pltpu.VMEM((8 * rows, model + LANES), BF16),
            pltpu.VMEM((8 * rows, 3 * half), BF16),
            pltpu.VMEM((model, 2 * half), F32),
            pltpu.VMEM((half, model), F32),
            dma((pieces,)),
            dma((pieces,)),
            *([dma((8,))] if keeps else []),
            dma((3 * (model // 256),)),
        ]

    def shared_weights(first, others):
        x = x_got.part(first, first + 8)
        return call(
            functools.partial(k_shared_weights, x.slots),
            weight_outs,
            [shared_in, shared_down, *(Far(a) for a in (*after(x.pieces, others), *d_got.part(first, first + 8).pieces))],
            6 * 2 * 8 * rows * model * half,
            "shared_weights",
            index=x.index,
            scratch=weight_scratch(False, len(x.pieces)),
        )

    def expert_weights(first, others):
        x = x_got.part(first, first + 8)
        return call(
            functools.partial(k_expert_weights, x.slots),
            weight_outs,
            [Far(a) for a in (*after(x.pieces, others), *d_got.part(first, first + 8).pieces, *e_keep[first : first + 8])],
            3 * 2 * 8 * rows * model * half,
            "expert_weights",
            index=x.index,
            scratch=weight_scratch(True, len(x.pieces)),
        )

    state = scatter_first(e_dx, "dx")
    if n_seq == 8:
        g_shared_in, g_shared_down = shared_weights(0, e_dx)
        state, g_shared_in, g_shared_down = lax.optimization_barrier((state, g_shared_in, g_shared_down))
        state = scatter_second(state, "dx")
        g_expert_in, g_expert_down = expert_weights(0, g_shared_down)
        state, g_expert_in, g_expert_down = lax.optimization_barrier((state, g_expert_in, g_expert_down))
    else:
        for first in range(0, n_seq, 8):
            a, b = shared_weights(first, e_dx)
            c, d = expert_weights(first, e_dx)
            g_shared_in, g_shared_down = g_shared_in + a, g_shared_down + b
            g_expert_in, g_expert_down = g_expert_in + c, g_expert_down + d
    dx_sum = scatter_last(state, "dx")
    if n_seq != 8:
        dx_sum = jnp.concatenate([low_sum(dx_sum[:, :model], dx_shared), dx_sum[:, model:]], axis=1)
    arrived = to_shares(dx_sum)
    out_sum = lax.psum_scatter(after(out_all, dx_sum), "seq", scatter_dimension=0, tiled=True)
    if n_seq != 8:
        out_sum = low_sum(out_sum, out_shared)
    dm_own, d_residual, g_two = call(
        k_rows_two,
        [struct((share, model + LANES), BF16), of_rows, struct((experts + 8, model), F32)],
        [d_own, two_own, residual, mixer_own, scales, norm_gains, router.T, arrived],
        0,
        "rows_two",
    )
    dm = gather_mp(dm_own)
    if n_seq == 8:
        n_got = gather_near(normed, piece, dx_sum, n_first)
        u = after(u, dx_sum)
        dm, u_first = lax.optimization_barrier((dm, first_hop(u)))
    else:
        normed, u = after((normed, u), (dm, g_expert_in, g_shared_in))
        n_got = gather_all(normed.reshape(rows, model))
        u_got = gather_all(u.reshape(rows, width))

    dz, dy, send, g_gn = call(
        k_back_gate,
        [
            both(piece, width, dtype=BF16),
            both(piece, width),
            both(width + FRONT, LANES, dtype=BF16),
            both(8, width),
        ],
        [Rows(dm, piece), Each(mixed), Each(gate_z), gn, out_w, Each(c_mat), Each(ecum), Each(totals)],
        2 * rows * width * (model + STATE),
        "back_gate",
        grid=seqs,
    )
    intra_back = call(
        k_back_intra,
        [both(piece, width), both(piece, STATE), both(piece, STATE), both(piece, LANES), both(piece, model)],
        [Each(xbc), Each(dt_raw), *small, Each(dy), Each(dz), in_z],
        2 * rows * width * (model + 4 * piece),
        "back_intra",
        grid=seqs,
    )
    dxw0, db0, dc0, dcum0, dn0 = intra_back
    steps = []
    dm_first = first_hop(dm) if n_seq == 8 else None
    leaving = scan(send, True, "scan_back", (None, None, (intra_back, dm_first)), steps)
    out_arrived = to_shares(after(out_sum, steps[1]))
    dz_first = first_hop(after(dz, leaving).reshape(rows, width)) if n_seq == 8 else None

    def in_order(rows):
        return jnp.transpose(rows.reshape(seqs, piece, model), (1, 0, 2)).astype(F32)

    d_xbc, d_dt, g_conv, g_hp = call(
        k_back_state,
        [
            both(piece + FRONT, width + bc),
            both(piece, LANES, dtype=BF16),
            both(8, width + bc),
            both(8, LANES),
        ],
        [
            Each(xbc), Each(dt_raw), *small, Each(dy), Each(dxw0), Each(db0), Each(dc0), Each(dcum0),
            Each(entering), Each(leaving),
        ],
        2 * rows * width * STATE * 20,
        "back_state",
        grid=seqs,
    )
    edge = passed_along(d_xbc[:, :FRONT], "seq", -1)
    if n_seq == 8:
        edge, out_arrived, dz_first = lax.optimization_barrier((edge, out_arrived, dz_first))
    dx, d_bc, part = call(
        k_back_in,
        [
            struct((rows + SMALL, width + LANES), BF16),
            struct((rows + beside, bc), BF16),
            both(piece, model, dtype=BF16),
        ],
        [
            Each(dn0), Each(d_xbc), Each(edge), Each(d_dt), Each(tok_front), g_conv, g_hp, g_gn, g_two,
            in_x, in_bc, in_dt.T,
        ],
        2 * rows * (width + bc + LANES) * model,
        "back_in",
        grid=seqs,
        scratch=[pltpu.VMEM((8, model), F32)],
    )
    arrived = to_shares(part.reshape(rows, model))
    [out_own] = call(
        k_rows_out, [struct((share, model), BF16)], [residual, after(out_arrived, part)], 0, "rows_out"
    )
    out_shares = [out_own if k == 0 else flip(out_own, "mp", k) for k in range(n_mp)]
    dm_got = gather_near(dm, piece, leaving, dm_first)
    if n_seq == 8:
        u_got = gather_near(u, piece, leaving, u_first)
    dz_got = gather_near(dz.reshape(rows, width), piece, part, dz_first)
    *head_bits, last_bit = bits_of("mp")
    for bit in head_bits:
        d_bc = low_sum(d_bc, flip(d_bc, "mp", bit))
    d_bc = low_sum(d_bc, flip(d_bc, "mp", last_bit))
    bc_got = gather_lean(d_bc, d_bc, False)
    dx_first = first_hop(dx) if n_seq == 8 else None
    if n_seq != 8:
        dx_got = gather_all(dx)

    g_in_z = g_in_x = g_out_w = small = 0.0
    size = min(8, len(n_got.slots))
    for first in range(0, len(n_got.slots), size):
        last = first + size
        g_out_w = g_out_w + out_weights(u_got.part(first, last), dm_got.part(first, last), size * rows)
    if n_seq == 8:
        arrived, g_out_w, d_bc, dx_first = lax.optimization_barrier((arrived, g_out_w, d_bc, dx_first))
        dx_got = gather_near(dx, piece, (), dx_first)
    [rows_own] = call(
        k_rows_three,
        [struct((n_mp, share, model), BF16)],
        [tok_own, d_residual, norm_gains, arrived],
        0,
        "rows_three",
    )
    rows_all = exchange_mp(rows_own)
    for first in range(0, len(n_got.slots), size):
        last = first + size
        [a] = outer(n_got.part(first, last), [dz_got.part(first, last)], size * rows, "weights_z")
        g_in_z = g_in_z + a
    [g_in_z] = both_cores(g_in_z, [width], "cores_z")
    [g_out_w] = both_cores(g_out_w, [model], "cores_out")
    for first in range(0, len(n_got.slots), size):
        last = first + size
        a, b = outer(
            n_got.part(first, last), [dx_got.part(first, last), bc_got.part(first, last)], size * rows, "weights_x",
            beside,
        )
        g_in_x, small = g_in_x + a, small + b
    order = after(jnp.stack([mp_at ^ k for k in range(n_mp)]).astype(jnp.int32), g_in_x)
    [out_rows] = call(k_assemble, [struct((rows, model), BF16)], [Scalars(order), *out_shares], 0, "output")
    output = in_order(out_rows)
    if n_seq == 8:
        rows_all, g_in_x, g_in_z, g_out_w, output = lax.optimization_barrier(
            (rows_all, g_in_x, g_in_z, g_out_w, output)
        )

    d_tokens = in_order(rows_all)
    g_in_x, g_dt, g_in_bc = both_cores(g_in_x, [width, LANES, bc], "cores_x")
    if n_seq == 8:
        small = small + after(flip(small, "seq", 1), g_in_x)
    summed = small[:, width + LANES :]
    cuts = model // bc
    g_router = summed[: cuts * experts].reshape(cuts, experts, bc)
    first = cuts * experts
    return (
        output,
        d_tokens,
        summed[first : first + 2 * cuts].reshape(2, model),
        g_in_z,
        g_in_x,
        g_in_bc,
        g_dt[:heads].T,
        small[: KCONV + 1, :width],
        summed[first + 2 * cuts : first + 2 * cuts + KCONV + 1],
        small[:3, width : width + heads],
        small[KCONV + 1, :width],
        g_out_w,
        jnp.transpose(g_router, (0, 2, 1)).reshape(model, experts),
        g_shared_in,
        g_shared_down,
        g_expert_in[None],
        g_expert_down[None],
    )


def solution(mesh):
    in_specs = (
        P("seq", None, None),
        P(),
        P("seq", None, None),
        P(),
        P(None, "mp"),
        P(None, "mp"),
        P(),
        P(None, "mp"),
        P(None, "mp"),
        P(),
        P(None, "mp"),
        P("mp"),
        P("mp", None),
        P(),
        P(None, None, "mp"),
        P("mp", None),
        P(("seq", "mp"), None, None, None),
        P(("seq", "mp"), None, None),
        P("seq", None, None),
    )
    out_specs = (
        P("seq", None, None),
        P("seq", None, None),
        P(),
        P(None, "mp"),
        P(None, "mp"),
        P(),
        P(None, "mp"),
        P(None, "mp"),
        P(),
        P(None, "mp"),
        P("mp"),
        P("mp", None),
        P(),
        P(None, None, "mp"),
        P("mp", None),
        P(("seq", "mp"), None, None, None),
        P(("seq", "mp"), None, None),
    )
    return jax.shard_map(body, mesh=mesh, in_specs=in_specs, out_specs=out_specs, check_vma=False)
```

```python
import functools

import jax
import jax.numpy as jnp
from jax import lax
from jax.experimental import pallas as pl
from jax.experimental.pallas import tpu as pltpu
from jax.sharding import PartitionSpec as P

HEAD_DIM = 64
STATE = 128
KCONV = 4
INNER = 3072
LANES = 128
SMALL = 16
FRONT = 16
EPSILON = 1e-05
F32 = jnp.float32
BF16 = jnp.bfloat16
HIGHEST = lax.Precision.HIGHEST
NN = (((1,), (0,)), ((), ()))
NT = (((1,), (1,)), ((), ()))
TN = (((0,), (0,)), ((), ()))


class Each:
    def __init__(self, array):
        self.array = array


class Scalars:
    def __init__(self, array):
        self.array = array


class Far:
    def __init__(self, array):
        self.array = array


class Rows:
    def __init__(self, array, rows):
        self.array, self.rows = array, rows


def struct(shape, dtype):
    return jax.ShapeDtypeStruct(tuple(shape), dtype)


def call(kernel, outs, args, flops, name, grid=1, index=None, scratch=(), aliases=None):
    def spec(a):
        if isinstance(a, Scalars):
            return pl.BlockSpec(memory_space=pltpu.SMEM)
        if isinstance(a, Far):
            return pl.BlockSpec(memory_space=pl.ANY)
        if isinstance(a, Rows):
            rest = a.array.shape[1:]
            return pl.BlockSpec((a.rows, *rest), lambda s, *_: (s,) + (0,) * len(rest))
        if isinstance(a, Each):
            rest = a.array.shape[1:]
            return pl.BlockSpec((None, *rest), lambda s, *_: (s,) + (0,) * len(rest))
        return pl.BlockSpec(a.shape, lambda s, *_: (0,) * len(a.shape))

    def plain(a):
        return a.array if isinstance(a, (Each, Scalars, Far, Rows)) else a

    arrays = [plain(a) for a in args]
    shapes = [plain(a) for a in outs]
    moved = sum(a.size * a.dtype.itemsize for a in (*arrays, *shapes))
    grid_spec = pltpu.PrefetchScalarGridSpec(
        num_scalar_prefetch=0 if index is None else 1,
        grid=(grid,),
        in_specs=[spec(a) for a in args],
        out_specs=[spec(a) for a in outs],
        scratch_shapes=list(scratch),
    )
    return pl.pallas_call(
        kernel,
        out_shape=shapes,
        grid_spec=grid_spec,
        input_output_aliases=aliases or {},
        compiler_params=pltpu.CompilerParams(vmem_limit_bytes=60 * 2**20),
        cost_estimate=pl.CostEstimate(flops=int(flops), bytes_accessed=int(moved), transcendentals=0),
        name=name,
    )(*([] if index is None else [index]), *arrays)


def dot(a, b, dims=NN):
    return lax.dot_general(a.astype(BF16), b.astype(BF16), dims, preferred_element_type=F32)


def exact(a, b, dims=NN):
    return lax.dot_general(a, b, dims, precision=HIGHEST, preferred_element_type=F32)


def fine(a, b, dims=NN):
    high, low = two_terms(a)
    return dot(high, b, dims) + dot(low, b, dims)


def sigmoid(v):
    return 1.0 / (1.0 + jnp.exp(-v))


def iota(shape, axis):
    return lax.broadcasted_iota(jnp.int32, shape, axis)


def two_terms(v):
    high = v.astype(BF16)
    return high, (v - high.astype(F32)).astype(BF16)


def to_lanes(v):
    return jnp.concatenate([v, jnp.zeros((v.shape[0], LANES - v.shape[1]), v.dtype)], axis=1)


def to_rows(v):
    return jnp.concatenate([v, jnp.zeros((LANES - v.shape[0], v.shape[1]), v.dtype)], axis=0)


def spread_matrix(width):
    return (iota((LANES, width), 1) // HEAD_DIM == iota((LANES, width), 0)).astype(BF16)


def prepared(xbc, dt, conv_x, conv_bc, head_par, meta):
    rows = dt.shape[0]
    width = conv_x.shape[1]
    conv = jnp.concatenate([conv_x[...], conv_bc[...]], axis=1)
    hp = to_lanes(head_par[...])
    where = iota((rows, 1), 0) + meta[2]
    live = (where < meta[pl.program_id(0)]).astype(F32)
    xf = xbc[...].astype(F32)
    summed = conv[KCONV : KCONV + 1]
    taps = []
    for j in range(KCONV):
        shifted = xf[FRONT - (KCONV - 1) + j : FRONT - (KCONV - 1) + j + rows]
        taps.append(shifted)
        summed = summed + conv[j : j + 1] * shifted
    sig = sigmoid(summed)
    act = summed * sig
    xs = act[:, :width] * live
    b = act[:, width : width + STATE]
    c = act[:, width + STATE :]
    raw = dt[...] + hp[0:1]
    step = (jnp.maximum(raw, 0.0) + jnp.log1p(jnp.exp(-jnp.abs(raw)))) * live
    rate = -jnp.exp(hp[1:2])
    logd = rate * step
    lower = (iota((rows, rows), 0) >= iota((rows, rows), 1)).astype(F32)
    cum = exact(lower, logd)
    return dict(
        conv=conv, skip=hp[2:3], live=live, taps=taps, summed=summed, sig=sig, xs=xs, b=b, c=c, raw=raw,
        step=step, rate=rate, logd=logd, cum=cum,
    )


def pack_state(o_send, state, decay):
    size = state.shape[0]
    high, low = two_terms(decay)
    row = iota((FRONT, LANES), 0)
    more = jnp.where(row == 0, high.astype(F32), 0.0) + jnp.where(row == 1, low.astype(F32), 0.0)
    o_send[:size, :] = state.astype(BF16)
    o_send[size:, :] = more.astype(BF16)


def unpack_state(send):
    size = send.shape[0] - FRONT
    more = send[size:, :].astype(F32)
    return send[:size, :].astype(F32), more[0:1] + more[1:2]


def k_in(tok, gains, wz, wx, wbc, wdt, conv_x, conv_bc, head_par, meta, o_norm, o_z, o_xbc, o_dt, o_send, o_tot):
    width = wz.shape[1]
    x = tok[...].astype(F32)
    scale = lax.rsqrt(jnp.mean(x * x, axis=-1, keepdims=True) + EPSILON)
    normed = (x * scale * gains[0:1]).astype(BF16)
    own = normed[FRONT:]
    o_norm[...] = own
    o_xbc[:, :width] = dot(normed, wx[...]).astype(BF16)
    o_xbc[:, width:] = dot(normed, wbc[...]).astype(BF16)
    o_dt[...] = to_lanes(dot(own, wdt[...], NT))
    o_z[...] = dot(own, wz[...])
    p = prepared(o_xbc, o_dt, conv_x, conv_bc, head_par, meta)
    rows = own.shape[0]
    last = p["cum"][rows - 1 : rows]
    weight = fine(p["step"] * jnp.exp(last - p["cum"]), spread_matrix(width))
    decay = jnp.exp(last)
    pack_state(o_send, dot(p["xs"] * weight, p["b"], TN), decay)
    o_tot[...] = jnp.broadcast_to(decay, o_tot.shape)


def pair_masks(rows):
    low = iota((rows, LANES), 1) < HEAD_DIM
    return low, jnp.logical_not(low)


def decays(cum, cum_t, h, ahead):
    gap = cum[:, h : h + 1] - cum_t[h : h + 1, :]
    return jnp.where(ahead, jnp.exp(jnp.where(ahead, gap, 0.0)), 0.0)


def by_halves(v, low, high):
    return jnp.concatenate(
        [jnp.where(low, v, 0.0).astype(BF16), jnp.where(high, v, 0.0).astype(BF16)], axis=0
    )


def k_intra(xbc, dt, conv_x, conv_bc, head_par, meta, o_y, o_c, o_ecum):
    width = o_y.shape[1]
    p = prepared(xbc, dt, conv_x, conv_bc, head_par, meta)
    xs, cum = p["xs"], p["cum"]
    rows = cum.shape[0]
    spread = spread_matrix(width)
    ahead = iota((rows, rows), 0) >= iota((rows, rows), 1)
    cum_t = cum.T
    scores = dot(p["c"], p["b"], NT)
    spread_out = fine(
        jnp.concatenate([p["step"], jnp.exp(cum), jnp.broadcast_to(p["skip"], (8, LANES))], axis=0), spread
    )
    xw = xs * spread_out[:rows]
    skip = spread_out[2 * rows : 2 * rows + 1]
    low, high = pair_masks(rows)
    o_c[...] = p["c"].astype(BF16)
    o_ecum[...] = spread_out[rows : 2 * rows]
    for pair in range(width // LANES):
        cols = slice(pair * LANES, (pair + 1) * LANES)
        mats = [(decays(cum, cum_t, h, ahead) * scores).astype(BF16) for h in (2 * pair, 2 * pair + 1)]
        within = dot(jnp.concatenate(mats, axis=1), by_halves(xw[:, cols], low, high))
        o_y[:, cols] = within + skip[:, cols] * xs[:, cols]


def k_scan(first, last, after, recv, own, *refs):
    whole, total = unpack_state(own)
    state, decay = unpack_state(recv)
    size = state.shape[0]
    mine = iota((size, LANES), 1) == iota((size, LANES), 0) // HEAD_DIM

    def rows_of(d):
        return jnp.sum(jnp.where(mine, d, 0.0), axis=1, keepdims=True)

    is_after = after[0] == 1
    if first:
        outs = refs
        outs[0][...] = jnp.where(is_after, state, 0.0)
        new_reach = jnp.where(is_after, decay, 1.0)
    else:
        before, reach = refs[:2]
        outs = refs[2:]
        outs[0][...] = jnp.where(is_after, before[...] + rows_of(reach[0:1]) * state, before[...])
        new_reach = jnp.where(is_after, reach[0:1] * decay, reach[0:1])
    if last:
        return
    outs[1][...] = jnp.broadcast_to(new_reach, outs[1].shape)
    new_whole = jnp.where(is_after, whole + rows_of(total) * state, state + rows_of(decay) * whole)
    pack_state(outs[2], new_whole, total * decay)


def k_out(y0, c, ecum, entering, z, gain, w, o_y, o_u, o_part):
    model = w.shape[1]
    y = y0[...] + ecum[...] * dot(c[...], entering[...], NT)
    o_y[...] = y
    zv = z[...]
    gated = y * zv * sigmoid(zv)
    high, low = two_terms(jnp.sum(gated * gated, axis=-1, keepdims=True))
    o_u[...] = (gated * gain[...]).astype(BF16)
    o_part[:, :model] = dot(o_u[...], w[...]).astype(BF16)
    o_part[:, model:] = to_lanes(jnp.concatenate([high, low], axis=1))


def k_back_gate(dm, y, z, gain, w, c, ecum, total, o_dz, o_dy, o_send, o_gain):
    model = w.shape[1]
    more = dm[:, model:].astype(F32)
    stat = more[:, 0:1] + more[:, 1:2]
    scale = more[:, 2:3] + more[:, 3:4]
    dn = dot(dm[:, :model], w[...], NT)
    zv = z[...]
    sig = sigmoid(zv)
    silu = zv * sig
    yv = y[...]
    gated = yv * silu
    dgated = scale * gain[...] * dn - gated * (scale * scale * stat / INNER)
    o_dz[...] = (dgated * yv * sig * (1.0 + zv * (1.0 - sig))).astype(BF16)
    dy = dgated * silu
    o_dy[...] = dy
    o_gain[...] = jnp.broadcast_to(jnp.sum(dn * gated * scale, axis=0, keepdims=True), o_gain.shape)
    pack_state(o_send, dot(ecum[...] * dy, c[...], TN), total[0:1])


def k_back_intra(xbc, dt, conv_x, conv_bc, head_par, meta, dy, dz, wz, o_dxw, o_db, o_dc, o_dcum, o_dn):
    width = dy.shape[1]
    p = prepared(xbc, dt, conv_x, conv_bc, head_par, meta)
    cum = p["cum"]
    rows = cum.shape[0]
    o_dn[...] = dot(dz[...], wz[...], NT)
    ahead = iota((rows, rows), 0) >= iota((rows, rows), 1)
    cum_t = cum.T
    scores = dot(p["c"], p["b"], NT)
    xw = p["xs"] * fine(p["step"], spread_matrix(width))
    low, high = pair_masks(rows)
    lane = iota((rows, LANES), 1)
    sub = iota((LANES, rows), 0)
    dscores = jnp.zeros((rows, rows), F32)
    plus = jnp.zeros((rows, LANES), F32)
    minus = jnp.zeros((LANES, rows), F32)
    for pair in range(width // LANES):
        cols = slice(pair * LANES, (pair + 1) * LANES)
        dstack = by_halves(dy[:, cols], low, high)
        dmats = dot(dstack, xw[:, cols], NT)
        mats = []
        for i, h in enumerate((2 * pair, 2 * pair + 1)):
            decay = decays(cum, cum_t, h, ahead)
            mat = decay * scores
            dmat = dmats[i * rows : (i + 1) * rows]
            dscores = dscores + dmat * decay
            flow = dmat * mat
            plus = jnp.where(lane == h, jnp.sum(flow, axis=1, keepdims=True), plus)
            minus = jnp.where(sub == h, jnp.sum(flow, axis=0, keepdims=True), minus)
            mats.append(mat.astype(BF16))
        o_dxw[:, cols] = dot(jnp.concatenate(mats, axis=0), dstack, TN)
    o_dcum[...] = plus - minus.T
    o_dc[...] = dot(dscores, p["b"])
    o_db[...] = dot(dscores, p["c"], TN)


def k_back_state(
    xbc, dt, conv_x, conv_bc, head_par, meta, dy, dxw0, db0, dc0, dcum0, entering, leaving,
    o_dxbc, o_ddt, o_conv, o_hp,
):
    width = dy.shape[1]
    p = prepared(xbc, dt, conv_x, conv_bc, head_par, meta)
    xs, b, c, cum, step, rate, live = (p[k] for k in ("xs", "b", "c", "cum", "step", "rate", "live"))
    summed, sig, conv = p["summed"], p["sig"], p["conv"]
    rows = cum.shape[0]
    spread = spread_matrix(width)
    last = cum[rows - 1 : rows]
    spread_out = fine(
        jnp.concatenate(
            [step, jnp.exp(cum), jnp.exp(last - cum), jnp.broadcast_to(p["skip"], (8, LANES))], axis=0
        ),
        spread,
    )
    step_x, ecum_x, rem_x = (spread_out[i * rows : (i + 1) * rows] for i in range(3))
    skip_x = spread_out[3 * rows : 3 * rows + 1]
    dyv = dy[...]
    h0 = entering[...]
    h1 = leaving[...]
    xw = xs * step_x
    scaled_dy = ecum_x * dyv
    dc = dc0[...] + dot(scaled_dy, h0)
    from_state = scaled_dy * dot(c, h0, NT)
    to_state = rem_x * dot(b, h1, NT)
    dxw = dxw0[...] + to_state
    db = db0[...] + dot(xw * rem_x, h1)
    high, low = two_terms(h1 * h0)
    dtotal = jnp.sum(dot(spread, high) + dot(spread, low), axis=1, keepdims=True)
    sums = fine(jnp.concatenate([from_state, xw * to_state, dxw * xs, dyv * xs], axis=0), spread, NT)
    flow = sums[rows : 2 * rows]
    dlast = jnp.broadcast_to(dtotal, (LANES, LANES)).T[0:1] * jnp.exp(last) + jnp.sum(
        flow, axis=0, keepdims=True
    )
    dcum = dcum0[...] + sums[:rows] - flow
    dcum = dcum + jnp.where(iota((rows, LANES), 0) == rows - 1, dlast, 0.0)
    upper = (iota((rows, rows), 0) <= iota((rows, rows), 1)).astype(F32)
    dlogd = exact(upper, dcum)
    draw = (sums[2 * rows : 3 * rows] + dlogd * rate) * live * sigmoid(p["raw"])
    o_ddt[...] = draw.astype(BF16)
    row = iota((8, LANES), 0)
    o_hp[...] = (
        jnp.where(row == 0, jnp.sum(draw, axis=0, keepdims=True), 0.0)
        + jnp.where(row == 1, jnp.sum(dlogd * p["logd"], axis=0, keepdims=True), 0.0)
        + jnp.where(row == 2, jnp.sum(sums[3 * rows : 4 * rows], axis=0, keepdims=True), 0.0)
    )
    dx = (dxw * step_x + skip_x * dyv) * live
    dsummed = jnp.concatenate([dx, db, dc], axis=1) * sig * (1.0 + summed * (1.0 - sig))
    zeros = jnp.zeros((FRONT, dsummed.shape[1]), F32)
    padded = jnp.concatenate([zeros, dsummed, zeros], axis=0)
    total = rows + FRONT
    out = jnp.zeros((total, dsummed.shape[1]), F32)
    for j in range(KCONV):
        shift = KCONV - 1 - j
        out = out + conv[j : j + 1] * padded[shift : shift + total]
        o_conv[j : j + 1] = jnp.sum(dsummed * p["taps"][j], axis=0, keepdims=True)
    o_conv[KCONV : KCONV + 1] = jnp.sum(dsummed, axis=0, keepdims=True)
    o_conv[KCONV + 1 :] = jnp.zeros((o_conv.shape[0] - KCONV - 1, dsummed.shape[1]), F32)
    o_dxbc[...] = out


def beside_rows(experts, model):
    need = (experts + 2) * model // (2 * STATE) + KCONV + 1
    return -(-need // 64) * 64


def k_back_in(dn0, dxbc, edge, ddt, tok, g_conv, g_hp, g_gn, g_two, wx, wbc, wdt, o_dx, o_bc, o_part, gain):
    width = wx.shape[1]
    rows, model = dn0.shape
    experts = g_two.shape[0] - 8
    step = pl.program_id(0)
    tail = jnp.concatenate([jnp.zeros((rows - FRONT, edge.shape[1]), F32), edge[...]], axis=0)
    own = (dxbc[FRONT:, :] + tail).astype(BF16)
    dx, dbc = own[:, :width], own[:, width:]
    to = pl.ds(pl.multiple_of(step * rows, rows), rows)
    o_dx[to, :width] = dx
    o_dx[to, width:] = ddt[...]
    o_bc[to, :] = dbc
    dn = dn0[...] + dot(dx, wx[...], NT) + dot(dbc, wbc[...], NT) + dot(ddt[...], to_rows(wdt[...]))
    o_part[...] = dn.astype(BF16)
    x = tok[FRONT:, :].astype(F32)
    scale = lax.rsqrt(jnp.mean(x * x, axis=-1, keepdims=True) + EPSILON)
    now = jnp.sum(dn * x * scale, axis=0, keepdims=True)

    @pl.when(step == 0)
    def _():
        gain[0:1, :] = now

    @pl.when(step > 0)
    def _():
        gain[0:1, :] += now

    @pl.when(step == pl.num_programs(0) - 1)
    def _():
        conv = jnp.sum(g_conv[...], axis=0)
        left = jnp.concatenate(
            [
                conv[: KCONV + 1, :width],
                jnp.sum(g_gn[...], axis=0)[0:1],
                jnp.zeros((SMALL - KCONV - 2, width), F32),
            ],
            axis=0,
        )
        right = jnp.concatenate([jnp.sum(g_hp[...], axis=0), jnp.zeros((SMALL - 8, LANES), F32)], axis=0)
        below = rows * pl.num_programs(0)
        more = pl.ds(pl.multiple_of(below, rows), SMALL)
        o_dx[more, :width] = left.astype(BF16)
        o_dx[more, width:] = right.astype(BF16)
        bc = dbc.shape[1]
        cuts = [slice(j * bc, (j + 1) * bc) for j in range(model // bc)]
        kept = [g_two[:experts, c] for c in cuts]
        kept += [gain[0:1, c] for c in cuts] + [g_two[experts : experts + 1, c] for c in cuts]
        kept.append(conv[: KCONV + 1, width:])
        size = beside_rows(experts, model)
        kept.append(jnp.zeros((size - sum(k.shape[0] for k in kept), bc), F32))
        o_bc[pl.ds(pl.multiple_of(below, rows), size), :] = jnp.concatenate(kept, axis=0).astype(BF16)


def total_of(arrived):
    return sum(arrived[k].astype(F32) for k in range(arrived.shape[0]))


def k_rows_one(tok, gains, arrived, o_residual, o_mixer, o_two, o_scales):
    model = tok.shape[1]
    total = total_of(arrived)
    scale = lax.rsqrt((total[:, model : model + 1] + total[:, model + 1 : model + 2]) / INNER + EPSILON)
    mixer = total[:, :model] * scale
    residual = tok[...].astype(F32) + mixer
    scale_two = lax.rsqrt(jnp.mean(residual * residual, axis=-1, keepdims=True) + EPSILON)
    o_residual[...] = residual
    o_mixer[...] = mixer
    o_two[...] = (residual * scale_two * gains[1:2]).astype(BF16)
    o_scales[...] = to_lanes(jnp.concatenate([scale, scale_two], axis=1))


def k_rows_two(dout, two, residual, mixer, scales, gains, router, arrived, o_dm, o_dr, o_small):
    model = two.shape[1]
    experts = router.shape[0]
    both = total_of(arrived)
    dn2, dgate = both[:, :model], both[:, model:]
    w = to_rows(router[...])
    probs = masked_softmax(dot(two[...], w, NT), dout[:, model:].astype(F32))
    dlog = (probs * (dgate - jnp.sum(probs * dgate, axis=-1, keepdims=True))).astype(BF16)
    dn2 = dn2 + dot(dlog, w)
    scale, scale_two = scales[:, 0:1], scales[:, 1:2]
    scaled = residual[...] * scale_two
    o_small[:experts, :] = dot(dlog, two[...], TN)[:experts]
    o_small[experts:, :] = jnp.broadcast_to(jnp.sum(dn2 * scaled, axis=0, keepdims=True), (8, model))
    gg = dn2 * gains[1:2]
    dr = dout[:, :model].astype(F32) + scale_two * (
        gg - scaled * jnp.mean(gg * scaled, axis=-1, keepdims=True)
    )
    o_dr[...] = dr
    dm = dr.astype(BF16)
    stat = jnp.sum(dm.astype(F32) * mixer[...], axis=-1, keepdims=True)
    o_dm[:, :model] = dm
    o_dm[:, model:] = to_lanes(jnp.concatenate([*two_terms(stat), *two_terms(scale)], axis=1))


def k_rows_out(residual, arrived, o):
    o[...] = (residual[...] + total_of(arrived)).astype(BF16)


def k_assemble(at, *refs):
    o = refs[-1]
    share = refs[0].shape[0]
    for k, r in enumerate(refs[:-1]):
        o[pl.ds(pl.multiple_of(at[k] * share, share), share), :] = r[...]


def k_rows_three(tok, dr, gains, arrived, o):
    dn1 = total_of(arrived)
    x = tok[...].astype(F32)
    scale = lax.rsqrt(jnp.mean(x * x, axis=-1, keepdims=True) + EPSILON)
    scaled = x * scale
    gg = dn1 * gains[0:1]
    dtok = (dr[...] + scale * (gg - scaled * jnp.mean(gg * scaled, axis=-1, keepdims=True))).astype(BF16)
    for k in range(o.shape[0]):
        o[k] = dtok


def masked_softmax(logits, mask):
    on = mask > 0.0
    top = jnp.max(jnp.where(on, logits, -3.0e38), axis=-1, keepdims=True)
    e = jnp.where(on, jnp.exp(jnp.where(on, logits - top, 0.0)), 0.0)
    return e / jnp.sum(e, axis=-1, keepdims=True)


def mlp(x, do, wg, wu, wd, gate):
    g = dot(x, wg)
    u = dot(x, wu)
    sig = sigmoid(g)
    silu = g * sig
    hid = (silu * u).astype(BF16)
    dh = dot(do, wd, NT)
    if gate is None:
        hg, dgate = hid, None
    else:
        hf = hid.astype(F32)
        dgate = jnp.sum(hf * dh, axis=-1, keepdims=True)
        hg = (hf * gate).astype(BF16)
        dh = dh * gate
    dg = (dh * u * sig * (1.0 + g * (1.0 - sig))).astype(BF16)
    du = (dh * silu).astype(BF16)
    return hg, dg, du, dgate


def start_all(copies):
    made = [pltpu.make_async_copy(src, dst, sem) for src, dst, sem in copies]
    for c in made:
        c.start()
    return made


def piece_copies(xs, slots, buffer, sems):
    out, at = [], 0
    rows = buffer.shape[0] // len(slots)
    for i, pieces in enumerate(slots):
        size = rows // pieces
        out.append(
            start_all(
                (xs[at + j].at[pl.ds(0, size)], buffer.at[pl.ds(i * rows + j * size, size)], sems.at[at + j])
                for j in range(pieces)
            )
        )
        at += pieces
    return out


def finish(copies):
    for c in copies:
        c.wait()


def k_expert(slots, with_shared, index, *refs):
    mine, router, w_in, w_down = refs[:4]
    slots, d_slots = slots
    pieces, d_pieces, count = sum(slots), sum(d_slots), len(slots)
    xs, ds = refs[4 : 4 + pieces], refs[4 + pieces : 4 + pieces + d_pieces]
    at = 4 + pieces + d_pieces
    shared = refs[at : at + 2] if with_shared else ()
    refs = refs[len(refs) - 9 - 2 * count :]
    o_all, outs = refs[0], refs[1 : 1 + 2 * count]
    x_buf, d_buf, out_buf, dx_buf, keep_buf, x_sem, d_sem, o_sem = refs[1 + 2 * count :]
    rows = x_buf.shape[0] // count
    x_copies = piece_copies(xs, slots, x_buf, x_sem)
    d_copies = piece_copies(ds, d_slots, d_buf, d_sem)
    width = w_in.shape[2]
    wg, wu, wd = w_in[0, 0], w_in[0, 1], w_down[0]
    w = to_rows(router[...])
    half = wg.shape[1]
    stores = []
    for i in range(count):
        at = pl.ds(i * rows, rows)
        finish(x_copies[i] + d_copies[i])
        x = x_buf[at, :]
        do = d_buf[at, :width]
        mask = d_buf[at, width:].astype(F32)
        lane = iota(mask.shape, 1)
        probs = masked_softmax(dot(x, w, NT), mask)
        gate = jnp.sum(jnp.where(lane == mine[0], probs, 0.0), axis=-1, keepdims=True)
        hg, dg, du, dgate = mlp(x, do, wg, wu, wd, gate)
        dx = dot(dg, wg, NT) + dot(du, wu, NT)
        out = dot(hg, wd)
        if with_shared and i == 0:
            out = out + shared[0][...].astype(F32)
            dx = dx + shared[1][...].astype(F32)
        dx_buf[at, :width] = dx.astype(BF16)
        chosen = jnp.sum(jnp.where(lane == mine[0], mask, 0.0), axis=-1, keepdims=True) > 0.0
        dx_buf[at, width:] = jnp.where(jnp.logical_and(lane == mine[0], chosen), dgate, 0.0).astype(BF16)
        stores += start_all([(dx_buf.at[at], outs[2 * i], o_sem.at[3 * i + 1])])
        out_buf[at, :] = out.astype(BF16)
        keep_buf[at, :half] = hg
        keep_buf[at, half : 2 * half] = dg
        keep_buf[at, 2 * half :] = du
        stores += start_all(
            [
                (
                    out_buf.at[at],
                    o_all.at[pl.ds(pl.multiple_of(index[i] * rows, rows), rows)],
                    o_sem.at[3 * i],
                ),
                (keep_buf.at[at], outs[2 * i + 1], o_sem.at[3 * i + 2]),
            ]
        )
    finish(stores)


def k_shared(x, do, w_in, w_down, o_out, o_dx):
    width = w_in.shape[1]
    wg, wu, wd = w_in[0], w_in[1], w_down[...]
    hg, dg, du, _ = mlp(x[...], do[:, :width], wg, wu, wd, None)
    o_out[...] = dot(hg, wd).astype(BF16)
    o_dx[...] = (dot(dg, wg, NT) + dot(du, wu, NT)).astype(BF16)


def store_in_cuts(buffer, at, cuts, outs, sems, first):
    return start_all(
        (buffer.at[at, pl.ds(begin, size)], out.at[at], sems.at[first + j])
        for j, (out, (begin, size)) in enumerate(zip(outs, cuts))
    )


def weight_products(x_buf, d_buf, keep_buf, in_buf, down_buf, o_in, o_down, o_sem):
    half = down_buf.shape[0]
    width = in_buf.shape[0]
    step = 256
    stores = []
    for c in range(width // step):
        to = pl.ds(c * step, step)
        in_buf[to, :] = dot(x_buf[:, to], keep_buf[:, half:], TN)
        stores += store_in_cuts(in_buf, to, [(0, half), (half, half)], [o_in.at[0], o_in.at[1]], o_sem, 3 * c)
        down_buf[:, to] = dot(keep_buf[:, :half], d_buf[:, to], TN)
        stores += start_all([(down_buf.at[:, to], o_down.at[:, to], o_sem.at[3 * c + 2])])
    finish(stores)


def k_expert_weights(slots, index, *refs):
    pieces, count = sum(slots), len(slots)
    xs, ds, ks = refs[:pieces], refs[pieces : 2 * pieces], refs[2 * pieces : 2 * pieces + count]
    o_in, o_down, x_buf, d_buf, keep_buf, in_buf, down_buf, x_sem, d_sem, k_sem, o_sem = refs[2 * pieces + count :]
    rows = x_buf.shape[0] // count
    copies = piece_copies(xs, slots, x_buf, x_sem) + piece_copies(ds, slots, d_buf, d_sem)
    copies += [start_all([(ks[i], keep_buf.at[pl.ds(i * rows, rows)], k_sem.at[i])]) for i in range(count)]
    for c in copies:
        finish(c)
    weight_products(x_buf, d_buf, keep_buf, in_buf, down_buf, o_in, o_down, o_sem)


def k_shared_weights(slots, index, *refs):
    s_in, s_down = refs[:2]
    pieces, count = sum(slots), len(slots)
    xs, ds = refs[2 : 2 + pieces], refs[2 + pieces : 2 + 2 * pieces]
    o_in, o_down, x_buf, d_buf, keep_buf, in_buf, down_buf, x_sem, d_sem, o_sem = refs[2 + 2 * pieces :]
    rows = x_buf.shape[0] // count
    x_copies = piece_copies(xs, slots, x_buf, x_sem)
    d_copies = piece_copies(ds, slots, d_buf, d_sem)
    half = s_down.shape[0]
    width = s_in.shape[1]
    for i in range(count):
        at = pl.ds(i * rows, rows)
        finish(x_copies[i] + d_copies[i])
        hg, dg, du, _ = mlp(x_buf[at, :], d_buf[at, :width], s_in[0], s_in[1], s_down[...], None)
        keep_buf[at, :half] = hg
        keep_buf[at, half : 2 * half] = dg
        keep_buf[at, 2 * half :] = du
    weight_products(x_buf, d_buf, keep_buf, in_buf, down_buf, o_in, o_down, o_sem)


def k_outer(groups, small, index, *refs):
    counts = [sum(g) for g in groups]
    total = sum(counts)
    o = refs[total]
    a_buf, b_buf, o_buf, sem, o_sem = refs[total + 1 + small : total + 6 + small]
    copies, at, column = [], 0, 0
    tails = []
    for g, slots in enumerate(groups):
        pieces = refs[at : at + counts[g]]
        width = pieces[0].shape[1]
        buffer = a_buf if g == 0 else b_buf.at[:, pl.ds(column, width)]
        column += 0 if g == 0 else width
        copies += piece_copies(pieces, slots, buffer, sem.at[pl.ds(at, counts[g])])
        at += counts[g]
        if small and g > 0:
            rows = a_buf.shape[0] // len(slots)
            first = 0
            for n in slots:
                piece = pieces[first + n - 1]
                tails.append((piece, rows // n, column - width, width))
                first += n
    if small:
        o_small, t_buf, t_sem = refs[total + 1], refs[-2], refs[-1]
        moves = []
        for k, (piece, begin, to, width) in enumerate(tails):
            size = piece.shape[0] - begin
            into = t_buf.at[k % len(groups[0]), pl.ds(0, size), pl.ds(to, width)]
            moves.append((piece.at[pl.ds(begin, size)], into, t_sem.at[k]))
        finish(start_all(moves))
        for k in (0, len(groups[0])):
            piece, begin, to, width = tails[k]
            size = piece.shape[0] - begin
            o_small[:, to : to + width] = jnp.zeros((o_small.shape[0], width), F32)
            o_small[:size, to : to + width] = sum(
                t_buf[j, :size, to : to + width].astype(F32) for j in range(len(groups[0]))
            )
    for c in copies:
        finish(c)
    step = 256
    stores = []
    for c in range(a_buf.shape[1] // step):
        at = pl.ds(c * step, step)
        o_buf[at, :] = dot(a_buf[:, at], b_buf[...], TN).astype(BF16)
        stores += start_all([(o_buf.at[at], o.at[at], o_sem.at[c])])
    finish(stores)


def outer(a, bs, rows, name, small=0):
    columns = a.pieces[0].shape[1]
    total = sum(b.pieces[0].shape[1] for b in bs)
    pieces = [p for g in (a, *bs) for p in g.pieces]
    blocks = len(a.slots)
    dma = pltpu.SemaphoreType.DMA
    more = [pltpu.VMEM((blocks, small, total), BF16), dma((blocks * len(bs),))] if small else []
    return call(
        functools.partial(k_outer, [g.slots for g in (a, *bs)], int(small > 0)),
        [Far(struct((columns, total), BF16)), *([struct((small, total), F32)] if small else [])],
        [Far(p) for p in pieces],
        2 * rows * columns * total,
        name,
        index=a.index,
        scratch=[
            pltpu.VMEM((rows, columns), BF16),
            pltpu.VMEM((rows, total), BF16),
            pltpu.VMEM((columns, total), BF16),
            dma((len(pieces),)),
            dma((columns // 256,)),
            *more,
        ],
    )


def k_out_weights(slots, d_slots, index, *refs):
    n, total = sum(slots), sum(slots) + sum(d_slots)
    us, ds = refs[:n], refs[n:total]
    o, u_buf, d_buf, o_buf, u_sem, d_sem, o_sem = refs[total:]
    model = o.shape[1]
    u_copies = piece_copies(us, slots, u_buf, u_sem)
    d_copies = piece_copies(ds, d_slots, d_buf, d_sem)
    rows = d_buf.shape[0] // len(slots)
    for i in range(len(slots)):
        finish(u_copies[i] + d_copies[i])
        at = pl.ds(i * rows, rows)
        more = d_buf[at, model:].astype(F32)
        d_buf[at, :model] = (d_buf[at, :model].astype(F32) * (more[:, 2:3] + more[:, 3:4])).astype(BF16)
    step = 256
    stores = []
    for c in range(u_buf.shape[1] // step):
        at = pl.ds(c * step, step)
        o_buf[at, :] = dot(u_buf[:, at], d_buf[:, :model], TN).astype(BF16)
        stores += start_all([(o_buf.at[at], o.at[at], o_sem.at[c])])
    finish(stores)


def out_weights(u, d, rows):
    width, model = u.pieces[0].shape[1], d.pieces[0].shape[1] - LANES
    dma = pltpu.SemaphoreType.DMA
    [out] = call(
        functools.partial(k_out_weights, u.slots, d.slots),
        [Far(struct((width, model), BF16))],
        [Far(p) for p in (*u.pieces, *d.pieces)],
        2 * rows * width * model,
        "out_weights",
        index=u.index,
        scratch=[
            pltpu.VMEM((rows, width), BF16),
            pltpu.VMEM((rows, model + LANES), BF16),
            pltpu.VMEM((width, model), BF16),
            dma((len(u.pieces),)),
            dma((len(d.pieces),)),
            dma((width // 256,)),
        ],
    )
    return out


def k_pair(widths, a, b, *refs):
    outs = refs[: len(widths)]
    a_buf, b_buf = refs[len(widths) : len(widths) + 2]
    bufs, sem, o_sem = refs[len(widths) + 2 : -2], refs[-2], refs[-1]
    steps = sem.shape[0] // 2
    rows = a_buf.shape[0] // steps
    loads = [
        start_all(
            (src.at[pl.ds(i * rows, rows)], buf.at[pl.ds(i * rows, rows)], sem.at[2 * i + j])
            for j, (src, buf) in enumerate(((a, a_buf), (b, b_buf)))
        )
        for i in range(steps)
    ]
    stores = []
    for i in range(steps):
        finish(loads[i])
        at = pl.ds(i * rows, rows)
        first = 0
        for k, (o, buf, w) in enumerate(zip(outs, bufs, widths)):
            total = a_buf[at, first : first + w].astype(F32) + b_buf[at, first : first + w].astype(F32)
            first += w
            where = (slice(None), at) if w == LANES else (at,)
            buf[where if w == LANES else (at, slice(None))] = total.T if w == LANES else total
            stores += start_all([(buf.at[where], o.at[where], o_sem.at[len(widths) * i + k])])
    finish(stores)


def both_cores(array, widths, name):
    if lax.axis_size("seq") != 8:
        outs = jnp.split(array.astype(F32), [sum(widths[:i]) for i in range(1, len(widths))], axis=1)
        return [o.T if w == LANES else o for o, w in zip(outs, widths)]
    rows = array.shape[0]
    steps = rows // 256
    shapes = [(w, rows) if w == LANES else (rows, w) for w in widths]
    dma = pltpu.SemaphoreType.DMA
    return call(
        functools.partial(k_pair, widths),
        [Far(struct(shape, F32)) for shape in shapes],
        [Far(array), Far(flip(array, "seq", 1))],
        0,
        name,
        scratch=[
            pltpu.VMEM(array.shape, BF16),
            pltpu.VMEM(array.shape, BF16),
            *(pltpu.VMEM(shape, F32) for shape in shapes),
            dma((2 * steps,)),
            dma((len(widths) * steps,)),
        ],
    )


def flip(array, axis, bit):
    return lax.ppermute(array, axis, [(i, i ^ bit) for i in range(lax.axis_size(axis))])


def bits_of(axis):
    return [1 << b for b in range(lax.axis_size(axis).bit_length() - 1)]


class Gathered:
    def __init__(self, pieces, slots, index):
        self.pieces, self.slots, self.index = pieces, slots, index

    def part(self, first, last):
        at, to = sum(self.slots[:first]), sum(self.slots[:last])
        return Gathered(self.pieces[at:to], self.slots[first:last], self.index[first:last])


XOR_ORDER = (0, 1, 2, 4, 3, 5, 6, 7)


def gather_all(own):
    every = lax.all_gather(own, "seq")
    size = every.shape[0]
    return Gathered([every[k] for k in range(size)], [1] * size, jnp.arange(size, dtype=jnp.int32))


def gather(own, half, between):
    if lax.axis_size("seq") != 8:
        return gather_all(own)
    core, x, y = bits_of("seq")
    by_x = flip(own, "seq", x)
    by_y = flip(own, "seq", y)
    far = [flip(own, "seq", core)]
    by_x, by_y = after((by_x, by_y), between[0](own, far[0]))
    top = flip(by_x[:half], "seq", y)
    bottom = flip(by_y[half:], "seq", x)
    far += [flip(by_x, "seq", core), flip(by_y, "seq", core)]
    top, bottom = after((top, bottom), between[1](by_x, by_y))
    far += [flip(top, "seq", core), flip(bottom, "seq", core)]
    pieces = [own, far[0], by_x, by_y, far[1], far[2], top, bottom, far[3], far[4]]
    return Gathered(pieces, [1, 1, 1, 1, 1, 1, 2, 2], xor_index())


def near_index():
    core, x, y = bits_of("seq")
    return jnp.stack([lax.axis_index("seq") ^ k for k in (0, x, y, x | y)]).astype(jnp.int32)


def gather_near(own, half, wait, first=None):
    if lax.axis_size("seq") != 8:
        return gather_all(own)
    core, x, y = bits_of("seq")
    by_x, by_y = after(first or first_hop(own), wait)
    near = [own, by_x, by_y, flip(by_x[:half], "seq", y), flip(by_y[half:], "seq", x)]
    return Gathered(near, [1, 1, 1, 2], near_index())


def first_hop(own):
    core, x, y = bits_of("seq")
    return flip(own, "seq", x), flip(own, "seq", y)


def gather_lean(own, wait, along_x, first=None):
    if lax.axis_size("seq") != 8:
        return gather_all(own)
    core, x, y = bits_of("seq")
    by_x, by_y = first or first_hop(own)
    diagonal = flip(after(by_y, wait), "seq", x) if along_x else flip(after(by_x, wait), "seq", y)
    return Gathered([own, by_x, by_y, diagonal], [1, 1, 1, 1], near_index())


def gather_direct(own, first=None):
    if lax.axis_size("seq") != 8:
        return gather_all(own)
    core, x, y = bits_of("seq")
    by_x, by_y = first or first_hop(own)
    return Gathered([own, by_x, by_y, flip(own, "seq", x | y)], [1, 1, 1, 1], near_index())


def xor_index():
    return jnp.stack([lax.axis_index("seq") ^ k for k in XOR_ORDER]).astype(jnp.int32)


def low_sum(*terms):
    return sum(t.astype(F32) for t in terms).astype(BF16)


def k_split(x0, x1, y0, y1, d0, d1, o_x, o_y, o_x_late, o_y_late):
    half = o_x_late.shape[0]
    x = low_sum(x0[...], x1[...])
    y = low_sum(y0[...], y1[...])
    d = low_sum(d0[...], d1[...])
    o_x[:half, :] = d[:half]
    o_x[half:, :] = x[:half]
    o_y[:half, :] = d[half:]
    o_y[half:, :] = y[half:]
    o_x_late[...] = x[half:]
    o_y_late[...] = y[:half]


def k_late(x, y, ax, ay, o_x, o_y):
    half = x.shape[0]
    o_x[...] = low_sum(x[...], ay[:half, :])
    o_y[...] = low_sum(y[...], ax[:half, :])


def k_join(a, b, ax, ay, bx, by, o):
    half = bx.shape[0]
    total = a[...].astype(F32) + b[...].astype(F32)
    o[:half, :] = low_sum(total[:half], ax[half:, :], by[...])
    o[half:, :] = low_sum(total[half:], ay[half:, :], bx[...])


def scatter_first(parts, name):
    if lax.axis_size("seq") != 8:
        return [lax.psum_scatter(jnp.concatenate(parts, axis=0), "seq", scatter_dimension=0, tiled=True)]
    parts = dict(zip(XOR_ORDER, parts))
    core, x, y = bits_of("seq")
    rows, width = parts[0].shape
    r3, r5, r7, r1 = (flip(parts[k], "seq", core) for k in (3, 5, 7, 1))
    full, part = struct((rows, width), BF16), struct((rows // 2, width), BF16)
    to_x, to_y, late_x, late_y = call(
        k_split, [full, full, part, part], [parts[2], r3, parts[4], r5, parts[6], r7], 0, name + "_split"
    )
    return [parts[0], r1, flip(to_x, "seq", x), flip(to_y, "seq", y), late_x, late_y]


def scatter_second(state, name):
    if lax.axis_size("seq") != 8:
        return state
    own, r1, ax, ay, late_x, late_y = state
    _, x, y = bits_of("seq")
    part = struct(late_x.shape, BF16)
    late_x, late_y = call(k_late, [part, part], [late_x, late_y, ax, ay], 0, name + "_late")
    return [own, r1, ax, ay, flip(late_x, "seq", x), flip(late_y, "seq", y)]


def scatter_last(state, name):
    if lax.axis_size("seq") != 8:
        return state[0]
    [out] = call(k_join, [struct(state[0].shape, BF16)], state, 0, name + "_join")
    return out


def scan(send, backward, name, beside=(None, None, None), steps=None):
    place = lax.axis_index("seq")
    seqs, size = send.shape[0], send.shape[1] - FRONT
    bits = bits_of("seq")
    state = struct((seqs, size, LANES), F32)
    row = struct((seqs, 8, LANES), F32)
    held = []
    for bit in bits_of("seq"):
        recv = flip(send, "seq", bit)
        is_set = (place & bit) != 0
        ahead = (jnp.logical_not(is_set) if backward else is_set).astype(jnp.int32)[None]
        last = bit == bits[-1]
        wait = beside[min(bit.bit_length() - 1, 2)]
        if wait is not None:
            recv = after(recv, wait)
        outs = [state] if last else [state, row, struct(send.shape, BF16)]
        made = call(
            functools.partial(k_scan, not held, last),
            [Each(o) for o in outs],
            [Scalars(ahead), Each(recv), Each(send), *(Each(a) for a in held)],
            0,
            name,
            grid=seqs,
        )
        if last:
            return made[0]
        held, send = made[:2], made[2]
        if steps is not None:
            steps.append(send)
    return before


def rows_of_mp(array):
    share = array.shape[0] // lax.axis_size("mp")
    return lax.dynamic_slice_in_dim(array, lax.axis_index("mp") * share, share, 0)


def exchange_mp(array):
    return lax.all_to_all(array, "mp", 0, 0, tiled=True)


def to_shares(array):
    size = lax.axis_size("mp")
    return exchange_mp(array.reshape(size, array.shape[0] // size, array.shape[1]))


def gather_mp(array):
    return lax.all_gather(array, "mp", tiled=True)


def after(values, others):
    return lax.optimization_barrier((values, others))[0]


def all_sum(array, axes):
    for axis in axes:
        for bit in bits_of(axis):
            array = array + flip(array, axis, bit)
    return array


def passed_along(block, axis, distance):
    devices = range(lax.axis_size(axis))
    route = [(i - distance, i) for i in devices if i - distance in devices]
    return lax.ppermute(block, axis, route)


def body(
    tokens, lengths, expert_ids, norm_gains, in_z, in_x, in_bc, in_dt, conv_x, conv_bc,
    head_par, gn_gain, out_w, router, shared_in, shared_down, expert_in, expert_down, d_out,
):
    piece, seqs, model = tokens.shape
    width = in_z.shape[1]
    heads = head_par.shape[1]
    experts = router.shape[1]
    half = expert_in.shape[-1]
    n_seq, n_mp = lax.axis_size("seq"), lax.axis_size("mp")
    seq_at, mp_at = lax.axis_index("seq"), lax.axis_index("mp")
    rows = seqs * piece
    share = rows // n_mp
    bc = 2 * STATE
    beside = beside_rows(experts, model)
    dma = pltpu.SemaphoreType.DMA

    meta = jnp.concatenate([lengths, (seq_at * piece).astype(jnp.int32)[None]])
    tok = jnp.transpose(tokens, (1, 0, 2))
    edge_in = passed_along(tokens[piece - (KCONV - 1) :], "seq", 1)
    front = jnp.pad(jnp.transpose(edge_in, (1, 0, 2)), ((0, 0), (FRONT - (KCONV - 1), 0), (0, 0)))
    tok_front = jnp.concatenate([front, tok], axis=1)
    gn = gn_gain[None]
    picked = jnp.sum(
        (expert_ids[..., None] == jnp.arange(LANES, dtype=jnp.int32)).astype(F32), axis=2
    ).astype(BF16)
    small = [conv_x, conv_bc, head_par, Scalars(meta)]
    d_ext = jnp.transpose(jnp.concatenate([d_out, picked], axis=-1), (1, 0, 2)).reshape(rows, model + LANES)

    def both(*shape, dtype=F32):
        return Each(struct((seqs, *shape), dtype))

    normed, gate_z, xbc, dt_raw, send, totals = call(
        k_in,
        [
            both(piece, model, dtype=BF16),
            both(piece, width),
            both(piece + FRONT, width + bc, dtype=BF16),
            both(piece, LANES),
            both(width + FRONT, LANES, dtype=BF16),
            both(8, LANES),
        ],
        [Each(tok_front), norm_gains, in_z, in_x, in_bc, in_dt.T, *small],
        2 * rows * model * (2 * width + bc + LANES),
        "mixer_in",
        grid=seqs,
    )
    entering = scan(send, False, "scan")
    intra, c_mat, ecum = call(
        k_intra,
        [both(piece, width), both(piece, STATE, dtype=BF16), both(piece, width)],
        [Each(xbc), Each(dt_raw), *small],
        2 * rows * piece * width * 4,
        "mixer_intra",
        grid=seqs,
    )
    of_rows = struct((share, model), F32)
    mixed, u, part = call(
        k_out,
        [both(piece, width), both(piece, width, dtype=BF16), both(piece, model + LANES, dtype=BF16)],
        [Each(intra), Each(c_mat), Each(ecum), Each(entering), Each(gate_z), gn, out_w],
        2 * rows * width * (STATE + model),
        "mixer_out",
        grid=seqs,
    )
    tok_own = rows_of_mp(tok.reshape(rows, model))
    d_own = rows_of_mp(d_ext)
    arrived = to_shares(part.reshape(rows, model + LANES))
    residual, mixer_own, two_own, scales = call(
        k_rows_one,
        [of_rows, of_rows, struct((share, model), BF16), struct((share, LANES), F32)],
        [tok_own, norm_gains, arrived],
        0,
        "rows_one",
    )
    d_got = gather(d_ext, piece, (lambda *_: entering, lambda *_: two_own))
    two = gather_mp(two_own)

    mine = ((seq_at * n_mp + mp_at) // 2).astype(jnp.int32)[None]

    x_slots = [1] * (n_seq - 2) + ([2, 2] if n_seq == 8 else [1, 1])

    def expert(pieces, first, last, o_all, shared=()):
        part_d = d_got.part(first, last)
        index, count = part_d.index, last - first
        slots = x_slots[first:last]
        size = rows * count
        return call(
            functools.partial(k_expert, (slots, part_d.slots), bool(shared)),
            [Far(struct((n_seq * rows, model), BF16))]
            + [Far(struct((rows, model + LANES), BF16)), Far(struct((rows, 3 * half), BF16))] * count,
            [
                Scalars(mine), router.T, expert_in, expert_down, *(Far(p) for p in (*pieces, *part_d.pieces)),
                *shared, *(Far(o) for o in o_all),
            ],
            2 * size * model * half * 6.5,
            "experts",
            index=index,
            aliases={5 + len(pieces) + len(part_d.pieces): 0} if o_all else None,
            scratch=[
                pltpu.VMEM((size, model), BF16),
                pltpu.VMEM((size, model + LANES), BF16),
                pltpu.VMEM((size, model), BF16),
                pltpu.VMEM((size, model + LANES), BF16),
                pltpu.VMEM((size, 3 * half), BF16),
                dma((len(pieces),)),
                dma((len(part_d.pieces),)),
                dma((3 * count,)),
            ],
        )

    def shared_of(x):
        return call(
            k_shared,
            [struct((rows, model), BF16), struct((rows, model), BF16)],
            [x, d_ext, shared_in, shared_down],
            2 * rows * model * half * 6,
            "shared",
        )

    made = []

    def near_experts(own, far):
        made.append(expert([own, far], 0, 2, [], shared_of(own)))
        return made[-1][1:]

    def chip_experts(by_x, by_y):
        made.append(expert([by_x, by_y], 2, 4, made[-1][:1]))
        return made[-1][1:]

    if n_seq == 8:
        normed, u = normed.reshape(rows, model), u.reshape(rows, width)
        n_first = first_hop(after(normed, part))
        two, d_got.pieces = lax.optimization_barrier((two, d_got.pieces))
        x_got = gather(two, piece, (near_experts, chip_experts))
        made.append(expert(x_got.pieces[4:], 4, 8, made[-1][:1]))
    else:
        x_got = gather_all(two)
        out_shared, dx_shared = shared_of(two)
        for i in range(0, n_seq, 4):
            made.append(expert(x_got.part(i, i + 4).pieces, i, i + 4, made[-1][:1] if made else []))
    out_all = made[-1][0]
    e_dx = [a for m in made for a in m[1::2]]
    e_keep = [a for m in made for a in m[2::2]]

    g_expert_in = g_expert_down = g_shared_in = g_shared_down = 0.0
    weight_outs = [Far(struct((2, model, half), F32)), Far(struct((half, model), F32))]

    def weight_scratch(keeps, pieces):
        return [
            pltpu.VMEM((8 * rows, model), BF16),
            pltpu.VMEM((8 * rows, model + LANES), BF16),
            pltpu.VMEM((8 * rows, 3 * half), BF16),
            pltpu.VMEM((model, 2 * half), F32),
            pltpu.VMEM((half, model), F32),
            dma((pieces,)),
            dma((pieces,)),
            *([dma((8,))] if keeps else []),
            dma((3 * (model // 256),)),
        ]

    def shared_weights(first, others):
        x = x_got.part(first, first + 8)
        return call(
            functools.partial(k_shared_weights, x.slots),
            weight_outs,
            [shared_in, shared_down, *(Far(a) for a in (*after(x.pieces, others), *d_got.part(first, first + 8).pieces))],
            6 * 2 * 8 * rows * model * half,
            "shared_weights",
            index=x.index,
            scratch=weight_scratch(False, len(x.pieces)),
        )

    def expert_weights(first, others):
        x = x_got.part(first, first + 8)
        return call(
            functools.partial(k_expert_weights, x.slots),
            weight_outs,
            [Far(a) for a in (*after(x.pieces, others), *d_got.part(first, first + 8).pieces, *e_keep[first : first + 8])],
            3 * 2 * 8 * rows * model * half,
            "expert_weights",
            index=x.index,
            scratch=weight_scratch(True, len(x.pieces)),
        )

    state = scatter_first(e_dx, "dx")
    if n_seq == 8:
        g_shared_in, g_shared_down = shared_weights(0, e_dx)
        state, g_shared_in, g_shared_down = lax.optimization_barrier((state, g_shared_in, g_shared_down))
        state = scatter_second(state, "dx")
        g_expert_in, g_expert_down = expert_weights(0, g_shared_down)
        state, g_expert_in, g_expert_down = lax.optimization_barrier((state, g_expert_in, g_expert_down))
    else:
        for first in range(0, n_seq, 8):
            a, b = shared_weights(first, e_dx)
            c, d = expert_weights(first, e_dx)
            g_shared_in, g_shared_down = g_shared_in + a, g_shared_down + b
            g_expert_in, g_expert_down = g_expert_in + c, g_expert_down + d
    dx_sum = scatter_last(state, "dx")
    if n_seq != 8:
        dx_sum = jnp.concatenate([low_sum(dx_sum[:, :model], dx_shared), dx_sum[:, model:]], axis=1)
    arrived = to_shares(dx_sum)
    out_sum = lax.psum_scatter(after(out_all, dx_sum), "seq", scatter_dimension=0, tiled=True)
    if n_seq != 8:
        out_sum = low_sum(out_sum, out_shared)
    dm_own, d_residual, g_two = call(
        k_rows_two,
        [struct((share, model + LANES), BF16), of_rows, struct((experts + 8, model), F32)],
        [d_own, two_own, residual, mixer_own, scales, norm_gains, router.T, arrived],
        0,
        "rows_two",
    )
    dm = gather_mp(dm_own)
    if n_seq == 8:
        n_got = gather_near(normed, piece, dx_sum, n_first)
        u = after(u, dx_sum)
        dm, u_first = lax.optimization_barrier((dm, first_hop(u)))
    else:
        normed, u = after((normed, u), (dm, g_expert_in, g_shared_in))
        n_got = gather_all(normed.reshape(rows, model))
        u_got = gather_all(u.reshape(rows, width))

    dz, dy, send, g_gn = call(
        k_back_gate,
        [
            both(piece, width, dtype=BF16),
            both(piece, width),
            both(width + FRONT, LANES, dtype=BF16),
            both(8, width),
        ],
        [Rows(dm, piece), Each(mixed), Each(gate_z), gn, out_w, Each(c_mat), Each(ecum), Each(totals)],
        2 * rows * width * (model + STATE),
        "back_gate",
        grid=seqs,
    )
    intra_back = call(
        k_back_intra,
        [both(piece, width), both(piece, STATE), both(piece, STATE), both(piece, LANES), both(piece, model)],
        [Each(xbc), Each(dt_raw), *small, Each(dy), Each(dz), in_z],
        2 * rows * width * (model + 4 * piece),
        "back_intra",
        grid=seqs,
    )
    dxw0, db0, dc0, dcum0, dn0 = intra_back
    steps = []
    dm_first = first_hop(dm) if n_seq == 8 else None
    leaving = scan(send, True, "scan_back", (None, None, (intra_back, dm_first)), steps)
    out_arrived = to_shares(after(out_sum, steps[1]))
    dz = after(dz, leaving).reshape(rows, width)
    dz_first = first_hop(dz) if n_seq == 8 else None

    def in_order(rows):
        return jnp.transpose(rows.reshape(seqs, piece, model), (1, 0, 2)).astype(F32)

    d_xbc, d_dt, g_conv, g_hp = call(
        k_back_state,
        [
            both(piece + FRONT, width + bc),
            both(piece, LANES, dtype=BF16),
            both(8, width + bc),
            both(8, LANES),
        ],
        [
            Each(xbc), Each(dt_raw), *small, Each(dy), Each(dxw0), Each(db0), Each(dc0), Each(dcum0),
            Each(entering), Each(leaving),
        ],
        2 * rows * width * STATE * 20,
        "back_state",
        grid=seqs,
    )
    edge = passed_along(d_xbc[:, :FRONT], "seq", -1)
    if n_seq == 8:
        edge, out_arrived, dz_first = lax.optimization_barrier((edge, out_arrived, dz_first))
    dx, d_bc, part = call(
        k_back_in,
        [
            struct((rows + SMALL, width + LANES), BF16),
            struct((rows + beside, bc), BF16),
            both(piece, model, dtype=BF16),
        ],
        [
            Each(dn0), Each(d_xbc), Each(edge), Each(d_dt), Each(tok_front), g_conv, g_hp, g_gn, g_two,
            in_x, in_bc, in_dt.T,
        ],
        2 * rows * (width + bc + LANES) * model,
        "back_in",
        grid=seqs,
        scratch=[pltpu.VMEM((8, model), F32)],
    )
    arrived = to_shares(part.reshape(rows, model))
    [out_own] = call(
        k_rows_out, [struct((share, model), BF16)], [residual, after(out_arrived, part)], 0, "rows_out"
    )
    out_shares = [out_own if k == 0 else flip(out_own, "mp", k) for k in range(n_mp)]
    dm_got = gather_near(dm, piece, leaving, dm_first)
    if n_seq == 8:
        u_got = gather_near(u, piece, leaving, u_first)
    dz_got = gather_direct(dz, dz_first)
    *head_bits, last_bit = bits_of("mp")
    for bit in head_bits:
        d_bc = low_sum(d_bc, flip(d_bc, "mp", bit))
    d_bc = low_sum(d_bc, flip(d_bc, "mp", last_bit))
    bc_got = gather_direct(d_bc)
    dx_first = first_hop(dx) if n_seq == 8 else None
    if n_seq != 8:
        dx_got = gather_all(dx)

    g_in_z = g_in_x = g_out_w = small = 0.0
    size = min(8, len(n_got.slots))
    for first in range(0, len(n_got.slots), size):
        last = first + size
        g_out_w = g_out_w + out_weights(u_got.part(first, last), dm_got.part(first, last), size * rows)
    if n_seq == 8:
        arrived, g_out_w, d_bc, dx_first = lax.optimization_barrier((arrived, g_out_w, d_bc, dx_first))
        dx_got = gather_near(dx, piece, (), dx_first)
    [rows_own] = call(
        k_rows_three,
        [struct((n_mp, share, model), BF16)],
        [tok_own, d_residual, norm_gains, arrived],
        0,
        "rows_three",
    )
    rows_all = exchange_mp(rows_own)
    for first in range(0, len(n_got.slots), size):
        last = first + size
        [a] = outer(n_got.part(first, last), [dz_got.part(first, last)], size * rows, "weights_z")
        g_in_z = g_in_z + a
    [g_in_z] = both_cores(g_in_z, [width], "cores_z")
    [g_out_w] = both_cores(g_out_w, [model], "cores_out")
    for first in range(0, len(n_got.slots), size):
        last = first + size
        a, b = outer(
            n_got.part(first, last), [dx_got.part(first, last), bc_got.part(first, last)], size * rows, "weights_x",
            beside,
        )
        g_in_x, small = g_in_x + a, small + b
    order = after(jnp.stack([mp_at ^ k for k in range(n_mp)]).astype(jnp.int32), g_in_x)
    [out_rows] = call(k_assemble, [struct((rows, model), BF16)], [Scalars(order), *out_shares], 0, "output")
    output = in_order(out_rows)
    if n_seq == 8:
        rows_all, g_in_x, g_in_z, g_out_w, output = lax.optimization_barrier(
            (rows_all, g_in_x, g_in_z, g_out_w, output)
        )

    d_tokens = in_order(rows_all)
    g_in_x, g_dt, g_in_bc = both_cores(g_in_x, [width, LANES, bc], "cores_x")
    if n_seq == 8:
        small = small + after(flip(small, "seq", 1), g_in_x)
    summed = small[:, width + LANES :]
    cuts = model // bc
    g_router = summed[: cuts * experts].reshape(cuts, experts, bc)
    first = cuts * experts
    return (
        output,
        d_tokens,
        summed[first : first + 2 * cuts].reshape(2, model),
        g_in_z,
        g_in_x,
        g_in_bc,
        g_dt[:heads].T,
        small[: KCONV + 1, :width],
        summed[first + 2 * cuts : first + 2 * cuts + KCONV + 1],
        small[:3, width : width + heads],
        small[KCONV + 1, :width],
        g_out_w,
        jnp.transpose(g_router, (0, 2, 1)).reshape(model, experts),
        g_shared_in,
        g_shared_down,
        g_expert_in[None],
        g_expert_down[None],
    )


def solution(mesh):
    in_specs = (
        P("seq", None, None),
        P(),
        P("seq", None, None),
        P(),
        P(None, "mp"),
        P(None, "mp"),
        P(),
        P(None, "mp"),
        P(None, "mp"),
        P(),
        P(None, "mp"),
        P("mp"),
        P("mp", None),
        P(),
        P(None, None, "mp"),
        P("mp", None),
        P(("seq", "mp"), None, None, None),
        P(("seq", "mp"), None, None),
        P("seq", None, None),
    )
    out_specs = (
        P("seq", None, None),
        P("seq", None, None),
        P(),
        P(None, "mp"),
        P(None, "mp"),
        P(),
        P(None, "mp"),
        P(None, "mp"),
        P(),
        P(None, "mp"),
        P("mp"),
        P("mp", None),
        P(),
        P(None, None, "mp"),
        P("mp", None),
        P(("seq", "mp"), None, None, None),
        P(("seq", "mp"), None, None),
    )
    return jax.shard_map(body, mesh=mesh, in_specs=in_specs, out_specs=out_specs, check_vma=False)
```
